32 devices in a mesh: groups: 2 (over y), rows: 16 (over z, x, core).
Axes of the slice: x: 2, y: 2, z: 4, core: 2. Of those that a mesh axis runs over, the one named last changes fastest.
Arguments:
- transition_tiles: bfloat16 [2048, 5, 128, 128], P(('groups', 'rows')), parts along dimension 0, may hold values from 0.049804688 to 1
- column_tiles: int32 [2048, 5], P(('groups', 'rows')), parts along dimension 0, may hold values from 0 to 1023, as said below
- schur_basis: bfloat16 [32, 262144], P(None, ('groups', 'rows')), parts along dimension 1, may hold values from -60 to 60
- membership_map: float32 [64, 32], P('groups'), parts along dimension 0, may hold values from -1 to 1
Outputs:
- memberships: float32 [32, 262144], P(None, ('groups', 'rows')), parts along dimension 1
The draws below stay inside these ranges and needn't reach their ends.
There are 2 independent parts, one for each index of `groups`. The reference program is written for one: setup_inputs(seed, part) draws one part's arguments, and reference() takes and returns one part's arrays. A program takes and returns all parts, laid end to end along the dimension named above; each array names one. Nothing has to cross between parts.
Inputs may be any that keep to these rules, and one draw needn't show every extreme that they name: `column_tiles`: the 5 entries of row tile r are distinct column tiles, r itself among them, all within 64 of r; some row tile has one at distance exactly 64.
All inputs are finite; a program needn't handle non-finite values.
Results may differ from the reference program's by a relative error of at most 0.0045.
Values may be sent and summed in bfloat16 or wider, within the bound.
No kernel may reach another device: no remote copies, remote signals or barrier semaphores. Data moves between devices by JAX's collectives and lax.ppermute only.
A program may use at most 64 MiB of HBM per device.

```python
import math
import jax
import jax.numpy as jnp
from jax import lax

NV = 32
TILE = 128
SLOTS = 5
PRODUCTS = 4
ROWT_DEV = 64
REACH = 64
ROWTILES = 1024
NSTATES = 131072
N_ROWS = 16


def draw_column_tiles(key, part):
    key_lower, key_upper, key_score = jax.random.split(jax.random.fold_in(key, 11), 3)
    lower_width = jax.random.randint(key_lower, (ROWTILES,), SLOTS - 1, REACH + 1)
    upper_width = jax.random.randint(key_upper, (ROWTILES,), SLOTS - 1, REACH + 1)
    upper_width = upper_width.at[0].set(REACH)
    window = 2 * REACH + 1
    offsets = jnp.arange(window, dtype=jnp.int32) - REACH
    row_index = jnp.arange(ROWTILES, dtype=jnp.int32)
    column_index = row_index[:, None] + offsets[None, :]
    inside = (column_index >= 0) & (column_index < ROWTILES) & (offsets[None, :] >= -lower_width[:, None]) & (offsets[None, :] <= upper_width[:, None])
    band_ends = (offsets[None, :] == -lower_width[:, None]) | (offsets[None, :] == upper_width[:, None])
    random_score = jax.random.randint(key_score, (ROWTILES, window), 0, 1000)
    priority = random_score * window + (offsets[None, :] + REACH)
    boost = 1000 * window
    priority = jnp.where(band_ends, priority + boost, priority)
    priority = jnp.where(offsets[None, :] == 0, 3 * boost, priority)
    priority = jnp.where(inside, priority, -1 - (offsets[None, :] + REACH))
    unused, chosen = lax.top_k(priority, SLOTS)
    return jnp.take_along_axis(column_index, chosen, axis=1).astype(jnp.int32)


def draw_schur_basis(key, part):
    key_noise = jax.random.fold_in(jax.random.fold_in(key, 23), 0)
    position = jnp.arange(NSTATES, dtype=jnp.float32) / NSTATES
    values = jnp.clip(jax.random.normal(key_noise, (NV, NSTATES), jnp.float32), -5.0, 5.0) * jnp.exp(position * 2.3)
    return values.astype(jnp.bfloat16)


def steps_of(rng, shape, cuts, least, largest):
    def one(dim, parts):
        draws = jax.random.uniform(jax.random.fold_in(jax.random.fold_in(rng, 6), dim), (parts,), jnp.float32, least / len(cuts), largest / len(cuts))
        return jnp.repeat(jnp.exp(draws), shape[dim] // parts).reshape((-1,) + (1,) * (len(shape) - dim - 1))

    gain = one(*cuts[0])
    for cut in cuts[1:]:
        gain = gain * one(*cut)
    return gain


def gaussian(rng, shape, scale, most, kind=jnp.bfloat16):
    entries = jax.random.normal(rng, shape, jnp.float32) * scale
    return jnp.minimum(jnp.maximum(entries, -most), most).astype(kind)


def setup_inputs(seed: int = 0, part: int = 0) -> dict:
    splits = jax.random.split(jax.random.key(seed), 5)
    part_keys = jax.random.split(jax.random.fold_in(splits[4], part), 5)
    return {
        "transition_tiles": jnp.clip(jnp.exp(math.log(1.0) - 2.9996462 * jax.random.uniform(part_keys[0], (ROWTILES, SLOTS, TILE, TILE), jnp.float32) ** steps_of(part_keys[0], (ROWTILES, SLOTS, TILE, TILE), ((0, 16),), -0.2, 0.2)), 0.049804688, 1.0).astype(jnp.bfloat16),
        "column_tiles": draw_column_tiles(jax.random.fold_in(jax.random.fold_in(splits[4], part), 71), part),
        "schur_basis": draw_schur_basis(jax.random.fold_in(jax.random.fold_in(splits[4], part), 71), part),
        "membership_map": gaussian(part_keys[3], (NV, NV), NV ** -0.5, 1.0, jnp.float32),
    }


def tile_product(tiles_block, columns_block, vectors):
    tile_size = tiles_block.shape[-1]
    blocks = vectors.reshape(vectors.shape[0], -1, tile_size)
    picked = jnp.take(blocks, columns_block, axis=1).astype(jnp.float32)
    weights = tiles_block.astype(jnp.float32)
    summed = jnp.einsum('rsij,vrsj->vri', weights, picked, precision=lax.Precision.HIGHEST)
    row_total = jnp.sum(weights, axis=(1, 3))
    return summed / row_total[None]

def apply_chain(transition_tiles, column_tiles, vectors):
    tiles_split = transition_tiles.reshape(N_ROWS, ROWT_DEV, SLOTS, TILE, TILE)
    columns_split = column_tiles.reshape(N_ROWS, ROWT_DEV, SLOTS)

    def one_panel(pair):
        return tile_product(pair[0], pair[1], vectors)
    result = lax.map(one_panel, (tiles_split, columns_split))
    return jnp.transpose(result, (1, 0, 2, 3)).reshape(NV, NSTATES)

def reference(transition_tiles, column_tiles, schur_basis, membership_map):
    result = apply_chain(transition_tiles, column_tiles, schur_basis)
    for step in range(PRODUCTS - 1):
        image = result.astype(jnp.bfloat16)
        result = apply_chain(transition_tiles, column_tiles, image)
    power_vec = result
    gram_total = jnp.dot(power_vec.astype(jnp.float32), power_vec.T.astype(jnp.float32), precision=lax.Precision.HIGHEST, preferred_element_type=jnp.float32) / NSTATES
    factor = jnp.linalg.cholesky(gram_total)
    basis_q = jax.scipy.linalg.solve_triangular(factor, power_vec, lower=True)
    return jnp.dot(membership_map.T.astype(jnp.float32), basis_q.astype(jnp.float32), precision=lax.Precision.HIGHEST, preferred_element_type=jnp.float32)
```

```python
import functools

import jax
import jax.numpy as jnp
from jax import lax
from jax.experimental import pallas as pl
from jax.experimental.pallas import tpu as pltpu
from jax.sharding import PartitionSpec as P

PRODUCTS = 4
BLOCK = 16
F32 = jnp.float32
BF16 = jnp.bfloat16
NN = (((1,), (0,)), ((), ()))
NT = (((1,), (1,)), ((), ()))
VM = pl.BlockSpec(memory_space=pltpu.VMEM)
SM = pl.BlockSpec(memory_space=pltpu.SMEM)


def in_vmem(array):
    return pltpu.with_memory_space_constraint(array, pltpu.VMEM)


def cost(flops, moved):
    return pl.CostEstimate(flops=flops, bytes_accessed=moved, transcendentals=0)


def params(mib):
    return pltpu.CompilerParams(vmem_limit_bytes=mib * 2**20)


def prep_kernel(where, columns, tiles, turned, inverse, index, order):
    rows, slots, size, _ = tiles.shape
    first, parity = where[0], where[1]
    low = jnp.where(parity == 0, 2 * rows, rows)
    high = jnp.where(parity == 0, rows, 2 * rows)
    ones = jnp.ones((16, slots * size), BF16)

    def place(r, counts):
        near, far = counts
        crosses = jnp.int32(0)
        for s in range(slots):
            offset = columns[s, r] - first
            spot = jnp.where(
                offset < 0,
                offset + rows + low,
                jnp.where(offset >= rows, offset - rows + high, offset),
            )
            index[r * slots + s] = spot
            crosses = jnp.maximum(crosses, jnp.where(spot >= 2 * rows, 1, 0))
        order[jnp.where(crosses == 1, rows - 1 - far, near)] = r
        return near + 1 - crosses, far + crosses

    def step(block, counts):
        for u in range(BLOCK // 2):
            r = block * (BLOCK // 2) + u
            counts = place(r, counts)
            for s in range(slots):
                turned[r, pl.ds(s * size, size), :] = tiles[r, s].T
            total = lax.dot_general(ones, turned[r], NN, preferred_element_type=F32)
            inverse[pl.ds(r, 1), :] = 1.0 / total[0:1]
        return counts

    near, _ = lax.fori_loop(
        0, 2 * rows // BLOCK, step, (jnp.int32(0), jnp.int32(0))
    )
    order[rows] = near


def prep(where, columns, tiles):
    rows, slots, size, _ = tiles.shape
    return pl.pallas_call(
        prep_kernel,
        out_shape=(
            pltpu.VMEM((rows, slots * size, size), BF16),
            pltpu.VMEM((rows, size), F32),
            pltpu.SMEM((rows * slots,), jnp.int32),
            pltpu.SMEM((rows + 8,), jnp.int32),
        ),
        in_specs=[SM, SM, VM],
        out_specs=(VM, VM, SM, SM),
        compiler_params=params(4),
        cost_estimate=cost(2 * tiles.size * 16, 4 * tiles.size),
        name="prep",
    )(where, columns, in_vmem(tiles))


def fill(window, start, panel, tile_major):
    rows = window.shape[0] // 3
    size = window.shape[2]
    if tile_major:
        window[start : start + rows] = panel[...]
    else:
        for t in range(rows):
            window[start + t] = panel[:, t * size : (t + 1) * size]


def row_block(start, index, order, turned, inverse, window, image):
    slots = turned.shape[1] // turned.shape[2]
    picked = [order[start + u] for u in range(BLOCK)]
    vectors = [
        jnp.concatenate([window[index[r * slots + s]] for s in range(slots)], axis=1)
        for r in picked
    ]
    sums = [
        lax.dot_general(x, turned[r], NN, preferred_element_type=F32)
        for x, r in zip(vectors, picked)
    ]
    for r, y in zip(picked, sums):
        image[r] = (y * inverse[pl.ds(r, 1), :]).astype(image.dtype)


def near_kernel(tile_major, index, order, turned, inverse, own, mate, window, image):
    rows = turned.shape[0]
    fill(window, 0, own, tile_major)
    fill(window, rows, mate, tile_major)

    def step(block, carry):
        row_block(block * BLOCK, index, order, turned, inverse, window, image)
        return carry

    lax.fori_loop(0, (order[rows] + BLOCK - 1) // BLOCK, step, 0)


def far_kernel(tile_major, index, order, turned, inverse, other, w_in, i_in, window, image):
    rows = turned.shape[0]
    fill(window, 2 * rows, other, tile_major)

    def step(block, carry):
        start = rows - (block + 1) * BLOCK
        row_block(start, index, order, turned, inverse, window, image)
        return carry

    lax.fori_loop(0, (rows - order[rows] + BLOCK - 1) // BLOCK, step, 0)


def product(plan, own, mate, other, tile_major, kind):
    index, order, turned, inverse = plan
    rows, depth, size = turned.shape
    vectors = own.shape[1 if tile_major else 0]
    shapes = (
        pltpu.VMEM((3 * rows, vectors, size), BF16),
        pltpu.VMEM((rows, vectors, size), kind),
    )
    estimate = cost(rows * depth * size * vectors, 2 * rows * depth * size)
    window, image = pl.pallas_call(
        functools.partial(near_kernel, tile_major),
        out_shape=shapes,
        in_specs=[SM, SM, VM, VM, VM, VM],
        out_specs=(VM, VM),
        compiler_params=params(4),
        cost_estimate=estimate,
        name="near_rows",
    )(index, order, in_vmem(turned), in_vmem(inverse), in_vmem(own), in_vmem(mate))
    window, image = pl.pallas_call(
        functools.partial(far_kernel, tile_major),
        out_shape=shapes,
        in_specs=[SM, SM, VM, VM, VM, VM, VM],
        out_specs=(VM, VM),
        input_output_aliases={5: 0, 6: 1},
        compiler_params=params(4),
        cost_estimate=estimate,
        name="far_rows",
    )(
        index,
        order,
        in_vmem(turned),
        in_vmem(inverse),
        in_vmem(other),
        in_vmem(window),
        in_vmem(image),
    )
    return image


def thirds(x):
    high = x.astype(BF16)
    rest = x - high.astype(F32)
    middle = rest.astype(BF16)
    low = (rest - middle.astype(F32)).astype(BF16)
    return high, middle, low


def fold(product3, vectors):
    total = None
    for a, b in ((2, 2), (1, 2), (2, 1), (0, 2), (2, 0), (1, 1), (0, 1), (1, 0), (0, 0)):
        part = product3[
            a * vectors : (a + 1) * vectors, b * vectors : (b + 1) * vectors
        ]
        total = part if total is None else total + part
    return total


def gram_kernel(power, parts, gram):
    rows, vectors, size = power.shape
    group = 8

    def step(block, total):
        taken = []
        for u in range(group):
            r = block * group + u
            stacked = jnp.concatenate(thirds(power[r]), axis=0)
            parts[r] = stacked
            taken.append(stacked)
        wide = jnp.concatenate(taken, axis=1)
        return total + lax.dot_general(wide, wide, NT, preferred_element_type=F32)

    total = lax.fori_loop(
        0, rows // group, step, jnp.zeros((3 * vectors, 3 * vectors), F32)
    )
    gram[...] = fold(total, vectors)


def gram_local(power):
    rows, vectors, size = power.shape
    return pl.pallas_call(
        gram_kernel,
        out_shape=(
            pltpu.VMEM((rows, 3 * vectors, size), BF16),
            pltpu.VMEM((vectors, vectors), F32),
        ),
        in_specs=[VM],
        out_specs=(VM, VM),
        compiler_params=params(4),
        cost_estimate=cost(18 * power.size * vectors, 10 * power.size),
        name="gram",
    )(in_vmem(power))


def inverse_factor(gram):
    count = gram.shape[0]
    row = lax.broadcasted_iota(jnp.int32, (count, count), 0)
    column = lax.broadcasted_iota(jnp.int32, (count, count), 1)
    work = jnp.concatenate([gram, jnp.where(row == column, 1.0, 0.0)], axis=1)
    below = lax.broadcasted_iota(jnp.int32, work.shape, 0)
    for k in range(count):
        pivot = work[k : k + 1]
        scaled = pivot * lax.rsqrt(pivot[:, k : k + 1])
        column_k = jnp.broadcast_to(work[:, k : k + 1], work.shape)
        head = lax.rsqrt(pivot[:, k : k + 1])
        work = jnp.where(
            below > k,
            work - (column_k * head) * scaled,
            jnp.where(below == k, scaled, work),
        )
    return work[:, count:]


def final_kernel(states, gram_a, gram_b, mapping, parts, out):
    rows, depth, size = parts.shape
    vectors = depth // 3
    total = (gram_a[...] + gram_b[...]) / states
    factor = inverse_factor(total)
    combined = lax.dot_general(
        mapping[...],
        factor,
        (((0,), (0,)), ((), ())),
        precision=lax.Precision.HIGHEST,
        preferred_element_type=F32,
    )
    high, middle, low = thirds(combined)
    blank = jnp.zeros_like(high)
    left = jnp.concatenate(
        [
            jnp.concatenate([high, high, high], axis=1),
            jnp.concatenate([middle, middle, blank], axis=1),
            jnp.concatenate([low, blank, blank], axis=1),
        ],
        axis=0,
    )
    for r in range(rows):
        y = lax.dot_general(left, parts[r], NN, preferred_element_type=F32)
        out[:, r * size : (r + 1) * size] = (
            y[2 * vectors :] + y[vectors : 2 * vectors]
        ) + y[:vectors]


def final(states, gram_a, gram_b, mapping, parts):
    rows, depth, size = parts.shape
    vectors = depth // 3
    return pl.pallas_call(
        functools.partial(final_kernel, float(states)),
        out_shape=jax.ShapeDtypeStruct((vectors, rows * size), F32),
        in_specs=[VM, VM, VM, VM],
        out_specs=VM,
        compiler_params=params(8),
        cost_estimate=cost(6 * parts.size * vectors, 4 * parts.size),
        name="memberships",
    )(gram_a, gram_b, mapping, in_vmem(parts))


def body(transition_tiles, column_tiles, schur_basis, membership_map):
    rows = transition_tiles.shape[0]
    count = lax.axis_size("rows")
    me = lax.axis_index("rows")
    mates = [(i, i ^ 1) for i in range(count)]
    others = []
    for i in range(1, count - 1, 2):
        others += [(i, i + 1), (i + 1, i)]

    def exchange(image):
        return lax.ppermute(image, "rows", mates), lax.ppermute(image, "rows", others)

    image = schur_basis
    mate, other = exchange(image)
    where = jnp.stack([me * rows, me % 2]).astype(jnp.int32)
    turned, inverse, index, order = prep(where, column_tiles.T, transition_tiles)
    plan = (index, order, turned, inverse)
    for step in range(PRODUCTS):
        if step:
            mate, other = exchange(image)
        kind = F32 if step == PRODUCTS - 1 else BF16
        image = product(plan, image, mate, other, step > 0, kind)
    parts, gram = gram_local(image)
    distance = 1
    while distance < count:
        partner = lax.ppermute(gram, "rows", [(i, i ^ distance) for i in range(count)])
        distance *= 2
        if distance < count:
            gram = gram + partner
    states = schur_basis.shape[1] * count
    return final(states, gram, partner, membership_map, parts)


def solution(mesh):
    return jax.shard_map(
        body,
        mesh=mesh,
        in_specs=(
            P(("groups", "rows"), None, None, None),
            P(("groups", "rows"), None),
            P(None, ("groups", "rows")),
            P("groups", None),
        ),
        out_specs=P(None, ("groups", "rows")),
        check_vma=False,
    )
```

```python
import functools

import jax
import jax.numpy as jnp
from jax import lax
from jax.experimental import pallas as pl
from jax.experimental.pallas import tpu as pltpu
from jax.sharding import PartitionSpec as P

PRODUCTS = 4
BLOCK = 16
CHUNK = 8
F32 = jnp.float32
BF16 = jnp.bfloat16
NN = (((1,), (0,)), ((), ()))
NT = (((1,), (1,)), ((), ()))
VM = pl.BlockSpec(memory_space=pltpu.VMEM)
SM = pl.BlockSpec(memory_space=pltpu.SMEM)


def in_vmem(array):
    return pltpu.with_memory_space_constraint(array, pltpu.VMEM)


def cost(flops, moved):
    return pl.CostEstimate(flops=flops, bytes_accessed=moved, transcendentals=0)


def params(mib):
    return pltpu.CompilerParams(vmem_limit_bytes=mib * 2**20)


def prep_kernel(where, columns, tiles, turned, inverse, index, order, landing, arrived):
    rows, slots, size, _ = tiles.shape
    depth, chunk = landing.shape[:2]
    chunks = rows // chunk
    first, parity = where[0], where[1]
    low = jnp.where(parity == 0, 2 * rows, rows)
    high = jnp.where(parity == 0, rows, 2 * rows)
    ones = jnp.ones((16, slots * size), BF16)

    def copy(i):
        slot = lax.rem(i, depth)
        return pltpu.make_async_copy(
            tiles.at[pl.ds(i * chunk, chunk)], landing.at[slot], arrived.at[slot]
        )

    def place(r, counts):
        near, far = counts
        crosses = jnp.int32(0)
        for s in range(slots):
            offset = columns[s, r] - first
            spot = jnp.where(
                offset < 0,
                offset + rows + low,
                jnp.where(offset >= rows, offset - rows + high, offset),
            )
            index[r * slots + s] = spot
            crosses = jnp.maximum(crosses, jnp.where(spot >= 2 * rows, 1, 0))
        order[jnp.where(crosses == 1, rows - 1 - far, near)] = r
        return near + 1 - crosses, far + crosses

    for i in range(depth):
        copy(i).start()

    def step(i, counts):
        slot = lax.rem(i, depth)
        copy(i).wait()
        for u in range(chunk):
            r = i * chunk + u
            counts = place(r, counts)
            for s in range(slots):
                turned[r, pl.ds(s * size, size), :] = landing[slot, u, s].T
            total = lax.dot_general(ones, turned[r], NN, preferred_element_type=F32)
            inverse[pl.ds(r, 1), :] = 1.0 / total[0:1]

        @pl.when(i + depth < chunks)
        def _():
            copy(i + depth).start()

        return counts

    near, _ = lax.fori_loop(0, chunks, step, (jnp.int32(0), jnp.int32(0)))
    order[rows] = near


def prep(where, columns, tiles):
    rows, slots, size, _ = tiles.shape
    chunk, depth = CHUNK, 3
    return pl.pallas_call(
        prep_kernel,
        out_shape=(
            pltpu.VMEM((rows, slots * size, size), BF16),
            pltpu.VMEM((rows, size), F32),
            pltpu.SMEM((rows * slots,), jnp.int32),
            pltpu.SMEM((rows + 8,), jnp.int32),
        ),
        in_specs=[SM, SM, pl.BlockSpec(memory_space=pltpu.HBM)],
        out_specs=(VM, VM, SM, SM),
        scratch_shapes=[
            pltpu.VMEM((depth, chunk, slots, size, size), BF16),
            pltpu.SemaphoreType.DMA((depth,)),
        ],
        compiler_params=params(10),
        cost_estimate=cost(2 * tiles.size * 16, 4 * tiles.size),
        name="prep",
    )(where, columns, pltpu.with_memory_space_constraint(tiles, pltpu.HBM))


def lists_kernel(limit, where, theirs, index, packed, sending, more, mark, asked, rank):
    slots, rows = theirs.shape
    first = where[0]
    unroll = 8

    def clear(block, carry):
        for u in range(unroll):
            h = block * unroll + u
            mark[h] = 0
            asked[h] = 0
            sending[h] = 0
        return carry

    def name(block, carry):
        for u in range(unroll):
            r = block * unroll + u
            for s in range(slots):
                t = index[r * slots + s] - 2 * rows
                mark[jnp.where(t >= 0, t, rows)] = 1
                c = theirs[s, r] - first
                asked[jnp.where((c >= 0) & (c < rows), c, rows)] = 1
        return carry

    def count(block, carry):
        read, sent = carry
        for u in range(unroll):
            h = block * unroll + u
            rank[h] = read
            sending[sent] = h
            read, sent = read + mark[h], sent + asked[h]
        return read, sent

    def renumber(block, carry):
        for u in range(unroll):
            r = block * unroll + u
            for s in range(slots):
                t = index[r * slots + s]
                far = t >= 2 * rows
                packed[r * slots + s] = jnp.where(
                    far, 2 * rows + rank[jnp.where(far, t - 2 * rows, 0)], t
                )
        return carry

    blocks = rows // unroll
    lax.fori_loop(0, blocks, clear, 0)
    lax.fori_loop(0, blocks, name, 0)
    read, sent = lax.fori_loop(0, blocks, count, (jnp.int32(0), jnp.int32(0)))
    lax.fori_loop(0, blocks, renumber, 0)
    more[0] = jnp.where(jnp.maximum(read, sent) > limit, 1, 0)


def lists(limit, where, theirs, index):
    slots, rows = theirs.shape
    return pl.pallas_call(
        functools.partial(lists_kernel, limit),
        out_shape=(
            pltpu.SMEM((rows * slots,), jnp.int32),
            pltpu.SMEM((rows + 8,), jnp.int32),
            jax.ShapeDtypeStruct((1,), jnp.int32),
        ),
        in_specs=[SM, SM, SM],
        out_specs=(SM, SM, SM),
        scratch_shapes=[pltpu.SMEM((rows + 8,), jnp.int32)] * 3,
        compiler_params=params(1),
        cost_estimate=cost(4000000, 4000),
        name="lists",
    )(where, theirs, index)


def fill(window, start, panel, tile_major):
    size = window.shape[2]
    if tile_major:
        window[start : start + panel.shape[0]] = panel[...]
    else:
        for t in range(panel.shape[1] // size):
            window[start + t] = panel[:, t * size : (t + 1) * size]


def row_block(start, index, order, turned, inverse, window, image):
    slots = turned.shape[1] // turned.shape[2]
    picked = [order[start + u] for u in range(BLOCK)]
    vectors = [
        jnp.concatenate([window[index[r * slots + s]] for s in range(slots)], axis=1)
        for r in picked
    ]
    sums = [
        lax.dot_general(x, turned[r], NN, preferred_element_type=F32)
        for x, r in zip(vectors, picked)
    ]
    for r, y in zip(picked, sums):
        image[r] = (y * inverse[pl.ds(r, 1), :]).astype(image.dtype)


def near_kernel(tile_major, index, order, turned, inverse, own, mate, window, image):
    rows = turned.shape[0]
    fill(window, 0, own, tile_major)
    fill(window, rows, mate, tile_major)

    def step(block, carry):
        row_block(block * BLOCK, index, order, turned, inverse, window, image)
        return carry

    lax.fori_loop(0, (order[rows] + BLOCK - 1) // BLOCK, step, 0)


def far_rows(index, order, turned, inverse, window, image):
    rows = turned.shape[0]

    def step(block, carry):
        start = rows - (block + 1) * BLOCK
        row_block(start, index, order, turned, inverse, window, image)
        return carry

    lax.fori_loop(0, (rows - order[rows] + BLOCK - 1) // BLOCK, step, 0)


def far_kernel(tile_major, packs, count, *refs):
    index, order, turned, inverse, sending = refs[:5]
    arrived = refs[5 : 5 + count]
    window, image = refs[7 + count : 9 + count]
    rows = turned.shape[0]
    start = 2 * rows
    for panel in arrived:
        fill(window, start, panel, tile_major)
        start += panel.shape[0]
    far_rows(index, order, turned, inverse, window, image)
    if packs:
        send, rest = refs[9 + count :]
        limit = send.shape[0]
        for k in range(rows):
            target = send.at[k] if k < limit else rest.at[k - limit]
            target[...] = image[sending[k]]


def product(plan, panels, tile_major, kind, limit):
    near_index, far_index, order, turned, inverse, sending = plan
    own, mate, *arrived = panels
    rows, depth, size = turned.shape
    vectors = own.shape[1 if tile_major else 0]
    shapes = (
        pltpu.VMEM((3 * rows, vectors, size), BF16),
        pltpu.VMEM((rows, vectors, size), kind),
    )
    estimate = cost(rows * depth * size * vectors, 2 * rows * depth * size)
    window, image = pl.pallas_call(
        functools.partial(near_kernel, tile_major),
        out_shape=shapes,
        in_specs=[SM, SM, VM, VM, VM, VM],
        out_specs=(VM, VM),
        compiler_params=params(4),
        cost_estimate=estimate,
        name="near_rows",
    )(near_index, order, *map(in_vmem, (turned, inverse, own, mate)))
    packs = limit > 0
    if packs:
        shapes += (
            pltpu.VMEM((limit, vectors, size), kind),
            pltpu.VMEM((rows - limit, vectors, size), kind),
        )
    count = len(arrived)
    return pl.pallas_call(
        functools.partial(far_kernel, tile_major, packs, count),
        out_shape=shapes,
        in_specs=[SM, SM, VM, VM, SM] + [VM] * (count + 2),
        out_specs=(VM,) * len(shapes),
        input_output_aliases={5 + count: 0, 6 + count: 1},
        compiler_params=params(4),
        cost_estimate=estimate,
        name="far_rows",
    )(
        far_index,
        order,
        in_vmem(turned),
        in_vmem(inverse),
        sending,
        *map(in_vmem, (*arrived, window, image)),
    )[1:]


def thirds(x):
    high = x.astype(BF16)
    rest = x - high.astype(F32)
    middle = rest.astype(BF16)
    low = (rest - middle.astype(F32)).astype(BF16)
    return high, middle, low


def fold(product3, vectors):
    total = None
    for a, b in ((2, 2), (1, 2), (2, 1), (0, 2), (2, 0), (1, 1), (0, 1), (1, 0), (0, 0)):
        part = product3[
            a * vectors : (a + 1) * vectors, b * vectors : (b + 1) * vectors
        ]
        total = part if total is None else total + part
    return total


def gram_kernel(power, parts, gram):
    rows, vectors, size = power.shape
    group = 8

    def step(block, total):
        taken = []
        for u in range(group):
            r = block * group + u
            stacked = jnp.concatenate(thirds(power[r]), axis=0)
            parts[r] = stacked
            taken.append(stacked)
        wide = jnp.concatenate(taken, axis=1)
        return total + lax.dot_general(wide, wide, NT, preferred_element_type=F32)

    total = lax.fori_loop(
        0, rows // group, step, jnp.zeros((3 * vectors, 3 * vectors), F32)
    )
    gram[...] = fold(total, vectors)


def gram_local(power):
    rows, vectors, size = power.shape
    return pl.pallas_call(
        gram_kernel,
        out_shape=(
            pltpu.VMEM((rows, 3 * vectors, size), BF16),
            pltpu.VMEM((vectors, vectors), F32),
        ),
        in_specs=[VM],
        out_specs=(VM, VM),
        compiler_params=params(4),
        cost_estimate=cost(18 * power.size * vectors, 10 * power.size),
        name="gram",
    )(in_vmem(power))


def inverse_factor(gram):
    count = gram.shape[0]
    row = lax.broadcasted_iota(jnp.int32, (count, count), 0)
    column = lax.broadcasted_iota(jnp.int32, (count, count), 1)
    work = jnp.concatenate([gram, jnp.where(row == column, 1.0, 0.0)], axis=1)
    below = lax.broadcasted_iota(jnp.int32, work.shape, 0)
    for k in range(count):
        pivot = work[k : k + 1]
        scaled = pivot * lax.rsqrt(pivot[:, k : k + 1])
        column_k = jnp.broadcast_to(work[:, k : k + 1], work.shape)
        head = lax.rsqrt(pivot[:, k : k + 1])
        work = jnp.where(
            below > k,
            work - (column_k * head) * scaled,
            jnp.where(below == k, scaled, work),
        )
    return work[:, count:]


def final_kernel(states, gram_a, gram_b, mapping, parts, out):
    rows, depth, size = parts.shape
    vectors = depth // 3
    total = (gram_a[...] + gram_b[...]) / states
    factor = inverse_factor(total)
    combined = lax.dot_general(
        mapping[...],
        factor,
        (((0,), (0,)), ((), ())),
        precision=lax.Precision.HIGHEST,
        preferred_element_type=F32,
    )
    high, middle, low = thirds(combined)
    blank = jnp.zeros_like(high)
    left = jnp.concatenate(
        [
            jnp.concatenate([high, high, high], axis=1),
            jnp.concatenate([middle, middle, blank], axis=1),
            jnp.concatenate([low, blank, blank], axis=1),
        ],
        axis=0,
    )
    for r in range(rows):
        y = lax.dot_general(left, parts[r], NN, preferred_element_type=F32)
        out[:, r * size : (r + 1) * size] = (
            y[2 * vectors :] + y[vectors : 2 * vectors]
        ) + y[:vectors]


def final(states, gram_a, gram_b, mapping, parts):
    rows, depth, size = parts.shape
    vectors = depth // 3
    return pl.pallas_call(
        functools.partial(final_kernel, float(states)),
        out_shape=jax.ShapeDtypeStruct((vectors, rows * size), F32),
        in_specs=[VM, VM, VM, VM],
        out_specs=VM,
        compiler_params=params(8),
        cost_estimate=cost(6 * parts.size * vectors, 4 * parts.size),
        name="memberships",
    )(gram_a, gram_b, mapping, in_vmem(parts))


def body(transition_tiles, column_tiles, schur_basis, membership_map):
    rows = transition_tiles.shape[0]
    count = lax.axis_size("rows")
    me = lax.axis_index("rows")
    mates = [(i, i ^ 1) for i in range(count)]
    others = []
    for i in range(1, count - 1, 2):
        others += [(i, i + 1), (i + 1, i)]

    def swap(array, pairs):
        return lax.ppermute(array, "rows", pairs)

    limit = 11 * rows // 16
    where = jnp.stack([me * rows, me % 2]).astype(jnp.int32)
    columns = column_tiles.T
    theirs = swap(columns, others)
    panels = schur_basis, swap(schur_basis, mates), swap(schur_basis, others)
    turned, inverse, index, order = prep(where, columns, transition_tiles)
    packed, sending, more = lists(limit, where, theirs, index)
    plan = (index, index, order, turned, inverse, sending)
    image, send, rest = product(plan, panels, False, BF16, limit)
    plan = (index, packed, order, turned, inverse, sending)
    for step in range(1, PRODUCTS):
        mate, other = swap(image, mates), swap(send, others)
        extra = lax.cond(more[0] > 0, lambda x: swap(x, others), lambda x: x, rest)
        last = step == PRODUCTS - 1
        out = product(
            plan, (image, mate, other, extra), True, F32 if last else BF16, 0 if last else limit
        )
        if last:
            (image,) = out
        else:
            image, send, rest = out
    parts, gram = gram_local(image)
    distance = 1
    while distance < count:
        partner = lax.ppermute(gram, "rows", [(i, i ^ distance) for i in range(count)])
        distance *= 2
        if distance < count:
            gram = gram + partner
    states = schur_basis.shape[1] * count
    return final(states, gram, partner, membership_map, parts)


def solution(mesh):
    return jax.shard_map(
        body,
        mesh=mesh,
        in_specs=(
            P(("groups", "rows"), None, None, None),
            P(("groups", "rows"), None),
            P(None, ("groups", "rows")),
            P("groups", None),
        ),
        out_specs=P(None, ("groups", "rows")),
        check_vma=False,
    )
```

```python
import functools

import jax
import jax.numpy as jnp
from jax import lax
from jax.experimental import pallas as pl
from jax.experimental.pallas import tpu as pltpu
from jax.sharding import PartitionSpec as P

PRODUCTS = 4
BLOCK = 16
CHUNK = 8
F32 = jnp.float32
BF16 = jnp.bfloat16
I32 = jnp.int32
NN = (((1,), (0,)), ((), ()))
NT = (((1,), (1,)), ((), ()))
VM = pl.BlockSpec(memory_space=pltpu.VMEM)
SM = pl.BlockSpec(memory_space=pltpu.SMEM)
HB = pl.BlockSpec(memory_space=pltpu.HBM)


def in_vmem(array):
    return pltpu.with_memory_space_constraint(array, pltpu.VMEM)


def cost(flops, moved):
    return pl.CostEstimate(flops=flops, bytes_accessed=moved, transcendentals=0)


def params(mib):
    return pltpu.CompilerParams(vmem_limit_bytes=mib * 2**20)


def prep_kernel(tiles, turned, inverse, landing, arrived):
    rows, slots, size, _ = tiles.shape
    chunks = rows // CHUNK
    ones = jnp.ones((16, slots * size), BF16)

    def copy(i):
        part = pl.ds(i * CHUNK, CHUNK)
        return pltpu.make_async_copy(tiles.at[part], landing.at[part], arrived.at[i])

    for i in range(chunks):
        copy(i).start()

    def step(i, carry):
        copy(i).wait()
        for u in range(CHUNK):
            r = i * CHUNK + u
            for s in range(slots):
                turned[r, pl.ds(s * size, size), :] = landing[r, s].T
            total = lax.dot_general(ones, turned[r], NN, preferred_element_type=F32)
            inverse[pl.ds(r, 1), :] = 1.0 / total[0:1]
        return carry

    lax.fori_loop(0, chunks, step, 0)


def prep(tiles):
    rows, slots, size, _ = tiles.shape
    return pl.pallas_call(
        prep_kernel,
        out_shape=(
            pltpu.VMEM((rows, slots * size, size), BF16),
            pltpu.VMEM((rows, size), F32),
        ),
        in_specs=[HB],
        out_specs=(VM, VM),
        scratch_shapes=[
            pltpu.VMEM(tiles.shape, BF16),
            pltpu.SemaphoreType.DMA((rows // CHUNK,)),
        ],
        compiler_params=params(14),
        cost_estimate=cost(2 * tiles.size * 16, 4 * tiles.size),
        name="prep",
    )(pltpu.with_memory_space_constraint(tiles, pltpu.HBM))


def ranks(named):
    rows = named.shape[0]
    h = lax.broadcasted_iota(I32, (rows, rows), 0)
    other = lax.broadcasted_iota(I32, (rows, rows), 1)
    before = jnp.where(other < h, 1.0, 0.0).astype(BF16)
    ones = jnp.ones((rows, rows), BF16)
    total = lax.dot_general(named.astype(BF16), ones, NN, preferred_element_type=F32)
    mark = jnp.where(total > 0.5, 1.0, 0.0)
    rank = lax.dot_general(before, mark.astype(BF16), NN, preferred_element_type=F32)
    return mark, rank


def plan_kernel(where, columns, plan, draft, done):
    slots, rows = columns.shape
    first, parity = where[0], where[1]
    low = jnp.where(parity == 0, 2 * rows, rows)
    high = jnp.where(parity == 0, rows, 2 * rows)
    offset = columns[...] - first
    spot = jnp.where(
        offset < 0,
        offset + (rows + low),
        jnp.where(offset >= rows, offset + (high - rows), offset),
    )
    h = lax.broadcasted_iota(I32, (rows, rows), 0)
    lane = lax.broadcasted_iota(I32, (rows, rows), 1)
    equal = [
        jnp.where(spot[s : s + 1] - 2 * rows == h, 1.0, 0.0) for s in range(slots)
    ]
    named = functools.reduce(jnp.add, equal)
    mark, rank = ranks(named)
    draft[0:slots, 0:rows] = spot
    for s in range(slots):
        place = jnp.sum(equal[s] * rank, axis=0, keepdims=True).astype(I32)
        line = spot[s : s + 1]
        draft[slots + s : slots + s + 1, 0:rows] = jnp.where(
            line >= 2 * rows, 2 * rows + place, line
        )
    far = jnp.where(jnp.sum(named, axis=0, keepdims=True) > 0.5, 1.0, 0.0)
    far = jnp.broadcast_to(far, (16, rows))
    before = jnp.where(h < lane, 1.0, 0.0).astype(BF16)
    far_before = lax.dot_general(far.astype(BF16), before, NN, preferred_element_type=F32)
    line = lax.broadcasted_iota(I32, (16, rows), 1).astype(F32)
    position = jnp.where(far > 0.5, rows - 1 - far_before, line - far_before)
    taken = jnp.where(position[0:1].astype(I32) == h, 1.0, 0.0).astype(BF16)
    order = lax.dot_general(line.astype(BF16), taken, NT, preferred_element_type=F32)
    ones = jnp.ones((rows, rows), BF16)
    near = lax.dot_general((1.0 - far).astype(BF16), ones, NN, preferred_element_type=F32)
    base = 2 * slots
    draft[base : base + 1, 0:rows] = order[0:1].astype(I32)
    draft[base + 1 : base + 2, 0:rows] = near[0:1].astype(I32)
    draft[base + 2 : base + 3, 0:rows] = jnp.sum(mark, axis=0, keepdims=True).astype(I32)
    copy = pltpu.make_async_copy(draft, plan, done)
    copy.start()
    copy.wait()


def make_plan(where, columns):
    slots, _ = columns.shape
    height = (2 * slots + 3 + 7) // 8 * 8
    return pl.pallas_call(
        plan_kernel,
        out_shape=pltpu.SMEM((height, 128), I32),
        in_specs=[SM, VM],
        out_specs=SM,
        scratch_shapes=[pltpu.VMEM((height, 128), I32), pltpu.SemaphoreType.DMA],
        compiler_params=params(2),
        cost_estimate=cost(1000000, 4000),
        name="plan",
    )(where, columns)


def fill(window, start, panel, tile_major):
    size = window.shape[2]
    if tile_major:
        window[start : start + panel.shape[0]] = panel[...]
    else:
        for t in range(panel.shape[1] // size):
            window[start + t] = panel[:, t * size : (t + 1) * size]


def row_block(start, base, plan, turned, inverse, window):
    slots = turned.shape[1] // turned.shape[2]
    picked = [plan[2 * slots, start + u] for u in range(BLOCK)]
    vectors = [
        jnp.concatenate([window[plan[base + s, r]] for s in range(slots)], axis=1)
        for r in picked
    ]
    sums = [
        lax.dot_general(x, turned[r], NN, preferred_element_type=F32)
        for x, r in zip(vectors, picked)
    ]
    return picked, [y * inverse[pl.ds(r, 1), :] for r, y in zip(picked, sums)]


def thirds(x):
    high = x.astype(BF16)
    rest = x - high.astype(F32)
    middle = rest.astype(BF16)
    low = (rest - middle.astype(F32)).astype(BF16)
    return high, middle, low


def fold(squares, vectors):
    total = None
    for a, b in ((2, 2), (1, 2), (2, 1), (0, 2), (2, 0), (1, 1), (0, 1), (1, 0), (0, 0)):
        part = squares[a * vectors : (a + 1) * vectors, b * vectors : (b + 1) * vectors]
        total = part if total is None else total + part
    return total


def run_rows(near_side, base, plan, turned, inverse, window, image, squares):
    rows = turned.shape[0]
    slots = turned.shape[1] // turned.shape[2]
    near = plan[2 * slots + 1, 0]
    count = near if near_side else rows - near

    def step(block, total):
        start = block * BLOCK if near_side else rows - (block + 1) * BLOCK
        picked, results = row_block(start, base, plan, turned, inverse, window)
        if squares is None:
            for r, y in zip(picked, results):
                image[r] = y.astype(BF16)
            return total
        counted = []
        for u, (r, y) in enumerate(zip(picked, results)):
            stacked = jnp.concatenate(thirds(y), axis=0)
            image[r] = stacked
            mine = start + u < near if near_side else start + u >= near
            counted.append(jnp.where(mine, stacked, jnp.zeros_like(stacked)))
        wide = jnp.concatenate(counted, axis=1)
        return total + lax.dot_general(wide, wide, NT, preferred_element_type=F32)

    begin = jnp.int32(0) if squares is None else squares
    return lax.fori_loop(0, (count + BLOCK - 1) // BLOCK, step, begin)


def near_kernel(tile_major, last, plan, turned, inverse, own, mate, window, image, *gram):
    rows, depth, size = turned.shape
    fill(window, 0, own, tile_major)
    fill(window, rows, mate, tile_major)
    zero = jnp.zeros(gram[0].shape, F32) if last else None
    total = run_rows(True, 0, plan, turned, inverse, window, image, zero)
    if last:
        gram[0][...] = total


def far_first_kernel(
    limit, where, theirs, plan, turned, inverse, other, w_in, i_in,
    window, image, send, rest, sending, more, draft, done,
):
    slots, rows = theirs.shape
    offset = theirs[...] - where[0]
    h = lax.broadcasted_iota(I32, (rows, rows), 0)
    lane = lax.broadcasted_iota(I32, (rows, rows), 1)
    named = functools.reduce(
        jnp.add,
        [jnp.where(offset[s : s + 1] == h, 1.0, 0.0) for s in range(slots)],
    )
    mark, rank = ranks(named)
    here = jnp.where((mark > 0.5) & (rank.astype(I32) == lane), h, 0)
    draft[0:1, 0:rows] = jnp.sum(here.astype(F32), axis=0, keepdims=True).astype(I32)
    sent = jnp.sum(mark, axis=0, keepdims=True).astype(I32)
    read = plan[2 * slots + 2, 0]
    draft[1:2, 0:rows] = jnp.where(jnp.maximum(sent, read) > limit, 1, 0)
    copy = pltpu.make_async_copy(draft, sending, done)
    copy.start()
    fill(window, 2 * rows, other, False)
    run_rows(False, 0, plan, turned, inverse, window, image, None)
    copy.wait()
    more[0] = sending[1, 0]
    pack(image, sending, send, rest)


def pack(image, sending, send, rest):
    limit = send.shape[0]
    for k in range(image.shape[0]):
        target = send.at[k] if k < limit else rest.at[k - limit]
        target[...] = image[sending[0, k]]


def far_kernel(plan, turned, inverse, sending, other, extra, w_in, i_in, window, image, send, rest):
    rows, depth, size = turned.shape
    limit = other.shape[0]
    fill(window, 2 * rows, other, True)
    fill(window, 2 * rows + limit, extra, True)
    run_rows(False, depth // size, plan, turned, inverse, window, image, None)
    pack(image, sending, send, rest)


def far_last_kernel(plan, turned, inverse, other, extra, near, w_in, i_in, window, image, gram):
    rows, depth, size = turned.shape
    limit = other.shape[0]
    fill(window, 2 * rows, other, True)
    fill(window, 2 * rows + limit, extra, True)
    total = run_rows(
        False, depth // size, plan, turned, inverse, window, image, near[...]
    )
    gram[...] = fold(total, gram.shape[0])


def near_rows(plan, turned, inverse, own, mate, tile_major, last):
    rows, depth, size = turned.shape
    vectors = own.shape[1 if tile_major else 0]
    height = 3 * vectors if last else vectors
    shapes = (
        pltpu.VMEM((3 * rows, vectors, size), BF16),
        pltpu.VMEM((rows, height, size), BF16),
    )
    if last:
        shapes += (pltpu.VMEM((height, height), F32),)
    return pl.pallas_call(
        functools.partial(near_kernel, tile_major, last),
        out_shape=shapes,
        in_specs=[SM, VM, VM, VM, VM],
        out_specs=(VM,) * len(shapes),
        compiler_params=params(4),
        cost_estimate=cost(rows * depth * size * vectors, 2 * rows * depth * size),
        name="near_rows",
    )(plan, *map(in_vmem, (turned, inverse, own, mate)))


def far_call(kernel, ins, in_specs, alias, outs, out_specs, turned, scratch=()):
    rows, depth, size = turned.shape
    return pl.pallas_call(
        kernel,
        out_shape=outs,
        in_specs=in_specs,
        out_specs=out_specs,
        scratch_shapes=scratch,
        input_output_aliases={alias: 0, alias + 1: 1},
        compiler_params=params(4),
        cost_estimate=cost(32 * rows * depth * size, 2 * rows * depth * size),
        name="far_rows",
    )(*ins)


def of(array):
    return pltpu.VMEM(array.shape, array.dtype)


def far_rows_first(limit, where, theirs, plan, turned, inverse, other, window, image):
    rows, vectors, size = image.shape
    return far_call(
        functools.partial(far_first_kernel, limit),
        (where, theirs, plan, *map(in_vmem, (turned, inverse, other, window, image))),
        [SM, VM, SM] + [VM] * 5,
        6,
        (
            of(window),
            of(image),
            pltpu.VMEM((limit, vectors, size), BF16),
            pltpu.VMEM((rows - limit, vectors, size), BF16),
            pltpu.SMEM((8, 128), I32),
            jax.ShapeDtypeStruct((1,), I32),
        ),
        (VM, VM, VM, VM, SM, SM),
        turned,
        [pltpu.VMEM((8, 128), I32), pltpu.SemaphoreType.DMA],
    )[1:]


def far_rows(plan, turned, inverse, sending, other, extra, window, image):
    return far_call(
        far_kernel,
        (
            plan,
            in_vmem(turned),
            in_vmem(inverse),
            sending,
            *map(in_vmem, (other, extra, window, image)),
        ),
        [SM, VM, VM, SM] + [VM] * 4,
        6,
        (of(window), of(image), of(other), of(extra)),
        (VM,) * 4,
        turned,
    )[1:]


def far_rows_last(plan, turned, inverse, other, extra, near, window, image):
    vectors = near.shape[0] // 3
    return far_call(
        far_last_kernel,
        (plan, *map(in_vmem, (turned, inverse, other, extra, near, window, image))),
        [SM] + [VM] * 7,
        6,
        (of(window), of(image), pltpu.VMEM((vectors, vectors), F32)),
        (VM,) * 3,
        turned,
    )[1:]


def inverse_factor(gram):
    count = gram.shape[0]
    step = 8
    row = lax.broadcasted_iota(I32, (count, count), 0)
    column = lax.broadcasted_iota(I32, (count, count), 1)
    work = jnp.concatenate([gram, jnp.where(row == column, 1.0, 0.0)], axis=1)
    below = lax.broadcasted_iota(I32, work.shape, 0)
    for begin in range(0, count, step):
        spread = [
            jnp.broadcast_to(work[:, k : k + 1], work.shape)
            for k in range(begin, begin + step)
        ]
        for j in range(step):
            k = begin + j
            factor = jnp.where(below > k, spread[j], 0.0)
            pivot = 1.0 / spread[j][k : k + 1]
            for q in range(j + 1, step):
                spread[q] = spread[q] - factor * (spread[q][k : k + 1] * pivot)
            work = work - factor * (work[k : k + 1] * pivot)
    pivots = jnp.sum(
        jnp.where(row == column, work[:, :count], 0.0), axis=1, keepdims=True
    )
    return work[:, count:] * lax.rsqrt(pivots)


def final_kernel(states, gram_a, gram_b, mapping, parts, out, ready, sent):
    rows, depth, size = parts.shape
    vectors = depth // 3
    factor = inverse_factor((gram_a[...] + gram_b[...]) / states)
    combined = lax.dot_general(
        mapping[...],
        factor,
        (((0,), (0,)), ((), ())),
        precision=lax.Precision.HIGHEST,
        preferred_element_type=F32,
    )
    high, middle, low = thirds(combined)
    blank = jnp.zeros_like(high)
    left = jnp.concatenate(
        [
            jnp.concatenate([high, high, high], axis=1),
            jnp.concatenate([middle, middle, blank], axis=1),
            jnp.concatenate([low, blank, blank], axis=1),
        ],
        axis=0,
    )
    copies = []
    for g in range(rows // CHUNK):
        for r in range(g * CHUNK, (g + 1) * CHUNK):
            y = lax.dot_general(left, parts[r], NN, preferred_element_type=F32)
            ready[:, r * size : (r + 1) * size] = (
                y[2 * vectors :] + y[vectors : 2 * vectors]
            ) + y[:vectors]
        part = pl.ds(g * CHUNK * size, CHUNK * size)
        copies.append(pltpu.make_async_copy(ready.at[:, part], out.at[:, part], sent.at[g]))
        copies[-1].start()
    for copy in copies:
        copy.wait()


def final(states, gram_a, gram_b, mapping, parts):
    rows, depth, size = parts.shape
    vectors = depth // 3
    return pl.pallas_call(
        functools.partial(final_kernel, float(states)),
        out_shape=jax.ShapeDtypeStruct((vectors, rows * size), F32),
        in_specs=[VM, VM, VM, VM],
        out_specs=HB,
        scratch_shapes=[
            pltpu.VMEM((vectors, rows * size), F32),
            pltpu.SemaphoreType.DMA((rows // CHUNK,)),
        ],
        compiler_params=params(8),
        cost_estimate=cost(6 * parts.size * vectors, 4 * parts.size),
        name="memberships",
    )(gram_a, gram_b, mapping, in_vmem(parts))


def body(transition_tiles, column_tiles, schur_basis, membership_map):
    rows = transition_tiles.shape[0]
    count = lax.axis_size("rows")
    me = lax.axis_index("rows")
    mates = [(i, i ^ 1) for i in range(count)]
    others = []
    for i in range(1, count - 1, 2):
        others += [(i, i + 1), (i + 1, i)]

    def swap(array, pairs):
        return lax.ppermute(array, "rows", pairs)

    limit = 11 * rows // 16
    where = jnp.stack([me * rows, me % 2]).astype(I32)
    columns = column_tiles.T
    mate, other = swap(schur_basis, mates), swap(schur_basis, others)
    theirs = swap(columns, others)
    plan = make_plan(where, columns)
    turned, inverse = prep(transition_tiles)
    window, image = near_rows(plan, turned, inverse, schur_basis, mate, False, False)
    image, send, rest, sending, more = far_rows_first(
        limit, where, theirs, plan, turned, inverse, other, window, image
    )
    for step in range(1, PRODUCTS):
        last = step == PRODUCTS - 1
        mate, other = swap(image, mates), swap(send, others)
        extra = lax.cond(more[0] > 0, lambda x: swap(x, others), lambda x: x, rest)
        window, image, *near = near_rows(plan, turned, inverse, image, mate, True, last)
        if last:
            parts, gram = far_rows_last(
                plan, turned, inverse, other, extra, near[0], window, image
            )
        else:
            image, send, rest = far_rows(
                plan, turned, inverse, sending, other, extra, window, image
            )
    distance = 1
    while distance < count:
        partner = swap(gram, [(i, i ^ distance) for i in range(count)])
        distance *= 2
        if distance < count:
            gram = gram + partner
    states = schur_basis.shape[1] * count
    return final(states, gram, partner, membership_map, parts)


def solution(mesh):
    return jax.shard_map(
        body,
        mesh=mesh,
        in_specs=(
            P(("groups", "rows"), None, None, None),
            P(("groups", "rows"), None),
            P(None, ("groups", "rows")),
            P("groups", None),
        ),
        out_specs=P(None, ("groups", "rows")),
        check_vma=False,
    )
```

```python
import functools

import jax
import jax.numpy as jnp
from jax import lax
from jax.experimental import pallas as pl
from jax.experimental.pallas import tpu as pltpu
from jax.sharding import PartitionSpec as P

PRODUCTS = 4
BLOCK = 16
CHUNK = 8
F32 = jnp.float32
BF16 = jnp.bfloat16
I32 = jnp.int32
NN = (((1,), (0,)), ((), ()))
NT = (((1,), (1,)), ((), ()))
VM = pl.BlockSpec(memory_space=pltpu.VMEM)
SM = pl.BlockSpec(memory_space=pltpu.SMEM)
HB = pl.BlockSpec(memory_space=pltpu.HBM)


def in_vmem(array):
    return pltpu.with_memory_space_constraint(array, pltpu.VMEM)


def in_hbm(array):
    return pltpu.with_memory_space_constraint(array, pltpu.HBM)


def cost(flops, moved):
    return pl.CostEstimate(flops=flops, bytes_accessed=moved, transcendentals=0)


def params(mib):
    return pltpu.CompilerParams(vmem_limit_bytes=mib * 2**20)


def ranks(named):
    rows = named.shape[0]
    h = lax.broadcasted_iota(I32, (rows, rows), 0)
    other = lax.broadcasted_iota(I32, (rows, rows), 1)
    before = jnp.where(other < h, 1.0, 0.0).astype(BF16)
    ones = jnp.ones((rows, rows), BF16)
    total = lax.dot_general(named.astype(BF16), ones, NN, preferred_element_type=F32)
    mark = jnp.where(total > 0.5, 1.0, 0.0)
    rank = lax.dot_general(before, mark.astype(BF16), NN, preferred_element_type=F32)
    return mark, rank


def draft_plan(first, parity, columns, draft, wanted):
    slots, rows = columns.shape
    low = jnp.where(parity == 0, 2 * rows, rows)
    high = jnp.where(parity == 0, rows, 2 * rows)
    offset = columns - first
    spot = jnp.where(
        offset < 0,
        offset + (rows + low),
        jnp.where(offset >= rows, offset + (high - rows), offset),
    )
    h = lax.broadcasted_iota(I32, (rows, rows), 0)
    lane = lax.broadcasted_iota(I32, (rows, rows), 1)
    equal = [
        jnp.where(spot[s : s + 1] - 2 * rows == h, 1.0, 0.0) for s in range(slots)
    ]
    named = functools.reduce(jnp.add, equal)
    mark, rank = ranks(named)
    draft[0:slots, 0:rows] = spot
    for s in range(slots):
        place = jnp.sum(equal[s] * rank, axis=0, keepdims=True).astype(I32)
        line = spot[s : s + 1]
        draft[slots + s : slots + s + 1, 0:rows] = jnp.where(
            line >= 2 * rows, 2 * rows + place, line
        )
    far = jnp.where(jnp.sum(named, axis=0, keepdims=True) > 0.5, 1.0, 0.0)
    far = jnp.broadcast_to(far, (16, rows))
    before = jnp.where(h < lane, 1.0, 0.0).astype(BF16)
    far_before = lax.dot_general(far.astype(BF16), before, NN, preferred_element_type=F32)
    line = lax.broadcasted_iota(I32, (16, rows), 1).astype(F32)
    position = jnp.where(far > 0.5, rows - 1 - far_before, line - far_before)
    taken = jnp.where(position[0:1].astype(I32) == h, 1.0, 0.0).astype(BF16)
    order = lax.dot_general(line.astype(BF16), taken, NT, preferred_element_type=F32)
    ones = jnp.ones((rows, rows), BF16)
    near = lax.dot_general((1.0 - far).astype(BF16), ones, NN, preferred_element_type=F32)
    base = 2 * slots
    draft[base : base + 1, 0:rows] = order[0:1].astype(I32)
    draft[base + 1 : base + 2, 0:rows] = near[0:1].astype(I32)
    read = jnp.sum(mark, axis=0, keepdims=True).astype(I32)
    draft[base + 2 : base + 3, 0:rows] = read
    here = jnp.where((mark > 0.5) & (rank.astype(I32) == lane), h, 0)
    wanted[0:1, 0:rows] = jnp.sum(here.astype(F32), axis=0, keepdims=True).astype(I32)
    wanted[1:2, 0:rows] = read


def prep_kernel(
    where, columns, tiles, turned, inverse, plan, wanted, kept,
    landing, named, draft, arrived, left, here, done,
):
    rows, slots, size, _ = tiles.shape
    chunks = rows // CHUNK
    ones = jnp.ones((16, slots * size), BF16)

    def part(i):
        return pl.ds(i * CHUNK, CHUNK)

    def copy_in(i):
        return pltpu.make_async_copy(tiles.at[part(i)], landing.at[part(i)], arrived.at[i])

    def copy_out(i):
        return pltpu.make_async_copy(turned.at[part(i)], kept.at[part(i)], left.at[i])

    copy_columns = pltpu.make_async_copy(columns, named, here)
    copy_columns.start()
    for i in range(chunks):
        copy_in(i).start()
    copy_columns.wait()
    draft_plan(where[0], where[1], named[...], draft, wanted)
    copy_plan = pltpu.make_async_copy(draft, plan, done)
    copy_plan.start()

    def step(i, carry):
        copy_in(i).wait()
        for u in range(CHUNK):
            r = i * CHUNK + u
            for s in range(slots):
                turned[r, pl.ds(s * size, size), :] = landing[r, s].T
            total = lax.dot_general(ones, turned[r], NN, preferred_element_type=F32)
            inverse[pl.ds(r, 1), :] = 1.0 / total[0:1]
        copy_out(i).start()
        return carry

    lax.fori_loop(0, chunks, step, 0)
    copy_plan.wait()
    for i in range(chunks):
        copy_out(i).wait()


def prep(where, columns, tiles):
    rows, slots, size, _ = tiles.shape
    height = (2 * slots + 3 + 7) // 8 * 8
    return pl.pallas_call(
        prep_kernel,
        out_shape=(
            pltpu.VMEM((rows, slots * size, size), BF16),
            pltpu.VMEM((rows, size), F32),
            pltpu.SMEM((height, 128), I32),
            pltpu.VMEM((8, 128), I32),
            pltpu.HBM((rows, slots * size, size), BF16),
        ),
        in_specs=[SM, HB, HB],
        out_specs=(VM, VM, SM, VM, HB),
        scratch_shapes=[
            pltpu.VMEM(tiles.shape, BF16),
            pltpu.VMEM(columns.shape, I32),
            pltpu.VMEM((height, 128), I32),
            pltpu.SemaphoreType.DMA((rows // CHUNK,)),
            pltpu.SemaphoreType.DMA((rows // CHUNK,)),
            pltpu.SemaphoreType.DMA,
            pltpu.SemaphoreType.DMA,
        ],
        compiler_params=params(14),
        cost_estimate=cost(2 * tiles.size * 16, 4 * tiles.size),
        name="prep",
    )(where, in_hbm(columns), in_hbm(tiles))


def fill(window, start, panel, tile_major):
    size = window.shape[2]
    if tile_major:
        window[start : start + panel.shape[0]] = panel[...]
    else:
        for t in range(panel.shape[1] // size):
            window[start + t] = panel[:, t * size : (t + 1) * size]


def row_block(start, base, plan, turned, inverse, window):
    slots = turned.shape[1] // turned.shape[2]
    picked = [plan[2 * slots, start + u] for u in range(BLOCK)]
    vectors = [
        jnp.concatenate([window[plan[base + s, r]] for s in range(slots)], axis=1)
        for r in picked
    ]
    sums = [
        lax.dot_general(x, turned[r], NN, preferred_element_type=F32)
        for x, r in zip(vectors, picked)
    ]
    return picked, [y * inverse[pl.ds(r, 1), :] for r, y in zip(picked, sums)]


def thirds(x):
    high = x.astype(BF16)
    rest = x - high.astype(F32)
    middle = rest.astype(BF16)
    low = (rest - middle.astype(F32)).astype(BF16)
    return high, middle, low


def fold(squares, vectors):
    total = None
    for a, b in ((2, 2), (1, 2), (2, 1), (0, 2), (2, 0), (1, 1), (0, 1), (1, 0), (0, 0)):
        part = squares[a * vectors : (a + 1) * vectors, b * vectors : (b + 1) * vectors]
        total = part if total is None else total + part
    return total


def run_rows(near_side, base, plan, turned, inverse, window, image, squares):
    rows = turned.shape[0]
    slots = turned.shape[1] // turned.shape[2]
    near = plan[2 * slots + 1, 0]
    count = near if near_side else rows - near

    def step(block, total):
        start = block * BLOCK if near_side else rows - (block + 1) * BLOCK
        picked, results = row_block(start, base, plan, turned, inverse, window)
        if squares is None:
            for r, y in zip(picked, results):
                image[r] = y.astype(BF16)
            return total
        counted = []
        for u, (r, y) in enumerate(zip(picked, results)):
            stacked = jnp.concatenate(thirds(y), axis=0)
            image[r] = stacked
            mine = start + u < near if near_side else start + u >= near
            counted.append(jnp.where(mine, stacked, jnp.zeros_like(stacked)))
        wide = jnp.concatenate(counted, axis=1)
        return total + lax.dot_general(wide, wide, NT, preferred_element_type=F32)

    begin = jnp.int32(0) if squares is None else squares
    return lax.fori_loop(0, (count + BLOCK - 1) // BLOCK, step, begin)


def near_kernel(tile_major, last, plan, turned, inverse, own, mate, window, image, *gram):
    rows, depth, size = turned.shape
    fill(window, 0, own, tile_major)
    fill(window, rows, mate, tile_major)
    zero = jnp.zeros(gram[0].shape, F32) if last else None
    total = run_rows(True, 0, plan, turned, inverse, window, image, zero)
    if last:
        gram[0][...] = total


def far_first_kernel(
    limit, asked, plan, turned, inverse, other, w_in, i_in,
    window, image, send, rest, sending, more, done,
):
    rows, depth, size = turned.shape
    copy = pltpu.make_async_copy(asked, sending, done)
    copy.start()
    fill(window, 2 * rows, other, False)
    run_rows(False, 0, plan, turned, inverse, window, image, None)
    copy.wait()
    read = plan[2 * (depth // size) + 2, 0]
    more[0] = jnp.where(jnp.maximum(sending[1, 0], read) > limit, 1, 0)
    pack(image, sending, send, rest)


def pack(image, sending, send, rest):
    limit = send.shape[0]
    for k in range(image.shape[0]):
        target = send.at[k] if k < limit else rest.at[k - limit]
        target[...] = image[sending[0, k]]


def far_kernel(plan, turned, inverse, sending, other, extra, w_in, i_in, window, image, send, rest):
    rows, depth, size = turned.shape
    limit = other.shape[0]
    fill(window, 2 * rows, other, True)
    fill(window, 2 * rows + limit, extra, True)
    run_rows(False, depth // size, plan, turned, inverse, window, image, None)
    pack(image, sending, send, rest)


def far_last_kernel(plan, turned, inverse, other, extra, near, w_in, i_in, window, image, gram):
    rows, depth, size = turned.shape
    limit = other.shape[0]
    fill(window, 2 * rows, other, True)
    fill(window, 2 * rows + limit, extra, True)
    total = run_rows(
        False, depth // size, plan, turned, inverse, window, image, near[...]
    )
    gram[...] = fold(total, gram.shape[0])


def near_rows(plan, turned, inverse, own, mate, tile_major, last):
    rows, depth, size = turned.shape
    vectors = own.shape[1 if tile_major else 0]
    height = 3 * vectors if last else vectors
    shapes = (
        pltpu.VMEM((3 * rows, vectors, size), BF16),
        pltpu.VMEM((rows, height, size), BF16),
    )
    if last:
        shapes += (pltpu.VMEM((height, height), F32),)
    return pl.pallas_call(
        functools.partial(near_kernel, tile_major, last),
        out_shape=shapes,
        in_specs=[SM, VM, VM, VM, VM],
        out_specs=(VM,) * len(shapes),
        compiler_params=params(4),
        cost_estimate=cost(rows * depth * size * vectors, 2 * rows * depth * size),
        name="near_rows",
    )(plan, *map(in_vmem, (turned, inverse, own, mate)))


def far_call(kernel, ins, in_specs, alias, outs, out_specs, turned, scratch=()):
    rows, depth, size = turned.shape
    return pl.pallas_call(
        kernel,
        out_shape=outs,
        in_specs=in_specs,
        out_specs=out_specs,
        scratch_shapes=scratch,
        input_output_aliases={alias: 0, alias + 1: 1},
        compiler_params=params(4),
        cost_estimate=cost(32 * rows * depth * size, 2 * rows * depth * size),
        name="far_rows",
    )(*ins)


def of(array):
    return pltpu.VMEM(array.shape, array.dtype)


def far_rows_first(limit, asked, plan, turned, inverse, other, window, image):
    rows, vectors, size = image.shape
    return far_call(
        functools.partial(far_first_kernel, limit),
        (in_vmem(asked), plan, *map(in_vmem, (turned, inverse, other, window, image))),
        [VM, SM] + [VM] * 5,
        5,
        (
            of(window),
            of(image),
            pltpu.VMEM((limit, vectors, size), BF16),
            pltpu.VMEM((rows - limit, vectors, size), BF16),
            pltpu.SMEM((8, 128), I32),
            jax.ShapeDtypeStruct((1,), I32),
        ),
        (VM, VM, VM, VM, SM, SM),
        turned,
        [pltpu.SemaphoreType.DMA],
    )[1:]


def far_rows(plan, turned, inverse, sending, other, extra, window, image):
    return far_call(
        far_kernel,
        (
            plan,
            in_vmem(turned),
            in_vmem(inverse),
            sending,
            *map(in_vmem, (other, extra, window, image)),
        ),
        [SM, VM, VM, SM] + [VM] * 4,
        6,
        (of(window), of(image), of(other), of(extra)),
        (VM,) * 4,
        turned,
    )[1:]


def far_rows_last(plan, turned, inverse, other, extra, near, window, image):
    vectors = near.shape[0] // 3
    return far_call(
        far_last_kernel,
        (plan, *map(in_vmem, (turned, inverse, other, extra, near, window, image))),
        [SM] + [VM] * 7,
        6,
        (of(window), of(image), pltpu.VMEM((vectors, vectors), F32)),
        (VM,) * 3,
        turned,
    )[1:]


def inverse_factor(gram):
    count = gram.shape[0]
    step = 8
    row = lax.broadcasted_iota(I32, (count, count), 0)
    column = lax.broadcasted_iota(I32, (count, count), 1)
    work = jnp.concatenate([gram, jnp.where(row == column, 1.0, 0.0)], axis=1)
    below = lax.broadcasted_iota(I32, work.shape, 0)
    for begin in range(0, count, step):
        spread = [
            jnp.broadcast_to(work[:, k : k + 1], work.shape)
            for k in range(begin, begin + step)
        ]
        for j in range(step):
            k = begin + j
            factor = jnp.where(below > k, spread[j], 0.0)
            pivot = 1.0 / spread[j][k : k + 1]
            for q in range(j + 1, step):
                spread[q] = spread[q] - factor * (spread[q][k : k + 1] * pivot)
            work = work - factor * (work[k : k + 1] * pivot)
    pivots = jnp.sum(
        jnp.where(row == column, work[:, :count], 0.0), axis=1, keepdims=True
    )
    return work[:, count:] * lax.rsqrt(pivots)


def final_kernel(states, gram_a, gram_b, mapping, parts, out, ready, sent):
    rows, depth, size = parts.shape
    vectors = depth // 3
    factor = inverse_factor((gram_a[...] + gram_b[...]) / states)
    combined = lax.dot_general(
        mapping[...],
        factor,
        (((0,), (0,)), ((), ())),
        precision=lax.Precision.HIGHEST,
        preferred_element_type=F32,
    )
    high, middle, low = thirds(combined)
    blank = jnp.zeros_like(high)
    left = jnp.concatenate(
        [
            jnp.concatenate([high, high, high], axis=1),
            jnp.concatenate([middle, middle, blank], axis=1),
            jnp.concatenate([low, blank, blank], axis=1),
        ],
        axis=0,
    )
    copies = []
    for g in range(rows // CHUNK):
        for r in range(g * CHUNK, (g + 1) * CHUNK):
            y = lax.dot_general(left, parts[r], NN, preferred_element_type=F32)
            ready[:, r * size : (r + 1) * size] = (
                y[2 * vectors :] + y[vectors : 2 * vectors]
            ) + y[:vectors]
        part = pl.ds(g * CHUNK * size, CHUNK * size)
        copies.append(pltpu.make_async_copy(ready.at[:, part], out.at[:, part], sent.at[g]))
        copies[-1].start()
    for copy in copies:
        copy.wait()


def final(states, gram_a, gram_b, mapping, parts):
    rows, depth, size = parts.shape
    vectors = depth // 3
    return pl.pallas_call(
        functools.partial(final_kernel, float(states)),
        out_shape=jax.ShapeDtypeStruct((vectors, rows * size), F32),
        in_specs=[VM, VM, VM, VM],
        out_specs=HB,
        scratch_shapes=[
            pltpu.VMEM((vectors, rows * size), F32),
            pltpu.SemaphoreType.DMA((rows // CHUNK,)),
        ],
        compiler_params=params(8),
        cost_estimate=cost(6 * parts.size * vectors, 4 * parts.size),
        name="memberships",
    )(gram_a, gram_b, mapping, in_vmem(parts))


def body(transition_tiles, column_tiles, schur_basis, membership_map):
    rows = transition_tiles.shape[0]
    count = lax.axis_size("rows")
    me = lax.axis_index("rows")
    mates = [(i, i ^ 1) for i in range(count)]
    others = []
    for i in range(1, count - 1, 2):
        others += [(i, i + 1), (i + 1, i)]

    def swap(array, pairs):
        return lax.ppermute(array, "rows", pairs)

    limit = 11 * rows // 16
    where = jnp.stack([me * rows, me % 2]).astype(I32)
    columns = column_tiles.T
    mate, other = swap(schur_basis, mates), swap(schur_basis, others)
    turned, inverse, plan, wanted, kept = prep(where, columns, transition_tiles)
    asked = swap(wanted, others)
    window, image = near_rows(plan, turned, inverse, schur_basis, mate, False, False)
    image, send, rest, sending, more = far_rows_first(
        limit, asked, plan, turned, inverse, other, window, image
    )
    turned = kept
    for step in range(1, PRODUCTS):
        last = step == PRODUCTS - 1
        mate, other = swap(image, mates), swap(send, others)
        extra = lax.cond(more[0] > 0, lambda x: swap(x, others), lambda x: x, rest)
        window, image, *near = near_rows(plan, turned, inverse, image, mate, True, last)
        if last:
            parts, gram = far_rows_last(
                plan, turned, inverse, other, extra, near[0], window, image
            )
        else:
            image, send, rest = far_rows(
                plan, turned, inverse, sending, other, extra, window, image
            )
    distance = 1
    while distance < count:
        partner = swap(gram, [(i, i ^ distance) for i in range(count)])
        distance *= 2
        if distance < count:
            gram = gram + partner
    states = schur_basis.shape[1] * count
    return final(states, gram, partner, membership_map, parts)


def solution(mesh):
    return jax.shard_map(
        body,
        mesh=mesh,
        in_specs=(
            P(("groups", "rows"), None, None, None),
            P(("groups", "rows"), None),
            P(None, ("groups", "rows")),
            P("groups", None),
        ),
        out_specs=P(None, ("groups", "rows")),
        check_vma=False,
    )
```

```python
import functools

import jax
import jax.numpy as jnp
from jax import lax
from jax.experimental import pallas as pl
from jax.experimental.pallas import tpu as pltpu
from jax.sharding import PartitionSpec as P

PRODUCTS = 4
BLOCK = 16
CHUNK = 8
F32 = jnp.float32
BF16 = jnp.bfloat16
I32 = jnp.int32
NN = (((1,), (0,)), ((), ()))
NT = (((1,), (1,)), ((), ()))
VM = pl.BlockSpec(memory_space=pltpu.VMEM)
SM = pl.BlockSpec(memory_space=pltpu.SMEM)
HB = pl.BlockSpec(memory_space=pltpu.HBM)


def in_vmem(array):
    return pltpu.with_memory_space_constraint(array, pltpu.VMEM)


def in_hbm(array):
    return pltpu.with_memory_space_constraint(array, pltpu.HBM)


def cost(flops, moved):
    return pl.CostEstimate(flops=flops, bytes_accessed=moved, transcendentals=0)


def params(mib):
    return pltpu.CompilerParams(vmem_limit_bytes=mib * 2**20)


def ranks(named):
    rows = named.shape[0]
    h = lax.broadcasted_iota(I32, (rows, rows), 0)
    other = lax.broadcasted_iota(I32, (rows, rows), 1)
    before = jnp.where(other < h, 1.0, 0.0).astype(BF16)
    ones = jnp.ones((rows, rows), BF16)
    total = lax.dot_general(named.astype(BF16), ones, NN, preferred_element_type=F32)
    mark = jnp.where(total > 0.5, 1.0, 0.0)
    rank = lax.dot_general(before, mark.astype(BF16), NN, preferred_element_type=F32)
    return mark, rank


def draft_plan(first, parity, columns, draft, wanted):
    slots, rows = columns.shape
    low = jnp.where(parity == 0, 2 * rows, rows)
    high = jnp.where(parity == 0, rows, 2 * rows)
    offset = columns - first
    spot = jnp.where(
        offset < 0,
        offset + (rows + low),
        jnp.where(offset >= rows, offset + (high - rows), offset),
    )
    h = lax.broadcasted_iota(I32, (rows, rows), 0)
    lane = lax.broadcasted_iota(I32, (rows, rows), 1)
    equal = [
        jnp.where(spot[s : s + 1] - 2 * rows == h, 1.0, 0.0) for s in range(slots)
    ]
    named = functools.reduce(jnp.add, equal)
    mark, rank = ranks(named)
    draft[0:slots, 0:rows] = spot
    for s in range(slots):
        place = jnp.sum(equal[s] * rank, axis=0, keepdims=True).astype(I32)
        line = spot[s : s + 1]
        draft[slots + s : slots + s + 1, 0:rows] = jnp.where(
            line >= 2 * rows, 2 * rows + place, line
        )
    far = jnp.where(jnp.sum(named, axis=0, keepdims=True) > 0.5, 1.0, 0.0)
    far = jnp.broadcast_to(far, (16, rows))
    before = jnp.where(h < lane, 1.0, 0.0).astype(BF16)
    far_before = lax.dot_general(far.astype(BF16), before, NN, preferred_element_type=F32)
    line = lax.broadcasted_iota(I32, (16, rows), 1).astype(F32)
    position = jnp.where(far > 0.5, rows - 1 - far_before, line - far_before)
    taken = jnp.where(position[0:1].astype(I32) == h, 1.0, 0.0).astype(BF16)
    order = lax.dot_general(line.astype(BF16), taken, NT, preferred_element_type=F32)
    ones = jnp.ones((rows, rows), BF16)
    near = lax.dot_general((1.0 - far).astype(BF16), ones, NN, preferred_element_type=F32)
    base = 2 * slots
    draft[base : base + 1, 0:rows] = order[0:1].astype(I32)
    draft[base + 1 : base + 2, 0:rows] = near[0:1].astype(I32)
    read = jnp.sum(mark, axis=0, keepdims=True).astype(I32)
    draft[base + 2 : base + 3, 0:rows] = read
    here = jnp.where((mark > 0.5) & (rank.astype(I32) == lane), h, 0)
    wanted[0:1, 0:rows] = jnp.sum(here.astype(F32), axis=0, keepdims=True).astype(I32)
    wanted[1:2, 0:rows] = read


def prep_kernel(
    where, columns, tiles, turned, inverse, plan, wanted,
    landing, named, draft, arrived, here, done,
):
    rows, slots, size, _ = tiles.shape
    chunks = rows // CHUNK
    ones = jnp.ones((16, slots * size), BF16)

    def part(i):
        return pl.ds(i * CHUNK, CHUNK)

    def copy_in(i):
        return pltpu.make_async_copy(tiles.at[part(i)], landing.at[part(i)], arrived.at[i])

    copy_columns = pltpu.make_async_copy(columns, named, here)
    copy_columns.start()
    for i in range(chunks):
        copy_in(i).start()
    copy_columns.wait()
    draft_plan(where[0], where[1], named[...], draft, wanted)
    copy_plan = pltpu.make_async_copy(draft, plan, done)
    copy_plan.start()

    def step(i, carry):
        copy_in(i).wait()
        for u in range(CHUNK):
            r = i * CHUNK + u
            for s in range(slots):
                turned[r, pl.ds(s * size, size), :] = landing[r, s].T
            total = lax.dot_general(ones, turned[r], NN, preferred_element_type=F32)
            inverse[pl.ds(r, 1), :] = 1.0 / total[0:1]
        return carry

    lax.fori_loop(0, chunks, step, 0)
    copy_plan.wait()


def prep(where, columns, tiles):
    rows, slots, size, _ = tiles.shape
    height = (2 * slots + 3 + 7) // 8 * 8
    return pl.pallas_call(
        prep_kernel,
        out_shape=(
            pltpu.VMEM((rows, slots * size, size), BF16),
            pltpu.VMEM((rows, size), F32),
            pltpu.SMEM((height, 128), I32),
            pltpu.VMEM((8, 128), I32),
        ),
        in_specs=[SM, HB, HB],
        out_specs=(VM, VM, SM, VM),
        scratch_shapes=[
            pltpu.VMEM(tiles.shape, BF16),
            pltpu.VMEM(columns.shape, I32),
            pltpu.VMEM((height, 128), I32),
            pltpu.SemaphoreType.DMA((rows // CHUNK,)),
            pltpu.SemaphoreType.DMA,
            pltpu.SemaphoreType.DMA,
        ],
        compiler_params=params(14),
        cost_estimate=cost(2 * tiles.size * 16, 4 * tiles.size),
        name="prep",
    )(where, in_hbm(columns), in_hbm(tiles))


def fill(window, start, panel, tile_major):
    size = window.shape[2]
    if tile_major:
        window[start : start + panel.shape[0]] = panel[...]
    else:
        for t in range(panel.shape[1] // size):
            window[start + t] = panel[:, t * size : (t + 1) * size]


def row_block(start, base, plan, turned, inverse, window):
    slots = turned.shape[1] // turned.shape[2]
    picked = [plan[2 * slots, start + u] for u in range(BLOCK)]
    vectors = [
        jnp.concatenate([window[plan[base + s, r]] for s in range(slots)], axis=1)
        for r in picked
    ]
    sums = [
        lax.dot_general(x, turned[r], NN, preferred_element_type=F32)
        for x, r in zip(vectors, picked)
    ]
    return picked, [y * inverse[pl.ds(r, 1), :] for r, y in zip(picked, sums)]


def thirds(x):
    high = x.astype(BF16)
    rest = x - high.astype(F32)
    middle = rest.astype(BF16)
    low = (rest - middle.astype(F32)).astype(BF16)
    return high, middle, low


def fold(squares, vectors):
    total = None
    for a, b in ((2, 2), (1, 2), (2, 1), (0, 2), (2, 0), (1, 1), (0, 1), (1, 0), (0, 0)):
        part = squares[a * vectors : (a + 1) * vectors, b * vectors : (b + 1) * vectors]
        total = part if total is None else total + part
    return total


def run_rows(near_side, base, plan, turned, inverse, window, image, squares):
    rows = turned.shape[0]
    slots = turned.shape[1] // turned.shape[2]
    near = plan[2 * slots + 1, 0]
    count = near if near_side else rows - near

    def step(block, total):
        start = block * BLOCK if near_side else rows - (block + 1) * BLOCK
        picked, results = row_block(start, base, plan, turned, inverse, window)
        if squares is None:
            for r, y in zip(picked, results):
                image[r] = y.astype(BF16)
            return total
        counted = []
        for u, (r, y) in enumerate(zip(picked, results)):
            stacked = jnp.concatenate(thirds(y), axis=0)
            image[r] = stacked
            mine = start + u < near if near_side else start + u >= near
            counted.append(jnp.where(mine, stacked, jnp.zeros_like(stacked)))
        wide = jnp.concatenate(counted, axis=1)
        return total + lax.dot_general(wide, wide, NT, preferred_element_type=F32)

    begin = jnp.int32(0) if squares is None else squares
    return lax.fori_loop(0, (count + BLOCK - 1) // BLOCK, step, begin)


def near_kernel(tile_major, last, plan, turned, inverse, own, mate, window, image, *gram):
    rows, depth, size = turned.shape
    fill(window, 0, own, tile_major)
    fill(window, rows, mate, tile_major)
    zero = jnp.zeros(gram[0].shape, F32) if last else None
    total = run_rows(True, 0, plan, turned, inverse, window, image, zero)
    if last:
        gram[0][...] = total


def far_first_kernel(
    limit, asked, plan, turned, inverse, other, w_in, i_in,
    window, image, send, rest, sending, more, done,
):
    rows, depth, size = turned.shape
    copy = pltpu.make_async_copy(asked, sending, done)
    copy.start()
    fill(window, 2 * rows, other, False)
    run_rows(False, 0, plan, turned, inverse, window, image, None)
    copy.wait()
    read = plan[2 * (depth // size) + 2, 0]
    more[0] = jnp.where(jnp.maximum(sending[1, 0], read) > limit, 1, 0)
    pack(image, sending, send, rest)


def pack(image, sending, send, rest):
    limit = send.shape[0]
    for k in range(image.shape[0]):
        target = send.at[k] if k < limit else rest.at[k - limit]
        target[...] = image[sending[0, k]]


def far_kernel(plan, turned, inverse, sending, other, extra, w_in, i_in, window, image, send, rest):
    rows, depth, size = turned.shape
    limit = other.shape[0]
    fill(window, 2 * rows, other, True)
    fill(window, 2 * rows + limit, extra, True)
    run_rows(False, depth // size, plan, turned, inverse, window, image, None)
    pack(image, sending, send, rest)


def far_last_kernel(plan, turned, inverse, other, extra, near, w_in, i_in, window, image, gram):
    rows, depth, size = turned.shape
    limit = other.shape[0]
    fill(window, 2 * rows, other, True)
    fill(window, 2 * rows + limit, extra, True)
    total = run_rows(
        False, depth // size, plan, turned, inverse, window, image, near[...]
    )
    gram[...] = fold(total, gram.shape[0])


def near_rows(plan, turned, inverse, own, mate, tile_major, last):
    rows, depth, size = turned.shape
    vectors = own.shape[1 if tile_major else 0]
    height = 3 * vectors if last else vectors
    shapes = (
        pltpu.VMEM((3 * rows, vectors, size), BF16),
        pltpu.VMEM((rows, height, size), BF16),
    )
    if last:
        shapes += (pltpu.VMEM((height, height), F32),)
    return pl.pallas_call(
        functools.partial(near_kernel, tile_major, last),
        out_shape=shapes,
        in_specs=[SM, VM, VM, VM, VM],
        out_specs=(VM,) * len(shapes),
        compiler_params=params(4),
        cost_estimate=cost(rows * depth * size * vectors, 2 * rows * depth * size),
        name="near_rows",
    )(plan, *map(in_vmem, (turned, inverse, own, mate)))


def far_call(kernel, ins, in_specs, alias, outs, out_specs, turned, scratch=()):
    rows, depth, size = turned.shape
    return pl.pallas_call(
        kernel,
        out_shape=outs,
        in_specs=in_specs,
        out_specs=out_specs,
        scratch_shapes=scratch,
        input_output_aliases={alias: 0, alias + 1: 1},
        compiler_params=params(4),
        cost_estimate=cost(32 * rows * depth * size, 2 * rows * depth * size),
        name="far_rows",
    )(*ins)


def of(array):
    return pltpu.VMEM(array.shape, array.dtype)


def far_rows_first(limit, asked, plan, turned, inverse, other, window, image):
    rows, vectors, size = image.shape
    return far_call(
        functools.partial(far_first_kernel, limit),
        (in_vmem(asked), plan, *map(in_vmem, (turned, inverse, other, window, image))),
        [VM, SM] + [VM] * 5,
        5,
        (
            of(window),
            of(image),
            pltpu.VMEM((limit, vectors, size), BF16),
            pltpu.VMEM((rows - limit, vectors, size), BF16),
            pltpu.SMEM((8, 128), I32),
            jax.ShapeDtypeStruct((1,), I32),
        ),
        (VM, VM, VM, VM, SM, SM),
        turned,
        [pltpu.SemaphoreType.DMA],
    )[1:]


def far_rows(plan, turned, inverse, sending, other, extra, window, image):
    return far_call(
        far_kernel,
        (
            plan,
            in_vmem(turned),
            in_vmem(inverse),
            sending,
            *map(in_vmem, (other, extra, window, image)),
        ),
        [SM, VM, VM, SM] + [VM] * 4,
        6,
        (of(window), of(image), of(other), of(extra)),
        (VM,) * 4,
        turned,
    )[1:]


def far_rows_last(plan, turned, inverse, other, extra, near, window, image):
    vectors = near.shape[0] // 3
    return far_call(
        far_last_kernel,
        (plan, *map(in_vmem, (turned, inverse, other, extra, near, window, image))),
        [SM] + [VM] * 7,
        6,
        (of(window), of(image), pltpu.VMEM((vectors, vectors), F32)),
        (VM,) * 3,
        turned,
    )[1:]


def inverse_factor(gram):
    count = gram.shape[0]
    step = 8
    row = lax.broadcasted_iota(I32, (count, count), 0)
    column = lax.broadcasted_iota(I32, (count, count), 1)
    work = jnp.concatenate([gram, jnp.where(row == column, 1.0, 0.0)], axis=1)
    below = lax.broadcasted_iota(I32, work.shape, 0)
    for begin in range(0, count, step):
        spread = [
            jnp.broadcast_to(work[:, k : k + 1], work.shape)
            for k in range(begin, begin + step)
        ]
        for j in range(step):
            k = begin + j
            factor = jnp.where(below > k, spread[j], 0.0)
            pivot = 1.0 / spread[j][k : k + 1]
            for q in range(j + 1, step):
                spread[q] = spread[q] - factor * (spread[q][k : k + 1] * pivot)
            work = work - factor * (work[k : k + 1] * pivot)
    pivots = jnp.sum(
        jnp.where(row == column, work[:, :count], 0.0), axis=1, keepdims=True
    )
    return work[:, count:] * lax.rsqrt(pivots)


def final_kernel(states, gram_a, gram_b, mapping, parts, out, ready, sent):
    rows, depth, size = parts.shape
    vectors = depth // 3
    factor = inverse_factor((gram_a[...] + gram_b[...]) / states)
    combined = lax.dot_general(
        mapping[...],
        factor,
        (((0,), (0,)), ((), ())),
        precision=lax.Precision.HIGHEST,
        preferred_element_type=F32,
    )
    high, middle, low = thirds(combined)
    blank = jnp.zeros_like(high)
    left = jnp.concatenate(
        [
            jnp.concatenate([high, high, high], axis=1),
            jnp.concatenate([middle, middle, blank], axis=1),
            jnp.concatenate([low, blank, blank], axis=1),
        ],
        axis=0,
    )
    copies = []
    for g in range(rows // CHUNK):
        for r in range(g * CHUNK, (g + 1) * CHUNK):
            y = lax.dot_general(left, parts[r], NN, preferred_element_type=F32)
            ready[:, r * size : (r + 1) * size] = (
                y[2 * vectors :] + y[vectors : 2 * vectors]
            ) + y[:vectors]
        part = pl.ds(g * CHUNK * size, CHUNK * size)
        copies.append(pltpu.make_async_copy(ready.at[:, part], out.at[:, part], sent.at[g]))
        copies[-1].start()
    for copy in copies:
        copy.wait()


def final(states, gram_a, gram_b, mapping, parts):
    rows, depth, size = parts.shape
    vectors = depth // 3
    return pl.pallas_call(
        functools.partial(final_kernel, float(states)),
        out_shape=jax.ShapeDtypeStruct((vectors, rows * size), F32),
        in_specs=[VM, VM, VM, VM],
        out_specs=HB,
        scratch_shapes=[
            pltpu.VMEM((vectors, rows * size), F32),
            pltpu.SemaphoreType.DMA((rows // CHUNK,)),
        ],
        compiler_params=params(8),
        cost_estimate=cost(6 * parts.size * vectors, 4 * parts.size),
        name="memberships",
    )(gram_a, gram_b, mapping, in_vmem(parts))


def body(transition_tiles, column_tiles, schur_basis, membership_map):
    rows = transition_tiles.shape[0]
    count = lax.axis_size("rows")
    me = lax.axis_index("rows")
    mates = [(i, i ^ 1) for i in range(count)]
    others = []
    for i in range(1, count - 1, 2):
        others += [(i, i + 1), (i + 1, i)]

    def swap(array, pairs):
        return lax.ppermute(array, "rows", pairs)

    limit = 11 * rows // 16
    where = jnp.stack([me * rows, me % 2]).astype(I32)
    columns = column_tiles.T
    mate, other = swap(schur_basis, mates), swap(schur_basis, others)
    turned, inverse, plan, wanted = prep(where, columns, transition_tiles)
    asked = swap(wanted, others)
    window, image = near_rows(plan, turned, inverse, schur_basis, mate, False, False)
    image, send, rest, sending, more = far_rows_first(
        limit, asked, plan, turned, inverse, other, window, image
    )
    for step in range(1, PRODUCTS):
        last = step == PRODUCTS - 1
        mate, other = swap(image, mates), swap(send, others)
        extra = lax.cond(more[0] > 0, lambda x: swap(x, others), lambda x: x, rest)
        window, image, *near = near_rows(plan, turned, inverse, image, mate, True, last)
        if last:
            parts, gram = far_rows_last(
                plan, turned, inverse, other, extra, near[0], window, image
            )
        else:
            image, send, rest = far_rows(
                plan, turned, inverse, sending, other, extra, window, image
            )
    distance = 1
    while distance < count:
        partner = swap(gram, [(i, i ^ distance) for i in range(count)])
        distance *= 2
        if distance < count:
            gram = gram + partner
    states = schur_basis.shape[1] * count
    return final(states, gram, partner, membership_map, parts)


def solution(mesh):
    return jax.shard_map(
        body,
        mesh=mesh,
        in_specs=(
            P(("groups", "rows"), None, None, None),
            P(("groups", "rows"), None),
            P(None, ("groups", "rows")),
            P("groups", None),
        ),
        out_specs=P(None, ("groups", "rows")),
        check_vma=False,
    )
```

```python
import functools

import jax
import jax.numpy as jnp
from jax import lax
from jax.experimental import pallas as pl
from jax.experimental.pallas import tpu as pltpu
from jax.sharding import PartitionSpec as P

PRODUCTS = 4
BLOCK = 16
CHUNK = 8
F32 = jnp.float32
BF16 = jnp.bfloat16
I32 = jnp.int32
NN = (((1,), (0,)), ((), ()))
NT = (((1,), (1,)), ((), ()))
VM = pl.BlockSpec(memory_space=pltpu.VMEM)
SM = pl.BlockSpec(memory_space=pltpu.SMEM)
HB = pl.BlockSpec(memory_space=pltpu.HBM)


def in_vmem(array):
    return pltpu.with_memory_space_constraint(array, pltpu.VMEM)


def in_hbm(array):
    return pltpu.with_memory_space_constraint(array, pltpu.HBM)


def cost(flops, moved):
    return pl.CostEstimate(flops=flops, bytes_accessed=moved, transcendentals=0)


def params(mib):
    return pltpu.CompilerParams(vmem_limit_bytes=mib * 2**20)


def ranks(named):
    rows = named.shape[0]
    h = lax.broadcasted_iota(I32, (rows, rows), 0)
    other = lax.broadcasted_iota(I32, (rows, rows), 1)
    before = jnp.where(other < h, 1.0, 0.0).astype(BF16)
    ones = jnp.ones((rows, rows), BF16)
    total = lax.dot_general(named.astype(BF16), ones, NN, preferred_element_type=F32)
    mark = jnp.where(total > 0.5, 1.0, 0.0)
    rank = lax.dot_general(before, mark.astype(BF16), NN, preferred_element_type=F32)
    return mark, rank


def lines(slots):
    far = slots - 1
    return slots, slots + far, slots + 2 * far, slots + 3 * far, slots + 3 * far + 1


def plan_height(slots):
    return (lines(slots)[-1] + 2 + 7) // 8 * 8


def draft_plan(first, parity, columns, draft, wanted):
    slots, rows = columns.shape
    panel, counted, slot, order, reads = lines(slots)
    low = jnp.where(parity == 0, 2 * rows, rows)
    high = jnp.where(parity == 0, rows, 2 * rows)
    offset = columns - first
    spot = jnp.where(
        offset < 0,
        offset + (rows + low),
        jnp.where(offset >= rows, offset + (high - rows), offset),
    )
    draft[0:slots, 0:rows] = jnp.minimum(spot, 2 * rows)
    h = lax.broadcasted_iota(I32, (rows, rows), 0)
    lane = lax.broadcasted_iota(I32, (rows, rows), 1)
    ones = jnp.ones((rows, rows), BF16)
    equal = [
        jnp.where(spot[s : s + 1] - 2 * rows == h, 1.0, 0.0) for s in range(slots)
    ]
    mark, rank = ranks(functools.reduce(jnp.add, equal))
    here = jnp.where((mark > 0.5) & (rank.astype(I32) == lane), h, 0)
    wanted[0:1, 0:rows] = jnp.sum(here.astype(F32), axis=0, keepdims=True).astype(I32)
    wanted[1:2, 0:rows] = jnp.sum(mark, axis=0, keepdims=True).astype(I32)
    none = jnp.zeros((1, rows), I32)
    seen = none
    tiles, places, named = [[none + start] * (slots - 1) for start in (rows, rows, 0)]
    for s in range(slots):
        place = jnp.sum(equal[s] * rank, axis=0, keepdims=True).astype(I32)
        tile = spot[s : s + 1] - 2 * rows
        far = jnp.where(tile >= 0, 1, 0)
        for j in range(min(s + 1, slots - 1)):
            hit = (far == 1) & (seen == j)
            tiles[j] = jnp.where(hit, tile, tiles[j])
            places[j] = jnp.where(hit, place, places[j])
            named[j] = jnp.where(hit, s, named[j])
        seen = seen + far
    for j in range(slots - 1):
        draft[panel + j : panel + j + 1, 0:rows] = tiles[j]
        draft[counted + j : counted + j + 1, 0:rows] = places[j]
        draft[slot + j : slot + j + 1, 0:rows] = named[j]
    along = jnp.broadcast_to(seen.astype(F32), (rows, rows))
    down = lax.dot_general(
        jnp.where(h == lane, along, 0.0).astype(BF16), ones, NN, preferred_element_type=F32
    )
    ahead = jnp.where((down < along) | ((down == along) & (h < lane)), 1.0, 0.0)
    position = jnp.sum(ahead, axis=0, keepdims=True).astype(I32)
    taken = jnp.where(position == h, 1.0, 0.0).astype(BF16)
    line = lax.broadcasted_iota(I32, (16, rows), 1).astype(BF16)
    sorted_rows = lax.dot_general(line, taken, NT, preferred_element_type=F32)
    draft[order : order + 1, 0:rows] = sorted_rows[0:1].astype(I32)
    draft[reads : reads + 1, 0:rows] = seen
    touched = jnp.sum(jnp.minimum(seen, 1).astype(F32), axis=1, keepdims=True)
    draft[reads + 1 : reads + 2, 0:rows] = jnp.broadcast_to(touched, (1, rows)).astype(I32)


def prep_kernel(
    where, columns, tiles, turned, inverse, plan, wanted,
    landing, named, draft, arrived, here, done,
):
    rows, slots, size, _ = tiles.shape
    chunks = rows // CHUNK

    def copy_in(i):
        part = pl.ds(i * CHUNK, CHUNK)
        return pltpu.make_async_copy(tiles.at[part], landing.at[part], arrived.at[i])

    copy_columns = pltpu.make_async_copy(columns, named, here)
    copy_columns.start()
    for i in range(chunks):
        copy_in(i).start()
    copy_columns.wait()
    draft_plan(where[0], where[1], named[...], draft, wanted)
    copy_plan = pltpu.make_async_copy(draft, plan, done)
    copy_plan.start()

    def step(i, carry):
        copy_in(i).wait()
        for u in range(CHUNK):
            r = i * CHUNK + u
            total = None
            for s in range(slots):
                tile = landing[r, s].T
                turned[r, pl.ds(s * size, size), :] = tile
                tile = tile.astype(F32)
                total = tile if total is None else total + tile
            inverse[pl.ds(r, 1), :] = 1.0 / jnp.sum(total, axis=0, keepdims=True)
        return carry

    lax.fori_loop(0, chunks, step, 0)
    copy_plan.wait()


def prep(where, columns, tiles):
    rows, slots, size, _ = tiles.shape
    height = plan_height(slots)
    return pl.pallas_call(
        prep_kernel,
        out_shape=(
            pltpu.VMEM((rows, slots * size, size), BF16),
            pltpu.VMEM((rows, size), F32),
            pltpu.SMEM((height, 128), I32),
            pltpu.VMEM((8, 128), I32),
        ),
        in_specs=[SM, HB, HB],
        out_specs=(VM, VM, SM, VM),
        scratch_shapes=[
            pltpu.VMEM(tiles.shape, BF16),
            pltpu.VMEM(columns.shape, I32),
            pltpu.VMEM((height, 128), I32),
            pltpu.SemaphoreType.DMA((rows // CHUNK,)),
            pltpu.SemaphoreType.DMA,
            pltpu.SemaphoreType.DMA,
        ],
        compiler_params=params(14),
        cost_estimate=cost(2 * tiles.size * 16, 4 * tiles.size),
        name="prep",
    )(where, in_hbm(columns), in_hbm(tiles))


def fill(window, start, panel, tile_major):
    size = window.shape[2]
    if tile_major:
        window[start : start + panel.shape[0]] = panel[...]
    else:
        for t in range(panel.shape[1] // size):
            window[start + t] = panel[:, t * size : (t + 1) * size]


def thirds(x):
    high = x.astype(BF16)
    rest = x - high.astype(F32)
    middle = rest.astype(BF16)
    low = (rest - middle.astype(F32)).astype(BF16)
    return high, middle, low


def fold(squares, vectors):
    total = None
    for a, b in ((2, 2), (1, 2), (2, 1), (0, 2), (2, 0), (1, 1), (0, 1), (1, 0), (0, 0)):
        part = squares[a * vectors : (a + 1) * vectors, b * vectors : (b + 1) * vectors]
        total = part if total is None else total + part
    return total


def store(image, squares, picked, results, mine):
    if squares is None:
        for r, y in zip(picked, results):
            image[r] = y.astype(BF16)
        return None
    counted = []
    for r, y, keep in zip(picked, results, mine):
        stacked = jnp.concatenate(thirds(y), axis=0)
        image[r] = stacked
        counted.append(jnp.where(keep, stacked, jnp.zeros_like(stacked)))
    wide = jnp.concatenate(counted, axis=1)
    return squares + lax.dot_general(wide, wide, NT, preferred_element_type=F32)


def near_kernel(tile_major, last, plan, turned, inverse, own, mate, image, sums, *refs):
    rows, depth, size = turned.shape
    slots = depth // size
    reads = lines(slots)[-1]
    window = refs[-1]
    fill(window, 0, own, tile_major)
    fill(window, rows, mate, tile_major)
    window[2 * rows] = jnp.zeros(window.shape[1:], BF16)

    def step(block, squares):
        picked = [block * BLOCK + u for u in range(BLOCK)]
        vectors = [
            jnp.concatenate([window[plan[s, r]] for s in range(slots)], axis=1)
            for r in picked
        ]
        products = [
            lax.dot_general(x, turned[r], NN, preferred_element_type=F32)
            for x, r in zip(vectors, picked)
        ]
        results = [y * inverse[pl.ds(r, 1), :] for r, y in zip(picked, products)]
        for r, y in zip(picked, results):
            sums[r] = y
        mine = [plan[reads, r] == 0 for r in picked]
        return store(image, squares, picked, results, mine)

    begin = jnp.zeros(refs[0].shape, F32) if last else None
    total = lax.fori_loop(0, rows // BLOCK, step, begin)
    if last:
        refs[0][...] = total


def far_part(base, plan, turned, inverse, sums, panel, image, squares):
    rows, depth, size = turned.shape
    slots = depth // size
    slot, order, reads = lines(slots)[2:]
    panel[rows] = jnp.zeros(panel.shape[1:], BF16)

    def rows_of(start, count):
        picked = [plan[order, start + u] for u in range(BLOCK)]
        products = []
        for r in picked:
            x = [panel[plan[base + j, r]] for j in range(count)]
            w = [
                turned[r, pl.ds(pl.multiple_of(plan[slot + j, r] * size, size), size), :]
                for j in range(count)
            ]
            products.append(
                lax.dot_general(
                    jnp.concatenate(x, axis=1),
                    jnp.concatenate(w, axis=0),
                    NN,
                    preferred_element_type=F32,
                )
            )
        return picked, [
            sums[r] + y * inverse[pl.ds(r, 1), :] for r, y in zip(picked, products)
        ]

    def step(block, carry):
        start = rows - (block + 1) * BLOCK
        most = plan[reads, plan[order, start + BLOCK - 1]]
        for count in range(1, slots):

            @pl.when(most == count)
            def _():
                picked, results = rows_of(start, count)
                mine = [plan[reads, r] > 0 for r in picked]
                if squares is None:
                    store(image, None, picked, results, mine)
                else:
                    squares[...] = store(image, squares[...], picked, results, mine)

        return carry

    touched = plan[reads + 1, 0]
    lax.fori_loop(0, (touched + BLOCK - 1) // BLOCK, step, 0)


def pack(image, sending, send, rest):
    limit = send.shape[0]
    for k in range(image.shape[0]):
        target = send.at[k] if k < limit else rest.at[k - limit]
        target[...] = image[sending[0, k]]


def far_first_kernel(
    asked, plan, turned, inverse, other, sums, i_in, image, send, rest, sending, panel, done
):
    rows, depth, size = turned.shape
    copy = pltpu.make_async_copy(asked, sending, done)
    copy.start()
    fill(panel, 0, other, False)
    base = lines(depth // size)[0]
    far_part(base, plan, turned, inverse, sums, panel, image, None)
    copy.wait()
    pack(image, sending, send, rest)


def far_kernel(
    sending, plan, turned, inverse, other, extra, sums, i_in, image, send, rest, panel
):
    rows, depth, size = turned.shape
    fill(panel, 0, other, True)
    fill(panel, other.shape[0], extra, True)
    base = lines(depth // size)[1]
    far_part(base, plan, turned, inverse, sums, panel, image, None)
    pack(image, sending, send, rest)


def far_last_kernel(
    plan, turned, inverse, other, extra, near, sums, i_in, image, gram, panel, squares
):
    rows, depth, size = turned.shape
    fill(panel, 0, other, True)
    fill(panel, other.shape[0], extra, True)
    squares[...] = near[...]
    base = lines(depth // size)[1]
    far_part(base, plan, turned, inverse, sums, panel, image, squares)
    gram[...] = fold(squares[...], gram.shape[0])


def near_rows(plan, turned, inverse, own, mate, tile_major, last):
    rows, depth, size = turned.shape
    vectors = own.shape[1 if tile_major else 0]
    height = 3 * vectors if last else vectors
    shapes = (
        pltpu.VMEM((rows, height, size), BF16),
        pltpu.VMEM((rows, vectors, size), F32),
    )
    if last:
        shapes += (pltpu.VMEM((height, height), F32),)
    return pl.pallas_call(
        functools.partial(near_kernel, tile_major, last),
        out_shape=shapes,
        in_specs=[SM, VM, VM, VM, VM],
        out_specs=(VM,) * len(shapes),
        scratch_shapes=[pltpu.VMEM((2 * rows + 1, vectors, size), BF16)],
        compiler_params=params(4),
        cost_estimate=cost(2 * rows * depth * size * vectors, 2 * rows * depth * size),
        name="near_rows",
    )(plan, *map(in_vmem, (turned, inverse, own, mate)))


def far_call(kernel, ins, in_specs, outs, out_specs, turned, vectors, scratch=()):
    rows, depth, size = turned.shape
    return pl.pallas_call(
        kernel,
        out_shape=outs,
        in_specs=in_specs,
        out_specs=out_specs,
        scratch_shapes=[pltpu.VMEM((rows + 1, vectors, size), BF16), *scratch],
        input_output_aliases={len(ins) - 1: 0},
        compiler_params=params(4),
        cost_estimate=cost(20 * rows * depth * size, rows * depth * size),
        name="far_rows",
    )(*ins)


def of(array):
    return pltpu.VMEM(array.shape, array.dtype)


def far_rows_first(limit, asked, plan, turned, inverse, other, sums, image):
    rows, vectors, size = image.shape
    return far_call(
        far_first_kernel,
        (in_vmem(asked), plan, *map(in_vmem, (turned, inverse, other, sums, image))),
        [VM, SM] + [VM] * 5,
        (
            of(image),
            pltpu.VMEM((limit, vectors, size), BF16),
            pltpu.VMEM((rows - limit, vectors, size), BF16),
            pltpu.SMEM((8, 128), I32),
        ),
        (VM, VM, VM, SM),
        turned,
        vectors,
        [pltpu.SemaphoreType.DMA],
    )


def far_rows(plan, turned, inverse, sending, other, extra, sums, image):
    return far_call(
        far_kernel,
        (sending, plan, *map(in_vmem, (turned, inverse, other, extra, sums, image))),
        [SM, SM] + [VM] * 6,
        (of(image), of(other), of(extra)),
        (VM,) * 3,
        turned,
        image.shape[1],
    )


def far_rows_last(plan, turned, inverse, other, extra, near, sums, image):
    vectors = near.shape[0] // 3
    return far_call(
        far_last_kernel,
        (plan, *map(in_vmem, (turned, inverse, other, extra, near, sums, image))),
        [SM] + [VM] * 7,
        (of(image), pltpu.VMEM((vectors, vectors), F32)),
        (VM,) * 2,
        turned,
        vectors,
        [pltpu.VMEM(near.shape, F32)],
    )


def inverse_factor(gram):
    count = gram.shape[0]
    step = 8
    row = lax.broadcasted_iota(I32, (count, count), 0)
    column = lax.broadcasted_iota(I32, (count, count), 1)
    work = jnp.concatenate([gram, jnp.where(row == column, 1.0, 0.0)], axis=1)
    below = lax.broadcasted_iota(I32, work.shape, 0)
    for begin in range(0, count, step):
        spread = [
            jnp.broadcast_to(work[:, k : k + 1], work.shape)
            for k in range(begin, begin + step)
        ]
        for j in range(step):
            k = begin + j
            factor = jnp.where(below > k, spread[j], 0.0)
            pivot = 1.0 / spread[j][k : k + 1]
            for q in range(j + 1, step):
                spread[q] = spread[q] - factor * (spread[q][k : k + 1] * pivot)
            work = work - factor * (work[k : k + 1] * pivot)
    pivots = jnp.sum(
        jnp.where(row == column, work[:, :count], 0.0), axis=1, keepdims=True
    )
    return work[:, count:] * lax.rsqrt(pivots)


def final_kernel(states, gram_a, gram_b, mapping, parts, out, ready, sent):
    rows, depth, size = parts.shape
    vectors = depth // 3
    factor = inverse_factor((gram_a[...] + gram_b[...]) / states)
    combined = lax.dot_general(
        mapping[...],
        factor,
        (((0,), (0,)), ((), ())),
        precision=lax.Precision.HIGHEST,
        preferred_element_type=F32,
    )
    high, middle, low = thirds(combined)
    blank = jnp.zeros_like(high)
    left = jnp.concatenate(
        [
            jnp.concatenate([high, high, high], axis=1),
            jnp.concatenate([middle, middle, blank], axis=1),
            jnp.concatenate([low, blank, blank], axis=1),
        ],
        axis=0,
    )
    copies = []
    for g in range(rows // CHUNK):
        for r in range(g * CHUNK, (g + 1) * CHUNK):
            y = lax.dot_general(left, parts[r], NN, preferred_element_type=F32)
            ready[:, r * size : (r + 1) * size] = (
                y[2 * vectors :] + y[vectors : 2 * vectors]
            ) + y[:vectors]
        part = pl.ds(g * CHUNK * size, CHUNK * size)
        copies.append(pltpu.make_async_copy(ready.at[:, part], out.at[:, part], sent.at[g]))
        copies[-1].start()
    for copy in copies:
        copy.wait()


def final(states, gram_a, gram_b, mapping, parts):
    rows, depth, size = parts.shape
    vectors = depth // 3
    return pl.pallas_call(
        functools.partial(final_kernel, float(states)),
        out_shape=jax.ShapeDtypeStruct((vectors, rows * size), F32),
        in_specs=[VM, VM, VM, VM],
        out_specs=HB,
        scratch_shapes=[
            pltpu.VMEM((vectors, rows * size), F32),
            pltpu.SemaphoreType.DMA((rows // CHUNK,)),
        ],
        compiler_params=params(8),
        cost_estimate=cost(6 * parts.size * vectors, 4 * parts.size),
        name="memberships",
    )(gram_a, gram_b, mapping, in_vmem(parts))


def body(transition_tiles, column_tiles, schur_basis, membership_map):
    rows = transition_tiles.shape[0]
    count = lax.axis_size("rows")
    me = lax.axis_index("rows")
    mates = [(i, i ^ 1) for i in range(count)]
    others = []
    for i in range(1, count - 1, 2):
        others += [(i, i + 1), (i + 1, i)]

    def swap(array, pairs):
        return lax.ppermute(array, "rows", pairs)

    limit = 11 * rows // 16
    where = jnp.stack([me * rows, me % 2]).astype(I32)
    columns = column_tiles.T
    mate, other = swap(schur_basis, mates), swap(schur_basis, others)
    turned, inverse, plan, wanted = prep(where, columns, transition_tiles)
    asked = swap(wanted, others)
    more = jnp.maximum(wanted[1, 0], asked[1, 0]) > limit
    image, sums = near_rows(plan, turned, inverse, schur_basis, mate, False, False)
    image, send, rest, sending = far_rows_first(
        limit, asked, plan, turned, inverse, other, sums, image
    )
    for step in range(1, PRODUCTS):
        last = step == PRODUCTS - 1
        mate, other = swap(image, mates), swap(send, others)
        extra = lax.cond(more, lambda x: swap(x, others), lambda x: x, rest)
        image, sums, *near = near_rows(plan, turned, inverse, image, mate, True, last)
        if last:
            parts, gram = far_rows_last(
                plan, turned, inverse, other, extra, near[0], sums, image
            )
        else:
            image, send, rest = far_rows(
                plan, turned, inverse, sending, other, extra, sums, image
            )
    distance = 1
    while distance < count:
        partner = swap(gram, [(i, i ^ distance) for i in range(count)])
        distance *= 2
        if distance < count:
            gram = gram + partner
    states = schur_basis.shape[1] * count
    return final(states, gram, partner, membership_map, parts)


def solution(mesh):
    return jax.shard_map(
        body,
        mesh=mesh,
        in_specs=(
            P(("groups", "rows"), None, None, None),
            P(("groups", "rows"), None),
            P(None, ("groups", "rows")),
            P("groups", None),
        ),
        out_specs=P(None, ("groups", "rows")),
        check_vma=False,
    )
```

```python
import functools

import jax
import jax.numpy as jnp
from jax import lax
from jax.experimental import pallas as pl
from jax.experimental.pallas import tpu as pltpu
from jax.sharding import PartitionSpec as P

PRODUCTS = 4
BLOCK = 16
CHUNK = 8
F32 = jnp.float32
BF16 = jnp.bfloat16
I32 = jnp.int32
NN = (((1,), (0,)), ((), ()))
NT = (((1,), (1,)), ((), ()))
VM = pl.BlockSpec(memory_space=pltpu.VMEM)
SM = pl.BlockSpec(memory_space=pltpu.SMEM)
HB = pl.BlockSpec(memory_space=pltpu.HBM)


def in_vmem(array):
    return pltpu.with_memory_space_constraint(array, pltpu.VMEM)


def in_hbm(array):
    return pltpu.with_memory_space_constraint(array, pltpu.HBM)


def cost(flops, moved):
    return pl.CostEstimate(flops=flops, bytes_accessed=moved, transcendentals=0)


def params(mib):
    return pltpu.CompilerParams(vmem_limit_bytes=mib * 2**20)


def ranks(named):
    rows = named.shape[0]
    h = lax.broadcasted_iota(I32, (rows, rows), 0)
    other = lax.broadcasted_iota(I32, (rows, rows), 1)
    before = jnp.where(other < h, 1.0, 0.0).astype(BF16)
    ones = jnp.ones((rows, rows), BF16)
    total = lax.dot_general(named.astype(BF16), ones, NN, preferred_element_type=F32)
    mark = jnp.where(total > 0.5, 1.0, 0.0)
    rank = lax.dot_general(before, mark.astype(BF16), NN, preferred_element_type=F32)
    return mark, rank


def lines(slots):
    far = slots - 1
    return slots, slots + far, slots + 2 * far, slots + 3 * far, slots + 3 * far + 1


def plan_height(slots):
    return (lines(slots)[-1] + 3 + 7) // 8 * 8


def draft_plan(first, parity, columns, draft, wanted):
    slots, rows = columns.shape
    panel, counted, slot, order, reads = lines(slots)
    low = jnp.where(parity == 0, 2 * rows, rows)
    high = jnp.where(parity == 0, rows, 2 * rows)
    offset = columns - first
    spot = jnp.where(
        offset < 0,
        offset + (rows + low),
        jnp.where(offset >= rows, offset + (high - rows), offset),
    )
    draft[0:slots, 0:rows] = jnp.minimum(spot, 2 * rows)
    h = lax.broadcasted_iota(I32, (rows, rows), 0)
    lane = lax.broadcasted_iota(I32, (rows, rows), 1)
    ones = jnp.ones((rows, rows), BF16)
    equal = [
        jnp.where(spot[s : s + 1] - 2 * rows == h, 1.0, 0.0) for s in range(slots)
    ]
    mark, rank = ranks(functools.reduce(jnp.add, equal))
    here = jnp.where((mark > 0.5) & (rank.astype(I32) == lane), h, 0)
    wanted[0:1, 0:rows] = jnp.sum(here.astype(F32), axis=0, keepdims=True).astype(I32)
    read = jnp.sum(mark, axis=0, keepdims=True).astype(I32)
    wanted[1:2, 0:rows] = read
    draft[reads + 2 : reads + 3, 0:rows] = read
    none = jnp.zeros((1, rows), I32)
    seen = none
    tiles, places, named = [[none + start] * (slots - 1) for start in (rows, rows, 0)]
    for s in range(slots):
        place = jnp.sum(equal[s] * rank, axis=0, keepdims=True).astype(I32)
        tile = spot[s : s + 1] - 2 * rows
        far = jnp.where(tile >= 0, 1, 0)
        for j in range(min(s + 1, slots - 1)):
            hit = (far == 1) & (seen == j)
            tiles[j] = jnp.where(hit, tile, tiles[j])
            places[j] = jnp.where(hit, place, places[j])
            named[j] = jnp.where(hit, s, named[j])
        seen = seen + far
    for j in range(slots - 1):
        draft[panel + j : panel + j + 1, 0:rows] = tiles[j]
        draft[counted + j : counted + j + 1, 0:rows] = places[j]
        draft[slot + j : slot + j + 1, 0:rows] = named[j]
    along = jnp.broadcast_to(seen.astype(F32), (rows, rows))
    down = lax.dot_general(
        jnp.where(h == lane, along, 0.0).astype(BF16), ones, NN, preferred_element_type=F32
    )
    ahead = jnp.where((down < along) | ((down == along) & (h < lane)), 1.0, 0.0)
    position = jnp.sum(ahead, axis=0, keepdims=True).astype(I32)
    taken = jnp.where(position == h, 1.0, 0.0).astype(BF16)
    line = lax.broadcasted_iota(I32, (16, rows), 1).astype(BF16)
    sorted_rows = lax.dot_general(line, taken, NT, preferred_element_type=F32)
    draft[order : order + 1, 0:rows] = sorted_rows[0:1].astype(I32)
    draft[reads : reads + 1, 0:rows] = seen
    touched = jnp.sum(jnp.minimum(seen, 1).astype(F32), axis=1, keepdims=True)
    draft[reads + 1 : reads + 2, 0:rows] = jnp.broadcast_to(touched, (1, rows)).astype(I32)


def prep_kernel(
    where, columns, tiles, turned, inverse, plan, wanted,
    landing, named, draft, arrived, here, done,
):
    rows, slots, size, _ = tiles.shape
    chunks = rows // CHUNK

    def copy_in(i):
        part = pl.ds(i * CHUNK, CHUNK)
        return pltpu.make_async_copy(tiles.at[part], landing.at[part], arrived.at[i])

    copy_columns = pltpu.make_async_copy(columns, named, here)
    copy_columns.start()
    for i in range(chunks):
        copy_in(i).start()
    copy_columns.wait()
    draft_plan(where[0], where[1], named[...], draft, wanted)
    copy_plan = pltpu.make_async_copy(draft, plan, done)
    copy_plan.start()

    def step(i, carry):
        copy_in(i).wait()
        for u in range(CHUNK):
            r = i * CHUNK + u
            total = None
            for s in range(slots):
                tile = landing[r, s].T
                turned[r, pl.ds(s * size, size), :] = tile
                tile = tile.astype(F32)
                total = tile if total is None else total + tile
            inverse[pl.ds(r, 1), :] = 1.0 / jnp.sum(total, axis=0, keepdims=True)
        return carry

    lax.fori_loop(0, chunks, step, 0)
    copy_plan.wait()


def prep(where, columns, tiles):
    rows, slots, size, _ = tiles.shape
    height = plan_height(slots)
    return pl.pallas_call(
        prep_kernel,
        out_shape=(
            pltpu.VMEM((rows, slots * size, size), BF16),
            pltpu.VMEM((rows, size), F32),
            pltpu.SMEM((height, 128), I32),
            pltpu.VMEM((8, 128), I32),
        ),
        in_specs=[SM, HB, HB],
        out_specs=(VM, VM, SM, VM),
        scratch_shapes=[
            pltpu.VMEM(tiles.shape, BF16),
            pltpu.VMEM(columns.shape, I32),
            pltpu.VMEM((height, 128), I32),
            pltpu.SemaphoreType.DMA((rows // CHUNK,)),
            pltpu.SemaphoreType.DMA,
            pltpu.SemaphoreType.DMA,
        ],
        compiler_params=params(14),
        cost_estimate=cost(2 * tiles.size * 16, 4 * tiles.size),
        name="prep",
    )(where, in_hbm(columns), in_hbm(tiles))


def fill(window, start, panel, tile_major):
    size = window.shape[2]
    if tile_major:
        window[start : start + panel.shape[0]] = panel[...]
    else:
        for t in range(panel.shape[1] // size):
            window[start + t] = panel[:, t * size : (t + 1) * size]


def thirds(x):
    high = x.astype(BF16)
    rest = x - high.astype(F32)
    middle = rest.astype(BF16)
    low = (rest - middle.astype(F32)).astype(BF16)
    return high, middle, low


def fold(squares, vectors):
    total = None
    for a, b in ((2, 2), (1, 2), (2, 1), (0, 2), (2, 0), (1, 1), (0, 1), (1, 0), (0, 0)):
        part = squares[a * vectors : (a + 1) * vectors, b * vectors : (b + 1) * vectors]
        total = part if total is None else total + part
    return total


def store(image, squares, picked, results, mine):
    if squares is None:
        for r, y in zip(picked, results):
            image[r] = y.astype(BF16)
        return None
    counted = []
    for r, y, keep in zip(picked, results, mine):
        stacked = jnp.concatenate(thirds(y), axis=0)
        image[r] = stacked
        counted.append(jnp.where(keep, stacked, jnp.zeros_like(stacked)))
    wide = jnp.concatenate(counted, axis=1)
    return squares + lax.dot_general(wide, wide, NT, preferred_element_type=F32)


def near_kernel(tile_major, last, plan, turned, inverse, own, mate, image, sums, *refs):
    rows, depth, size = turned.shape
    slots = depth // size
    reads = lines(slots)[-1]
    window = refs[-1]
    fill(window, 0, own, tile_major)
    fill(window, rows, mate, tile_major)
    window[2 * rows] = jnp.zeros(window.shape[1:], BF16)

    def step(block, squares):
        picked = [block * BLOCK + u for u in range(BLOCK)]
        vectors = [
            jnp.concatenate([window[plan[s, r]] for s in range(slots)], axis=1)
            for r in picked
        ]
        products = [
            lax.dot_general(x, turned[r], NN, preferred_element_type=F32)
            for x, r in zip(vectors, picked)
        ]
        results = [y * inverse[pl.ds(r, 1), :] for r, y in zip(picked, products)]
        for r, y in zip(picked, results):
            sums[r] = y
        mine = [plan[reads, r] == 0 for r in picked]
        return store(image, squares, picked, results, mine)

    begin = jnp.zeros(refs[0].shape, F32) if last else None
    total = lax.fori_loop(0, rows // BLOCK, step, begin)
    if last:
        refs[0][...] = total


def far_part(base, plan, turned, inverse, sums, panel, image, squares):
    rows, depth, size = turned.shape
    slots = depth // size
    slot, order, reads = lines(slots)[2:]
    panel[rows] = jnp.zeros(panel.shape[1:], BF16)

    def rows_of(start, count):
        picked = [plan[order, start + u] for u in range(BLOCK)]
        products = []
        for r in picked:
            x = [panel[plan[base + j, r]] for j in range(count)]
            w = [
                turned[r, pl.ds(pl.multiple_of(plan[slot + j, r] * size, size), size), :]
                for j in range(count)
            ]
            products.append(
                lax.dot_general(
                    jnp.concatenate(x, axis=1),
                    jnp.concatenate(w, axis=0),
                    NN,
                    preferred_element_type=F32,
                )
            )
        return picked, [
            sums[r] + y * inverse[pl.ds(r, 1), :] for r, y in zip(picked, products)
        ]

    def step(block, carry):
        start = rows - (block + 1) * BLOCK
        most = plan[reads, plan[order, start + BLOCK - 1]]
        for count in range(1, slots):

            @pl.when(most == count)
            def _():
                picked, results = rows_of(start, count)
                mine = [plan[reads, r] > 0 for r in picked]
                if squares is None:
                    store(image, None, picked, results, mine)
                else:
                    squares[...] = store(image, squares[...], picked, results, mine)

        return carry

    touched = plan[reads + 1, 0]
    lax.fori_loop(0, (touched + BLOCK - 1) // BLOCK, step, 0)


def pack(image, sending, send):
    for k in range(send.shape[0]):
        send[k] = image[sending[0, k]]


def far_first_kernel(
    asked, plan, turned, inverse, other, sums, i_in, image, send, sending, panel, done
):
    rows, depth, size = turned.shape
    copy = pltpu.make_async_copy(asked, sending, done)
    copy.start()
    fill(panel, 0, other, False)
    base = lines(depth // size)[0]
    far_part(base, plan, turned, inverse, sums, panel, image, None)
    copy.wait()
    pack(image, sending, send)


def far_kernel(sending, plan, turned, inverse, other, sums, i_in, image, send, panel):
    rows, depth, size = turned.shape
    fill(panel, 0, other, True)
    base = lines(depth // size)[1]
    far_part(base, plan, turned, inverse, sums, panel, image, None)
    pack(image, sending, send)


def far_whole_kernel(tile_major, plan, turned, inverse, other, sums, i_in, image, panel):
    rows, depth, size = turned.shape
    fill(panel, 0, other, tile_major)
    base = lines(depth // size)[0]
    far_part(base, plan, turned, inverse, sums, panel, image, None)


def far_last_kernel(
    whole, sending, plan, turned, inverse, other, near, sums, i_in, image, gram, panel, squares
):
    rows, depth, size = turned.shape
    slots = depth // size
    vectors = gram.shape[1]
    fill(panel, 0, other, True)
    squares[...] = near[...]
    base = lines(slots)[0 if whole else 1]
    far_part(base, plan, turned, inverse, sums, panel, image, squares)
    gram[0:vectors] = fold(squares[...], vectors)
    read = plan[lines(slots)[-1] + 2, 0]
    short = jnp.maximum(read, sending[1, 0]) > other.shape[0]
    gram[vectors:] = jnp.zeros((8, vectors), F32) + jnp.where(short, 1.0, 0.0)


def near_rows(plan, turned, inverse, own, mate, tile_major, last):
    rows, depth, size = turned.shape
    vectors = own.shape[1 if tile_major else 0]
    height = 3 * vectors if last else vectors
    shapes = (
        pltpu.VMEM((rows, height, size), BF16),
        pltpu.VMEM((rows, vectors, size), F32),
    )
    if last:
        shapes += (pltpu.VMEM((height, height), F32),)
    return pl.pallas_call(
        functools.partial(near_kernel, tile_major, last),
        out_shape=shapes,
        in_specs=[SM, VM, VM, VM, VM],
        out_specs=(VM,) * len(shapes),
        scratch_shapes=[pltpu.VMEM((2 * rows + 1, vectors, size), BF16)],
        compiler_params=params(4),
        cost_estimate=cost(2 * rows * depth * size * vectors, 2 * rows * depth * size),
        name="near_rows",
    )(plan, *map(in_vmem, (turned, inverse, own, mate)))


def far_call(kernel, ins, in_specs, outs, out_specs, turned, vectors, scratch=()):
    rows, depth, size = turned.shape
    return pl.pallas_call(
        kernel,
        out_shape=outs,
        in_specs=in_specs,
        out_specs=out_specs,
        scratch_shapes=[pltpu.VMEM((rows + 1, vectors, size), BF16), *scratch],
        input_output_aliases={len(ins) - 1: 0},
        compiler_params=params(4),
        cost_estimate=cost(20 * rows * depth * size, rows * depth * size),
        name="far_rows",
    )(*ins)


def of(array):
    return pltpu.VMEM(array.shape, array.dtype)


def far_rows_first(limit, asked, plan, turned, inverse, other, sums, image):
    rows, vectors, size = image.shape
    return far_call(
        far_first_kernel,
        (in_vmem(asked), plan, *map(in_vmem, (turned, inverse, other, sums, image))),
        [VM, SM] + [VM] * 5,
        (of(image), pltpu.VMEM((limit, vectors, size), BF16), pltpu.SMEM((8, 128), I32)),
        (VM, VM, SM),
        turned,
        vectors,
        [pltpu.SemaphoreType.DMA],
    )


def far_rows(plan, turned, inverse, sending, other, sums, image):
    return far_call(
        far_kernel,
        (sending, plan, *map(in_vmem, (turned, inverse, other, sums, image))),
        [SM, SM] + [VM] * 5,
        (of(image), of(other)),
        (VM,) * 2,
        turned,
        image.shape[1],
    )


def far_rows_whole(plan, turned, inverse, other, sums, image, tile_major):
    return far_call(
        functools.partial(far_whole_kernel, tile_major),
        (plan, *map(in_vmem, (turned, inverse, other, sums, image))),
        [SM] + [VM] * 5,
        (of(image),),
        (VM,),
        turned,
        image.shape[1],
    )[0]


def far_rows_last(whole, plan, turned, inverse, sending, other, near, sums, image):
    vectors = near.shape[0] // 3
    return far_call(
        functools.partial(far_last_kernel, whole),
        (sending, plan, *map(in_vmem, (turned, inverse, other, near, sums, image))),
        [SM, SM] + [VM] * 6,
        (of(image), pltpu.VMEM((vectors + 8, vectors), F32)),
        (VM,) * 2,
        turned,
        vectors,
        [pltpu.VMEM(near.shape, F32)],
    )


def inverse_factor(gram):
    count = gram.shape[0]
    step = 8
    row = lax.broadcasted_iota(I32, (count, count), 0)
    column = lax.broadcasted_iota(I32, (count, count), 1)
    work = jnp.concatenate([gram, jnp.where(row == column, 1.0, 0.0)], axis=1)
    below = lax.broadcasted_iota(I32, work.shape, 0)
    for begin in range(0, count, step):
        spread = [
            jnp.broadcast_to(work[:, k : k + 1], work.shape)
            for k in range(begin, begin + step)
        ]
        for j in range(step):
            k = begin + j
            factor = jnp.where(below > k, spread[j], 0.0)
            pivot = 1.0 / spread[j][k : k + 1]
            for q in range(j + 1, step):
                spread[q] = spread[q] - factor * (spread[q][k : k + 1] * pivot)
            work = work - factor * (work[k : k + 1] * pivot)
    pivots = jnp.sum(
        jnp.where(row == column, work[:, :count], 0.0), axis=1, keepdims=True
    )
    return work[:, count:] * lax.rsqrt(pivots)


def final_kernel(states, gram_a, gram_b, mapping, parts, out, short, ready, sent):
    rows, depth, size = parts.shape
    vectors = depth // 3
    total = gram_a[...] + gram_b[...]
    short[0] = jnp.max(total[vectors:]).astype(I32)
    factor = inverse_factor(total[:vectors] / states)
    combined = lax.dot_general(
        mapping[...],
        factor,
        (((0,), (0,)), ((), ())),
        precision=lax.Precision.HIGHEST,
        preferred_element_type=F32,
    )
    high, middle, low = thirds(combined)
    blank = jnp.zeros_like(high)
    left = jnp.concatenate(
        [
            jnp.concatenate([high, high, high], axis=1),
            jnp.concatenate([middle, middle, blank], axis=1),
            jnp.concatenate([low, blank, blank], axis=1),
        ],
        axis=0,
    )
    copies = []
    for g in range(rows // CHUNK):
        for r in range(g * CHUNK, (g + 1) * CHUNK):
            y = lax.dot_general(left, parts[r], NN, preferred_element_type=F32)
            ready[:, r * size : (r + 1) * size] = (
                y[2 * vectors :] + y[vectors : 2 * vectors]
            ) + y[:vectors]
        part = pl.ds(g * CHUNK * size, CHUNK * size)
        copies.append(pltpu.make_async_copy(ready.at[:, part], out.at[:, part], sent.at[g]))
        copies[-1].start()
    for copy in copies:
        copy.wait()


def final(states, gram_a, gram_b, mapping, parts):
    rows, depth, size = parts.shape
    vectors = depth // 3
    return pl.pallas_call(
        functools.partial(final_kernel, float(states)),
        out_shape=(
            jax.ShapeDtypeStruct((vectors, rows * size), F32),
            pltpu.SMEM((1,), I32),
        ),
        in_specs=[VM, VM, VM, VM],
        out_specs=(HB, SM),
        scratch_shapes=[
            pltpu.VMEM((vectors, rows * size), F32),
            pltpu.SemaphoreType.DMA((rows // CHUNK,)),
        ],
        compiler_params=params(8),
        cost_estimate=cost(6 * parts.size * vectors, 4 * parts.size),
        name="memberships",
    )(gram_a, gram_b, mapping, in_vmem(parts))


def memberships(whole, transition_tiles, column_tiles, schur_basis, membership_map):
    rows = transition_tiles.shape[0]
    count = lax.axis_size("rows")
    me = lax.axis_index("rows")
    mates = [(i, i ^ 1) for i in range(count)]
    others = []
    for i in range(1, count - 1, 2):
        others += [(i, i + 1), (i + 1, i)]

    def swap(array, pairs):
        return lax.ppermute(array, "rows", pairs)

    limit = 11 * rows // 16
    where = jnp.stack([me * rows, me % 2]).astype(I32)
    columns = column_tiles.T
    mate, other = swap(schur_basis, mates), swap(schur_basis, others)
    turned, inverse, plan, wanted = prep(where, columns, transition_tiles)
    asked = swap(wanted, others)
    image, sums = near_rows(plan, turned, inverse, schur_basis, mate, False, False)
    if whole:
        image = send = far_rows_whole(plan, turned, inverse, other, sums, image, False)
        sending = asked
    else:
        image, send, sending = far_rows_first(
            limit, asked, plan, turned, inverse, other, sums, image
        )
    for step in range(1, PRODUCTS):
        last = step == PRODUCTS - 1
        mate, other = swap(image, mates), swap(send, others)
        image, sums, *near = near_rows(plan, turned, inverse, image, mate, True, last)
        if last:
            parts, gram = far_rows_last(
                whole, plan, turned, inverse, sending, other, near[0], sums, image
            )
        elif whole:
            image = send = far_rows_whole(plan, turned, inverse, other, sums, image, True)
        else:
            image, send = far_rows(plan, turned, inverse, sending, other, sums, image)
    distance = 1
    while distance < count:
        partner = swap(gram, [(i, i ^ distance) for i in range(count)])
        distance *= 2
        if distance < count:
            gram = gram + partner
    states = schur_basis.shape[1] * count
    return final(states, gram, partner, membership_map, parts)


def body(transition_tiles, column_tiles, schur_basis, membership_map):
    arguments = transition_tiles, column_tiles, schur_basis, membership_map
    out, short = memberships(False, *arguments)
    return lax.cond(
        short[0] > 0,
        lambda *given: memberships(True, *given[:4])[0],
        lambda *given: given[4],
        *arguments,
        out,
    )


def solution(mesh):
    return jax.shard_map(
        body,
        mesh=mesh,
        in_specs=(
            P(("groups", "rows"), None, None, None),
            P(("groups", "rows"), None),
            P(None, ("groups", "rows")),
            P("groups", None),
        ),
        out_specs=P(None, ("groups", "rows")),
        check_vma=False,
    )
```

```python
import functools

import jax
import jax.numpy as jnp
from jax import lax
from jax.experimental import pallas as pl
from jax.experimental.pallas import tpu as pltpu
from jax.sharding import PartitionSpec as P

PRODUCTS = 4
BLOCK = 16
CHUNK = 8
F32 = jnp.float32
BF16 = jnp.bfloat16
I32 = jnp.int32
NN = (((1,), (0,)), ((), ()))
NT = (((1,), (1,)), ((), ()))
VM = pl.BlockSpec(memory_space=pltpu.VMEM)
SM = pl.BlockSpec(memory_space=pltpu.SMEM)
HB = pl.BlockSpec(memory_space=pltpu.HBM)


def in_vmem(array):
    return pltpu.with_memory_space_constraint(array, pltpu.VMEM)


def in_hbm(array):
    return pltpu.with_memory_space_constraint(array, pltpu.HBM)


def cost(flops, moved):
    return pl.CostEstimate(flops=flops, bytes_accessed=moved, transcendentals=0)


def params(mib):
    return pltpu.CompilerParams(vmem_limit_bytes=mib * 2**20)


def ranks(named):
    rows = named.shape[0]
    h = lax.broadcasted_iota(I32, (rows, rows), 0)
    other = lax.broadcasted_iota(I32, (rows, rows), 1)
    before = jnp.where(other < h, 1.0, 0.0).astype(BF16)
    ones = jnp.ones((rows, rows), BF16)
    total = lax.dot_general(named.astype(BF16), ones, NN, preferred_element_type=F32)
    mark = jnp.where(total > 0.5, 1.0, 0.0)
    rank = lax.dot_general(before, mark.astype(BF16), NN, preferred_element_type=F32)
    return mark, rank


def lines(slots):
    far = slots - 1
    return slots, slots + far, slots + 2 * far, slots + 3 * far, slots + 3 * far + 1


def plan_height(slots):
    return (lines(slots)[-1] + 3 + 7) // 8 * 8


def draft_plan(first, parity, columns, draft, wanted):
    slots, rows = columns.shape
    panel, counted, slot, order, reads = lines(slots)
    low = jnp.where(parity == 0, 2 * rows, rows)
    high = jnp.where(parity == 0, rows, 2 * rows)
    offset = columns - first
    spot = jnp.where(
        offset < 0,
        offset + (rows + low),
        jnp.where(offset >= rows, offset + (high - rows), offset),
    )
    draft[0:slots, 0:rows] = jnp.minimum(spot, 2 * rows)
    h = lax.broadcasted_iota(I32, (rows, rows), 0)
    lane = lax.broadcasted_iota(I32, (rows, rows), 1)
    ones = jnp.ones((rows, rows), BF16)
    equal = [
        jnp.where(spot[s : s + 1] - 2 * rows == h, 1.0, 0.0) for s in range(slots)
    ]
    mark, rank = ranks(functools.reduce(jnp.add, equal))
    here = jnp.where((mark > 0.5) & (rank.astype(I32) == lane), h, 0)
    wanted[0:1, 0:rows] = jnp.sum(here.astype(F32), axis=0, keepdims=True).astype(I32)
    read = jnp.sum(mark, axis=0, keepdims=True).astype(I32)
    wanted[1:2, 0:rows] = read
    draft[reads + 2 : reads + 3, 0:rows] = read
    none = jnp.zeros((1, rows), I32)
    seen = none
    tiles, places, named = [[none + start] * (slots - 1) for start in (rows, rows, 0)]
    for s in range(slots):
        place = jnp.sum(equal[s] * rank, axis=0, keepdims=True).astype(I32)
        tile = spot[s : s + 1] - 2 * rows
        far = jnp.where(tile >= 0, 1, 0)
        for j in range(min(s + 1, slots - 1)):
            hit = (far == 1) & (seen == j)
            tiles[j] = jnp.where(hit, tile, tiles[j])
            places[j] = jnp.where(hit, place, places[j])
            named[j] = jnp.where(hit, s, named[j])
        seen = seen + far
    for j in range(slots - 1):
        draft[panel + j : panel + j + 1, 0:rows] = tiles[j]
        draft[counted + j : counted + j + 1, 0:rows] = places[j]
        draft[slot + j : slot + j + 1, 0:rows] = named[j]
    along = jnp.broadcast_to(seen.astype(F32), (rows, rows))
    down = lax.dot_general(
        jnp.where(h == lane, along, 0.0).astype(BF16), ones, NN, preferred_element_type=F32
    )
    ahead = jnp.where((down < along) | ((down == along) & (h < lane)), 1.0, 0.0)
    position = jnp.sum(ahead, axis=0, keepdims=True).astype(I32)
    taken = jnp.where(position == h, 1.0, 0.0).astype(BF16)
    line = lax.broadcasted_iota(I32, (16, rows), 1).astype(BF16)
    sorted_rows = lax.dot_general(line, taken, NT, preferred_element_type=F32)
    draft[order : order + 1, 0:rows] = sorted_rows[0:1].astype(I32)
    draft[reads : reads + 1, 0:rows] = seen
    touched = jnp.sum(jnp.minimum(seen, 1).astype(F32), axis=1, keepdims=True)
    draft[reads + 1 : reads + 2, 0:rows] = jnp.broadcast_to(touched, (1, rows)).astype(I32)


def prep_kernel(
    where, columns, tiles, turned, inverse, plan, wanted,
    landing, named, draft, arrived, here, done,
):
    rows, slots, size, _ = tiles.shape
    chunks = rows // CHUNK

    def copy_in(i):
        part = pl.ds(i * CHUNK, CHUNK)
        return pltpu.make_async_copy(tiles.at[part], landing.at[part], arrived.at[i])

    copy_columns = pltpu.make_async_copy(columns, named, here)
    copy_columns.start()
    for i in range(chunks):
        copy_in(i).start()
    copy_columns.wait()
    draft_plan(where[0], where[1], named[...], draft, wanted)
    copy_plan = pltpu.make_async_copy(draft, plan, done)
    copy_plan.start()

    def step(i, carry):
        copy_in(i).wait()
        for u in range(CHUNK):
            r = i * CHUNK + u
            total = None
            for s in range(slots):
                tile = landing[r, s].T
                turned[r, pl.ds(s * size, size), :] = tile
                tile = tile.astype(F32)
                total = tile if total is None else total + tile
            inverse[pl.ds(r, 1), :] = 1.0 / jnp.sum(total, axis=0, keepdims=True)
        return carry

    lax.fori_loop(0, chunks, step, 0)
    copy_plan.wait()


def prep(where, columns, tiles):
    rows, slots, size, _ = tiles.shape
    height = plan_height(slots)
    return pl.pallas_call(
        prep_kernel,
        out_shape=(
            pltpu.VMEM((rows, slots * size, size), BF16),
            pltpu.VMEM((rows, size), F32),
            pltpu.SMEM((height, 128), I32),
            pltpu.VMEM((8, 128), I32),
        ),
        in_specs=[SM, HB, HB],
        out_specs=(VM, VM, SM, VM),
        scratch_shapes=[
            pltpu.VMEM(tiles.shape, BF16),
            pltpu.VMEM(columns.shape, I32),
            pltpu.VMEM((height, 128), I32),
            pltpu.SemaphoreType.DMA((rows // CHUNK,)),
            pltpu.SemaphoreType.DMA,
            pltpu.SemaphoreType.DMA,
        ],
        compiler_params=params(14),
        cost_estimate=cost(2 * tiles.size * 16, 4 * tiles.size),
        name="prep",
    )(where, in_hbm(columns), in_hbm(tiles))


def fill(window, start, panel, tile_major):
    size = window.shape[2]
    if tile_major:
        window[start : start + panel.shape[0]] = panel[...]
    else:
        for t in range(panel.shape[1] // size):
            window[start + t] = panel[:, t * size : (t + 1) * size]


def thirds(x):
    high = x.astype(BF16)
    rest = x - high.astype(F32)
    middle = rest.astype(BF16)
    low = (rest - middle.astype(F32)).astype(BF16)
    return high, middle, low


def fold(squares, vectors):
    total = None
    for a, b in ((2, 2), (1, 2), (2, 1), (0, 2), (2, 0), (1, 1), (0, 1), (1, 0), (0, 0)):
        part = squares[a * vectors : (a + 1) * vectors, b * vectors : (b + 1) * vectors]
        total = part if total is None else total + part
    return total


def store(image, squares, picked, results, mine):
    if squares is None:
        for r, y in zip(picked, results):
            image[r] = y.astype(BF16)
        return None
    counted = []
    for r, y, keep in zip(picked, results, mine):
        stacked = jnp.concatenate(thirds(y), axis=0)
        image[r] = stacked
        counted.append(jnp.where(keep, stacked, jnp.zeros_like(stacked)))
    wide = jnp.concatenate(counted, axis=1)
    return squares + lax.dot_general(wide, wide, NT, preferred_element_type=F32)


def near_kernel(tile_major, last, count, plan, turned, inverse, own, *refs):
    mate, (image, sums, *refs) = refs[:count], refs[count:]
    rows, depth, size = turned.shape
    slots = depth // size
    reads = lines(slots)[-1]
    window = refs[-1]
    fill(window, 0, own, tile_major)
    start = rows
    for panel in mate:
        fill(window, start, panel, tile_major)
        start += panel.shape[0]
    window[2 * rows] = jnp.zeros(window.shape[1:], BF16)

    def step(block, squares):
        picked = [block * BLOCK + u for u in range(BLOCK)]
        vectors = [
            jnp.concatenate([window[plan[s, r]] for s in range(slots)], axis=1)
            for r in picked
        ]
        products = [
            lax.dot_general(x, turned[r], NN, preferred_element_type=F32)
            for x, r in zip(vectors, picked)
        ]
        results = [y * inverse[pl.ds(r, 1), :] for r, y in zip(picked, products)]
        for r, y in zip(picked, results):
            sums[r] = y
        mine = [plan[reads, r] == 0 for r in picked]
        return store(image, squares, picked, results, mine)

    begin = jnp.zeros(refs[0].shape, F32) if last else None
    total = lax.fori_loop(0, rows // BLOCK, step, begin)
    if last:
        refs[0][...] = total


def far_part(base, plan, turned, inverse, sums, panel, image, squares):
    rows, depth, size = turned.shape
    slots = depth // size
    slot, order, reads = lines(slots)[2:]
    panel[rows] = jnp.zeros(panel.shape[1:], BF16)

    def rows_of(start, count):
        picked = [plan[order, start + u] for u in range(BLOCK)]
        products = []
        for r in picked:
            x = [panel[plan[base + j, r]] for j in range(count)]
            w = [
                turned[r, pl.ds(pl.multiple_of(plan[slot + j, r] * size, size), size), :]
                for j in range(count)
            ]
            products.append(
                lax.dot_general(
                    jnp.concatenate(x, axis=1),
                    jnp.concatenate(w, axis=0),
                    NN,
                    preferred_element_type=F32,
                )
            )
        return picked, [
            sums[r] + y * inverse[pl.ds(r, 1), :] for r, y in zip(picked, products)
        ]

    def step(block, carry):
        start = rows - (block + 1) * BLOCK
        most = plan[reads, plan[order, start + BLOCK - 1]]
        for count in range(1, slots):

            @pl.when(most == count)
            def _():
                picked, results = rows_of(start, count)
                mine = [plan[reads, r] > 0 for r in picked]
                if squares is None:
                    store(image, None, picked, results, mine)
                else:
                    squares[...] = store(image, squares[...], picked, results, mine)

        return carry

    touched = plan[reads + 1, 0]
    lax.fori_loop(0, (touched + BLOCK - 1) // BLOCK, step, 0)


def pack(image, sending, send):
    for k in range(send.shape[0]):
        send[k] = image[sending[0, k]]


def halve(image, halves):
    half = halves[0].shape[0]
    for i, part in enumerate(halves):
        part[...] = image[i * half : (i + 1) * half]


def far_first_kernel(
    asked, plan, turned, inverse, other, sums, i_in, image, left, right, send, sending, panel, done
):
    rows, depth, size = turned.shape
    copy = pltpu.make_async_copy(asked, sending, done)
    copy.start()
    fill(panel, 0, other, False)
    base = lines(depth // size)[0]
    far_part(base, plan, turned, inverse, sums, panel, image, None)
    copy.wait()
    pack(image, sending, send)
    halve(image, (left, right))


def far_kernel(sending, plan, turned, inverse, other, sums, i_in, image, left, right, send, panel):
    rows, depth, size = turned.shape
    fill(panel, 0, other, True)
    base = lines(depth // size)[1]
    far_part(base, plan, turned, inverse, sums, panel, image, None)
    pack(image, sending, send)
    halve(image, (left, right))


def far_whole_kernel(
    tile_major, plan, turned, inverse, other, sums, i_in, image, left, right, panel
):
    rows, depth, size = turned.shape
    fill(panel, 0, other, tile_major)
    base = lines(depth // size)[0]
    far_part(base, plan, turned, inverse, sums, panel, image, None)
    halve(image, (left, right))


def far_last_kernel(
    whole, sending, plan, turned, inverse, other, near, sums, i_in, image, gram, panel, squares
):
    rows, depth, size = turned.shape
    slots = depth // size
    vectors = gram.shape[1]
    fill(panel, 0, other, True)
    squares[...] = near[...]
    base = lines(slots)[0 if whole else 1]
    far_part(base, plan, turned, inverse, sums, panel, image, squares)
    gram[0:vectors] = fold(squares[...], vectors)
    read = plan[lines(slots)[-1] + 2, 0]
    short = jnp.maximum(read, sending[1, 0]) > other.shape[0]
    gram[vectors:] = jnp.zeros((8, vectors), F32) + jnp.where(short, 1.0, 0.0)


def near_rows(plan, turned, inverse, own, mate, tile_major, last):
    rows, depth, size = turned.shape
    vectors = own.shape[1 if tile_major else 0]
    height = 3 * vectors if last else vectors
    shapes = (
        pltpu.VMEM((rows, height, size), BF16),
        pltpu.VMEM((rows, vectors, size), F32),
    )
    if last:
        shapes += (pltpu.VMEM((height, height), F32),)
    return pl.pallas_call(
        functools.partial(near_kernel, tile_major, last, len(mate)),
        out_shape=shapes,
        in_specs=[SM, VM, VM, VM] + [VM] * len(mate),
        out_specs=(VM,) * len(shapes),
        scratch_shapes=[pltpu.VMEM((2 * rows + 1, vectors, size), BF16)],
        compiler_params=params(4),
        cost_estimate=cost(0, 1024),
        name="near_rows",
    )(plan, *map(in_vmem, (turned, inverse, own, *mate)))


def far_call(kernel, ins, in_specs, outs, out_specs, turned, vectors, scratch=()):
    rows, depth, size = turned.shape
    return pl.pallas_call(
        kernel,
        out_shape=outs,
        in_specs=in_specs,
        out_specs=out_specs,
        scratch_shapes=[pltpu.VMEM((rows + 1, vectors, size), BF16), *scratch],
        input_output_aliases={len(ins) - 1: 0},
        compiler_params=params(4),
        cost_estimate=cost(20 * rows * depth * size, rows * depth * size),
        name="far_rows",
    )(*ins)


def of(array):
    return pltpu.VMEM(array.shape, array.dtype)


def halves_of(image):
    rows, vectors, size = image.shape
    return (pltpu.VMEM((rows // 2, vectors, size), BF16),) * 2


def far_rows_first(limit, asked, plan, turned, inverse, other, sums, image):
    rows, vectors, size = image.shape
    return far_call(
        far_first_kernel,
        (in_vmem(asked), plan, *map(in_vmem, (turned, inverse, other, sums, image))),
        [VM, SM] + [VM] * 5,
        (
            of(image),
            *halves_of(image),
            pltpu.VMEM((limit, vectors, size), BF16),
            pltpu.SMEM((8, 128), I32),
        ),
        (VM, VM, VM, VM, SM),
        turned,
        vectors,
        [pltpu.SemaphoreType.DMA],
    )


def far_rows(plan, turned, inverse, sending, other, sums, image):
    return far_call(
        far_kernel,
        (sending, plan, *map(in_vmem, (turned, inverse, other, sums, image))),
        [SM, SM] + [VM] * 5,
        (of(image), *halves_of(image), of(other)),
        (VM,) * 4,
        turned,
        image.shape[1],
    )


def far_rows_whole(plan, turned, inverse, other, sums, image, tile_major):
    return far_call(
        functools.partial(far_whole_kernel, tile_major),
        (plan, *map(in_vmem, (turned, inverse, other, sums, image))),
        [SM] + [VM] * 5,
        (of(image), *halves_of(image)),
        (VM,) * 3,
        turned,
        image.shape[1],
    )


def far_rows_last(whole, plan, turned, inverse, sending, other, near, sums, image):
    vectors = near.shape[0] // 3
    return far_call(
        functools.partial(far_last_kernel, whole),
        (sending, plan, *map(in_vmem, (turned, inverse, other, near, sums, image))),
        [SM, SM] + [VM] * 6,
        (of(image), pltpu.VMEM((vectors + 8, vectors), F32)),
        (VM,) * 2,
        turned,
        vectors,
        [pltpu.VMEM(near.shape, F32)],
    )


def inverse_factor(gram):
    count = gram.shape[0]
    step = 8
    row = lax.broadcasted_iota(I32, (count, count), 0)
    column = lax.broadcasted_iota(I32, (count, count), 1)
    work = jnp.concatenate([gram, jnp.where(row == column, 1.0, 0.0)], axis=1)
    below = lax.broadcasted_iota(I32, work.shape, 0)
    for begin in range(0, count, step):
        spread = [
            jnp.broadcast_to(work[:, k : k + 1], work.shape)
            for k in range(begin, begin + step)
        ]
        for j in range(step):
            k = begin + j
            factor = jnp.where(below > k, spread[j], 0.0)
            pivot = 1.0 / spread[j][k : k + 1]
            for q in range(j + 1, step):
                spread[q] = spread[q] - factor * (spread[q][k : k + 1] * pivot)
            work = work - factor * (work[k : k + 1] * pivot)
    pivots = jnp.sum(
        jnp.where(row == column, work[:, :count], 0.0), axis=1, keepdims=True
    )
    return work[:, count:] * lax.rsqrt(pivots)


def final_kernel(states, gram_a, gram_b, mapping, parts, out, short, ready, sent):
    rows, depth, size = parts.shape
    vectors = depth // 3
    total = gram_a[...] + gram_b[...]
    short[0] = jnp.max(total[vectors:]).astype(I32)
    factor = inverse_factor(total[:vectors] / states)
    combined = lax.dot_general(
        mapping[...],
        factor,
        (((0,), (0,)), ((), ())),
        precision=lax.Precision.HIGHEST,
        preferred_element_type=F32,
    )
    high, middle, low = thirds(combined)
    blank = jnp.zeros_like(high)
    left = jnp.concatenate(
        [
            jnp.concatenate([high, high, high], axis=1),
            jnp.concatenate([middle, middle, blank], axis=1),
            jnp.concatenate([low, blank, blank], axis=1),
        ],
        axis=0,
    )
    copies = []
    for g in range(rows // CHUNK):
        for r in range(g * CHUNK, (g + 1) * CHUNK):
            y = lax.dot_general(left, parts[r], NN, preferred_element_type=F32)
            ready[:, r * size : (r + 1) * size] = (
                y[2 * vectors :] + y[vectors : 2 * vectors]
            ) + y[:vectors]
        part = pl.ds(g * CHUNK * size, CHUNK * size)
        copies.append(pltpu.make_async_copy(ready.at[:, part], out.at[:, part], sent.at[g]))
        copies[-1].start()
    for copy in copies:
        copy.wait()


def final(states, gram_a, gram_b, mapping, parts):
    rows, depth, size = parts.shape
    vectors = depth // 3
    return pl.pallas_call(
        functools.partial(final_kernel, float(states)),
        out_shape=(
            jax.ShapeDtypeStruct((vectors, rows * size), F32),
            pltpu.SMEM((1,), I32),
        ),
        in_specs=[VM, VM, VM, VM],
        out_specs=(HB, SM),
        scratch_shapes=[
            pltpu.VMEM((vectors, rows * size), F32),
            pltpu.SemaphoreType.DMA((rows // CHUNK,)),
        ],
        compiler_params=params(8),
        cost_estimate=cost(6 * parts.size * vectors, 4 * parts.size),
        name="memberships",
    )(gram_a, gram_b, mapping, in_vmem(parts))


def memberships(whole, transition_tiles, column_tiles, schur_basis, membership_map):
    rows = transition_tiles.shape[0]
    count = lax.axis_size("rows")
    me = lax.axis_index("rows")
    mates = [(i, i ^ 1) for i in range(count)]
    others = []
    for i in range(1, count - 1, 2):
        others += [(i, i + 1), (i + 1, i)]

    def swap(array, pairs):
        return lax.ppermute(array, "rows", pairs)

    limit = 11 * rows // 16
    where = jnp.stack([me * rows, me % 2]).astype(I32)
    columns = column_tiles.T
    mate, other = swap(schur_basis, mates), swap(schur_basis, others)
    turned, inverse, plan, wanted = prep(where, columns, transition_tiles)
    asked = swap(wanted, others)
    image, sums = near_rows(plan, turned, inverse, schur_basis, (mate,), False, False)
    if whole:
        image, *halves = far_rows_whole(plan, turned, inverse, other, sums, image, False)
        send, sending = image, asked
    else:
        image, *halves, send, sending = far_rows_first(
            limit, asked, plan, turned, inverse, other, sums, image
        )
    for step in range(1, PRODUCTS):
        last = step == PRODUCTS - 1
        other = swap(send, others)
        mate = [swap(half, mates) for half in halves]
        image, sums, *near = near_rows(plan, turned, inverse, image, mate, True, last)
        if last:
            parts, gram = far_rows_last(
                whole, plan, turned, inverse, sending, other, near[0], sums, image
            )
        elif whole:
            image, *halves = far_rows_whole(plan, turned, inverse, other, sums, image, True)
            send = image
        else:
            image, *halves, send = far_rows(plan, turned, inverse, sending, other, sums, image)
    distance = 1
    while distance < count:
        partner = swap(gram, [(i, i ^ distance) for i in range(count)])
        distance *= 2
        if distance < count:
            gram = gram + partner
    states = schur_basis.shape[1] * count
    return final(states, gram, partner, membership_map, parts)


def body(transition_tiles, column_tiles, schur_basis, membership_map):
    arguments = transition_tiles, column_tiles, schur_basis, membership_map
    out, short = memberships(False, *arguments)
    return lax.cond(
        short[0] > 0,
        lambda *given: memberships(True, *given[:4])[0],
        lambda *given: given[4],
        *arguments,
        out,
    )


def solution(mesh):
    return jax.shard_map(
        body,
        mesh=mesh,
        in_specs=(
            P(("groups", "rows"), None, None, None),
            P(("groups", "rows"), None),
            P(None, ("groups", "rows")),
            P("groups", None),
        ),
        out_specs=P(None, ("groups", "rows")),
        check_vma=False,
    )
```

```python
import functools

import jax
import jax.numpy as jnp
from jax import lax
from jax.experimental import pallas as pl
from jax.experimental.pallas import tpu as pltpu
from jax.sharding import PartitionSpec as P

PRODUCTS = 4
BLOCK = 16
CHUNK = 8
F32 = jnp.float32
BF16 = jnp.bfloat16
I32 = jnp.int32
NN = (((1,), (0,)), ((), ()))
NT = (((1,), (1,)), ((), ()))
VM = pl.BlockSpec(memory_space=pltpu.VMEM)
SM = pl.BlockSpec(memory_space=pltpu.SMEM)
HB = pl.BlockSpec(memory_space=pltpu.HBM)


def in_vmem(array):
    return pltpu.with_memory_space_constraint(array, pltpu.VMEM)


def in_hbm(array):
    return pltpu.with_memory_space_constraint(array, pltpu.HBM)


def cost(flops, moved):
    return pl.CostEstimate(flops=flops, bytes_accessed=moved, transcendentals=0)


def params(mib):
    return pltpu.CompilerParams(vmem_limit_bytes=mib * 2**20)


def ranks(named):
    rows = named.shape[0]
    h = lax.broadcasted_iota(I32, (rows, rows), 0)
    other = lax.broadcasted_iota(I32, (rows, rows), 1)
    before = jnp.where(other < h, 1.0, 0.0).astype(BF16)
    ones = jnp.ones((rows, rows), BF16)
    total = lax.dot_general(named.astype(BF16), ones, NN, preferred_element_type=F32)
    mark = jnp.where(total > 0.5, 1.0, 0.0)
    rank = lax.dot_general(before, mark.astype(BF16), NN, preferred_element_type=F32)
    return mark, rank


def lines(slots):
    far = slots - 1
    return slots, slots + far, slots + 2 * far, slots + 3 * far, slots + 3 * far + 1


def plan_height(slots):
    return (lines(slots)[-1] + 3 + 7) // 8 * 8


def draft_plan(first, parity, columns, draft, wanted):
    slots, rows = columns.shape
    panel, counted, slot, order, reads = lines(slots)
    low = jnp.where(parity == 0, 2 * rows, rows)
    high = jnp.where(parity == 0, rows, 2 * rows)
    offset = columns - first
    spot = jnp.where(
        offset < 0,
        offset + (rows + low),
        jnp.where(offset >= rows, offset + (high - rows), offset),
    )
    draft[0:slots, 0:rows] = jnp.minimum(spot, 2 * rows)
    h = lax.broadcasted_iota(I32, (rows, rows), 0)
    lane = lax.broadcasted_iota(I32, (rows, rows), 1)
    ones = jnp.ones((rows, rows), BF16)
    equal = [
        jnp.where(spot[s : s + 1] - 2 * rows == h, 1.0, 0.0) for s in range(slots)
    ]
    mark, rank = ranks(functools.reduce(jnp.add, equal))
    here = jnp.where((mark > 0.5) & (rank.astype(I32) == lane), h, 0)
    wanted[0:1, 0:rows] = jnp.sum(here.astype(F32), axis=0, keepdims=True).astype(I32)
    read = jnp.sum(mark, axis=0, keepdims=True).astype(I32)
    wanted[1:2, 0:rows] = read
    draft[reads + 2 : reads + 3, 0:rows] = read
    none = jnp.zeros((1, rows), I32)
    seen = none
    tiles, places, named = [[none + start] * (slots - 1) for start in (rows, rows, 0)]
    for s in range(slots):
        place = jnp.sum(equal[s] * rank, axis=0, keepdims=True).astype(I32)
        tile = spot[s : s + 1] - 2 * rows
        far = jnp.where(tile >= 0, 1, 0)
        for j in range(min(s + 1, slots - 1)):
            hit = (far == 1) & (seen == j)
            tiles[j] = jnp.where(hit, tile, tiles[j])
            places[j] = jnp.where(hit, place, places[j])
            named[j] = jnp.where(hit, s, named[j])
        seen = seen + far
    for j in range(slots - 1):
        draft[panel + j : panel + j + 1, 0:rows] = tiles[j]
        draft[counted + j : counted + j + 1, 0:rows] = places[j]
        draft[slot + j : slot + j + 1, 0:rows] = named[j]
    along = jnp.broadcast_to(seen.astype(F32), (rows, rows))
    down = lax.dot_general(
        jnp.where(h == lane, along, 0.0).astype(BF16), ones, NN, preferred_element_type=F32
    )
    ahead = jnp.where((down < along) | ((down == along) & (h < lane)), 1.0, 0.0)
    position = jnp.sum(ahead, axis=0, keepdims=True).astype(I32)
    taken = jnp.where(position == h, 1.0, 0.0).astype(BF16)
    line = lax.broadcasted_iota(I32, (16, rows), 1).astype(BF16)
    sorted_rows = lax.dot_general(line, taken, NT, preferred_element_type=F32)
    draft[order : order + 1, 0:rows] = sorted_rows[0:1].astype(I32)
    draft[reads : reads + 1, 0:rows] = seen
    touched = jnp.sum(jnp.minimum(seen, 1).astype(F32), axis=1, keepdims=True)
    draft[reads + 1 : reads + 2, 0:rows] = jnp.broadcast_to(touched, (1, rows)).astype(I32)


def prep_kernel(
    where, columns, tiles, turned, inverse, plan, wanted,
    landing, named, draft, arrived, here, done,
):
    rows, slots, size, _ = tiles.shape
    chunks = rows // CHUNK

    def copy_in(i):
        part = pl.ds(i * CHUNK, CHUNK)
        return pltpu.make_async_copy(tiles.at[part], landing.at[part], arrived.at[i])

    copy_columns = pltpu.make_async_copy(columns, named, here)
    copy_columns.start()
    for i in range(chunks):
        copy_in(i).start()
    copy_plan = pltpu.make_async_copy(draft, plan, done)

    def step(i, carry):
        copy_in(i).wait()
        for u in range(CHUNK):
            r = i * CHUNK + u
            total = None
            for s in range(slots):
                tile = landing[r, s].T
                turned[r, pl.ds(s * size, size), :] = tile
                tile = tile.astype(F32)
                total = tile if total is None else total + tile
            inverse[pl.ds(r, 1), :] = 1.0 / jnp.sum(total, axis=0, keepdims=True)
        return carry

    lax.fori_loop(0, chunks // 2, step, 0)
    copy_columns.wait()
    draft_plan(where[0], where[1], named[...], draft, wanted)
    copy_plan.start()
    lax.fori_loop(chunks // 2, chunks, step, 0)
    copy_plan.wait()


def prep(where, columns, tiles):
    rows, slots, size, _ = tiles.shape
    height = plan_height(slots)
    return pl.pallas_call(
        prep_kernel,
        out_shape=(
            pltpu.VMEM((rows, slots * size, size), BF16),
            pltpu.VMEM((rows, size), F32),
            pltpu.SMEM((height, 128), I32),
            pltpu.VMEM((8, 128), I32),
        ),
        in_specs=[SM, HB, HB],
        out_specs=(VM, VM, SM, VM),
        scratch_shapes=[
            pltpu.VMEM(tiles.shape, BF16),
            pltpu.VMEM(columns.shape, I32),
            pltpu.VMEM((height, 128), I32),
            pltpu.SemaphoreType.DMA((rows // CHUNK,)),
            pltpu.SemaphoreType.DMA,
            pltpu.SemaphoreType.DMA,
        ],
        compiler_params=params(14),
        cost_estimate=cost(2 * tiles.size * 16, 4 * tiles.size),
        name="prep",
    )(where, in_hbm(columns), in_hbm(tiles))


def fill(window, start, panel, tile_major):
    size = window.shape[2]
    if tile_major:
        window[start : start + panel.shape[0]] = panel[...]
    else:
        for t in range(panel.shape[1] // size):
            window[start + t] = panel[:, t * size : (t + 1) * size]


def thirds(x):
    high = x.astype(BF16)
    rest = x - high.astype(F32)
    middle = rest.astype(BF16)
    low = (rest - middle.astype(F32)).astype(BF16)
    return high, middle, low


def fold(squares, vectors):
    total = None
    for a, b in ((1, 1), (0, 1), (1, 0), (0, 0)):
        part = squares[a * vectors : (a + 1) * vectors, b * vectors : (b + 1) * vectors]
        total = part if total is None else total + part
    return total


def store(image, squares, picked, results, mine):
    if squares is None:
        for r, y in zip(picked, results):
            image[r] = y.astype(BF16)
        return None
    counted = []
    for r, y, keep in zip(picked, results, mine):
        stacked = jnp.concatenate(thirds(y)[:2], axis=0)
        image[r] = stacked
        counted.append(jnp.where(keep, stacked, jnp.zeros_like(stacked)))
    wide = jnp.concatenate(counted, axis=1)
    return squares + lax.dot_general(wide, wide, NT, preferred_element_type=F32)


def near_kernel(tile_major, last, count, plan, turned, inverse, own, *refs):
    mate, (image, sums, *refs) = refs[:count], refs[count:]
    rows, depth, size = turned.shape
    slots = depth // size
    reads = lines(slots)[-1]
    window = refs[-1]
    fill(window, 0, own, tile_major)
    start = rows
    for panel in mate:
        fill(window, start, panel, tile_major)
        start += panel.shape[0]
    window[2 * rows] = jnp.zeros(window.shape[1:], BF16)

    def step(block, squares):
        picked = [block * BLOCK + u for u in range(BLOCK)]
        vectors = [
            jnp.concatenate([window[plan[s, r]] for s in range(slots)], axis=1)
            for r in picked
        ]
        products = [
            lax.dot_general(x, turned[r], NN, preferred_element_type=F32)
            for x, r in zip(vectors, picked)
        ]
        results = [y * inverse[pl.ds(r, 1), :] for r, y in zip(picked, products)]
        for r, y in zip(picked, results):
            sums[r] = y
        mine = [plan[reads, r] == 0 for r in picked]
        return store(image, squares, picked, results, mine)

    begin = jnp.zeros(refs[0].shape, F32) if last else None
    total = lax.fori_loop(0, rows // BLOCK, step, begin)
    if last:
        refs[0][...] = total


def far_part(base, plan, turned, inverse, sums, panel, image, squares):
    rows, depth, size = turned.shape
    slots = depth // size
    slot, order, reads = lines(slots)[2:]
    panel[rows] = jnp.zeros(panel.shape[1:], BF16)

    def rows_of(start, count):
        picked = [plan[order, start + u] for u in range(BLOCK)]
        products = []
        for r in picked:
            x = [panel[plan[base + j, r]] for j in range(count)]
            w = [
                turned[r, pl.ds(pl.multiple_of(plan[slot + j, r] * size, size), size), :]
                for j in range(count)
            ]
            products.append(
                lax.dot_general(
                    jnp.concatenate(x, axis=1),
                    jnp.concatenate(w, axis=0),
                    NN,
                    preferred_element_type=F32,
                )
            )
        return picked, [
            sums[r] + y * inverse[pl.ds(r, 1), :] for r, y in zip(picked, products)
        ]

    def step(block, carry):
        start = rows - (block + 1) * BLOCK
        most = plan[reads, plan[order, start + BLOCK - 1]]
        for count in range(1, slots):

            @pl.when(most == count)
            def _():
                picked, results = rows_of(start, count)
                mine = [plan[reads, r] > 0 for r in picked]
                if squares is None:
                    store(image, None, picked, results, mine)
                else:
                    squares[...] = store(image, squares[...], picked, results, mine)

        return carry

    touched = plan[reads + 1, 0]
    lax.fori_loop(0, (touched + BLOCK - 1) // BLOCK, step, 0)


def pack(image, sending, send):
    for k in range(send.shape[0]):
        send[k] = image[sending[0, k]]


def halve(image, halves):
    half = halves[0].shape[0]
    for i, part in enumerate(halves):
        part[...] = image[i * half : (i + 1) * half]


def far_first_kernel(
    asked, plan, turned, inverse, other, sums, i_in, image, left, right, send, sending, panel, done
):
    rows, depth, size = turned.shape
    copy = pltpu.make_async_copy(asked, sending, done)
    copy.start()
    fill(panel, 0, other, False)
    base = lines(depth // size)[0]
    far_part(base, plan, turned, inverse, sums, panel, image, None)
    copy.wait()
    pack(image, sending, send)
    halve(image, (left, right))


def far_kernel(sending, plan, turned, inverse, other, sums, i_in, image, left, right, send, panel):
    rows, depth, size = turned.shape
    fill(panel, 0, other, True)
    base = lines(depth // size)[1]
    far_part(base, plan, turned, inverse, sums, panel, image, None)
    pack(image, sending, send)
    halve(image, (left, right))


def far_whole_kernel(
    tile_major, plan, turned, inverse, other, sums, i_in, image, left, right, panel
):
    rows, depth, size = turned.shape
    fill(panel, 0, other, tile_major)
    base = lines(depth // size)[0]
    far_part(base, plan, turned, inverse, sums, panel, image, None)
    halve(image, (left, right))


def far_last_kernel(
    whole, sending, plan, turned, inverse, other, near, sums, i_in, image, gram, panel, squares
):
    rows, depth, size = turned.shape
    slots = depth // size
    vectors = gram.shape[1]
    fill(panel, 0, other, True)
    squares[...] = near[...]
    base = lines(slots)[0 if whole else 1]
    far_part(base, plan, turned, inverse, sums, panel, image, squares)
    gram[0:vectors] = fold(squares[...], vectors)
    read = plan[lines(slots)[-1] + 2, 0]
    short = jnp.maximum(read, sending[1, 0]) > other.shape[0]
    gram[vectors:] = jnp.zeros((8, vectors), F32) + jnp.where(short, 1.0, 0.0)


def near_rows(plan, turned, inverse, own, mate, tile_major, last):
    rows, depth, size = turned.shape
    vectors = own.shape[1 if tile_major else 0]
    height = 2 * vectors if last else vectors
    shapes = (
        pltpu.VMEM((rows, height, size), BF16),
        pltpu.VMEM((rows, vectors, size), F32),
    )
    if last:
        shapes += (pltpu.VMEM((height, height), F32),)
    return pl.pallas_call(
        functools.partial(near_kernel, tile_major, last, len(mate)),
        out_shape=shapes,
        in_specs=[SM, VM, VM, VM] + [VM] * len(mate),
        out_specs=(VM,) * len(shapes),
        scratch_shapes=[pltpu.VMEM((2 * rows + 1, vectors, size), BF16)],
        compiler_params=params(4),
        cost_estimate=cost(0, 1024),
        name="near_rows",
    )(plan, *map(in_vmem, (turned, inverse, own, *mate)))


def far_call(kernel, ins, in_specs, outs, out_specs, turned, vectors, scratch=()):
    rows, depth, size = turned.shape
    return pl.pallas_call(
        kernel,
        out_shape=outs,
        in_specs=in_specs,
        out_specs=out_specs,
        scratch_shapes=[pltpu.VMEM((rows + 1, vectors, size), BF16), *scratch],
        input_output_aliases={len(ins) - 1: 0},
        compiler_params=params(4),
        cost_estimate=cost(20 * rows * depth * size, rows * depth * size),
        name="far_rows",
    )(*ins)


def of(array):
    return pltpu.VMEM(array.shape, array.dtype)


def halves_of(image):
    rows, vectors, size = image.shape
    return (pltpu.VMEM((rows // 2, vectors, size), BF16),) * 2


def far_rows_first(limit, asked, plan, turned, inverse, other, sums, image):
    rows, vectors, size = image.shape
    return far_call(
        far_first_kernel,
        (in_vmem(asked), plan, *map(in_vmem, (turned, inverse, other, sums, image))),
        [VM, SM] + [VM] * 5,
        (
            of(image),
            *halves_of(image),
            pltpu.VMEM((limit, vectors, size), BF16),
            pltpu.SMEM((8, 128), I32),
        ),
        (VM, VM, VM, VM, SM),
        turned,
        vectors,
        [pltpu.SemaphoreType.DMA],
    )


def far_rows(plan, turned, inverse, sending, other, sums, image):
    return far_call(
        far_kernel,
        (sending, plan, *map(in_vmem, (turned, inverse, other, sums, image))),
        [SM, SM] + [VM] * 5,
        (of(image), *halves_of(image), of(other)),
        (VM,) * 4,
        turned,
        image.shape[1],
    )


def far_rows_whole(plan, turned, inverse, other, sums, image, tile_major):
    return far_call(
        functools.partial(far_whole_kernel, tile_major),
        (plan, *map(in_vmem, (turned, inverse, other, sums, image))),
        [SM] + [VM] * 5,
        (of(image), *halves_of(image)),
        (VM,) * 3,
        turned,
        image.shape[1],
    )


def far_rows_last(whole, plan, turned, inverse, sending, other, near, sums, image):
    vectors = near.shape[0] // 2
    return far_call(
        functools.partial(far_last_kernel, whole),
        (sending, plan, *map(in_vmem, (turned, inverse, other, near, sums, image))),
        [SM, SM] + [VM] * 6,
        (of(image), pltpu.VMEM((vectors + 8, vectors), F32)),
        (VM,) * 2,
        turned,
        vectors,
        [pltpu.VMEM(near.shape, F32)],
    )


def inverse_factor(gram):
    count = gram.shape[0]
    step = 8
    row = lax.broadcasted_iota(I32, (count, count), 0)
    column = lax.broadcasted_iota(I32, (count, count), 1)
    work = jnp.concatenate([gram, jnp.where(row == column, 1.0, 0.0)], axis=1)
    below = lax.broadcasted_iota(I32, work.shape, 0)
    for begin in range(0, count, step):
        spread = [
            jnp.broadcast_to(work[:, k : k + 1], work.shape)
            for k in range(begin, begin + step)
        ]
        for j in range(step):
            k = begin + j
            factor = jnp.where(below > k, spread[j], 0.0)
            pivot = 1.0 / spread[j][k : k + 1]
            for q in range(j + 1, step):
                spread[q] = spread[q] - factor * (spread[q][k : k + 1] * pivot)
            work = work - factor * (work[k : k + 1] * pivot)
    pivots = jnp.sum(
        jnp.where(row == column, work[:, :count], 0.0), axis=1, keepdims=True
    )
    return work[:, count:] * lax.rsqrt(pivots)


def final_kernel(states, gram_a, gram_b, mapping, parts, out, short, ready, sent):
    rows, depth, size = parts.shape
    vectors = depth // 2
    total = gram_a[...] + gram_b[...]
    short[0] = jnp.max(total[vectors:]).astype(I32)
    factor = inverse_factor(total[:vectors] / states)
    combined = lax.dot_general(
        mapping[...],
        factor,
        (((0,), (0,)), ((), ())),
        precision=lax.Precision.HIGHEST,
        preferred_element_type=F32,
    )
    high, middle, low = thirds(combined)
    blank = jnp.zeros_like(high)
    left = jnp.concatenate(
        [
            jnp.concatenate([high, high], axis=1),
            jnp.concatenate([middle, middle], axis=1),
            jnp.concatenate([low, blank], axis=1),
        ],
        axis=0,
    )
    copies = []
    for g in range(rows // CHUNK):
        for r in range(g * CHUNK, (g + 1) * CHUNK):
            y = lax.dot_general(left, parts[r], NN, preferred_element_type=F32)
            ready[:, r * size : (r + 1) * size] = (
                y[2 * vectors :] + y[vectors : 2 * vectors]
            ) + y[:vectors]
        part = pl.ds(g * CHUNK * size, CHUNK * size)
        copies.append(pltpu.make_async_copy(ready.at[:, part], out.at[:, part], sent.at[g]))
        copies[-1].start()
    for copy in copies:
        copy.wait()


def final(states, gram_a, gram_b, mapping, parts):
    rows, depth, size = parts.shape
    vectors = depth // 2
    return pl.pallas_call(
        functools.partial(final_kernel, float(states)),
        out_shape=(
            jax.ShapeDtypeStruct((vectors, rows * size), F32),
            pltpu.SMEM((1,), I32),
        ),
        in_specs=[VM, VM, VM, VM],
        out_specs=(HB, SM),
        scratch_shapes=[
            pltpu.VMEM((vectors, rows * size), F32),
            pltpu.SemaphoreType.DMA((rows // CHUNK,)),
        ],
        compiler_params=params(8),
        cost_estimate=cost(6 * parts.size * vectors, 4 * parts.size),
        name="memberships",
    )(gram_a, gram_b, mapping, in_vmem(parts))


def memberships(whole, transition_tiles, column_tiles, schur_basis, membership_map):
    rows = transition_tiles.shape[0]
    count = lax.axis_size("rows")
    me = lax.axis_index("rows")
    mates = [(i, i ^ 1) for i in range(count)]
    others = []
    for i in range(1, count - 1, 2):
        others += [(i, i + 1), (i + 1, i)]

    def swap(array, pairs):
        return lax.ppermute(array, "rows", pairs)

    limit = 11 * rows // 16
    where = jnp.stack([me * rows, me % 2]).astype(I32)
    columns = column_tiles.T
    mate, other = swap(schur_basis, mates), swap(schur_basis, others)
    turned, inverse, plan, wanted = prep(where, columns, transition_tiles)
    asked = swap(wanted, others)
    image, sums = near_rows(plan, turned, inverse, schur_basis, (mate,), False, False)
    if whole:
        image, *halves = far_rows_whole(plan, turned, inverse, other, sums, image, False)
        send, sending = image, asked
    else:
        image, *halves, send, sending = far_rows_first(
            limit, asked, plan, turned, inverse, other, sums, image
        )
    for step in range(1, PRODUCTS):
        last = step == PRODUCTS - 1
        other = swap(send, others)
        mate = [swap(half, mates) for half in halves]
        image, sums, *near = near_rows(plan, turned, inverse, image, mate, True, last)
        if last:
            parts, gram = far_rows_last(
                whole, plan, turned, inverse, sending, other, near[0], sums, image
            )
        elif whole:
            image, *halves = far_rows_whole(plan, turned, inverse, other, sums, image, True)
            send = image
        else:
            image, *halves, send = far_rows(plan, turned, inverse, sending, other, sums, image)
    distance = 1
    while distance < count:
        partner = swap(gram, [(i, i ^ distance) for i in range(count)])
        distance *= 2
        if distance < count:
            gram = gram + partner
    states = schur_basis.shape[1] * count
    return final(states, gram, partner, membership_map, parts)


def body(transition_tiles, column_tiles, schur_basis, membership_map):
    arguments = transition_tiles, column_tiles, schur_basis, membership_map
    out, short = memberships(False, *arguments)
    return lax.cond(
        short[0] > 0,
        lambda *given: memberships(True, *given[:4])[0],
        lambda *given: given[4],
        *arguments,
        out,
    )


def solution(mesh):
    return jax.shard_map(
        body,
        mesh=mesh,
        in_specs=(
            P(("groups", "rows"), None, None, None),
            P(("groups", "rows"), None),
            P(None, ("groups", "rows")),
            P("groups", None),
        ),
        out_specs=P(None, ("groups", "rows")),
        check_vma=False,
    )
```

```python
import functools

import jax
import jax.numpy as jnp
from jax import lax
from jax.experimental import pallas as pl
from jax.experimental.pallas import tpu as pltpu
from jax.sharding import PartitionSpec as P

PRODUCTS = 4
BLOCK = 16
CHUNK = 8
F32 = jnp.float32
BF16 = jnp.bfloat16
I32 = jnp.int32
NN = (((1,), (0,)), ((), ()))
NT = (((1,), (1,)), ((), ()))
VM = pl.BlockSpec(memory_space=pltpu.VMEM)
SM = pl.BlockSpec(memory_space=pltpu.SMEM)
HB = pl.BlockSpec(memory_space=pltpu.HBM)


def in_vmem(array):
    return pltpu.with_memory_space_constraint(array, pltpu.VMEM)


def in_hbm(array):
    return pltpu.with_memory_space_constraint(array, pltpu.HBM)


def cost(flops, moved):
    return pl.CostEstimate(flops=flops, bytes_accessed=moved, transcendentals=0)


def params(mib):
    return pltpu.CompilerParams(vmem_limit_bytes=mib * 2**20)


def ranks(named):
    rows = named.shape[0]
    h = lax.broadcasted_iota(I32, (rows, rows), 0)
    other = lax.broadcasted_iota(I32, (rows, rows), 1)
    before = jnp.where(other < h, 1.0, 0.0).astype(BF16)
    ones = jnp.ones((rows, rows), BF16)
    total = lax.dot_general(named.astype(BF16), ones, NN, preferred_element_type=F32)
    mark = jnp.where(total > 0.5, 1.0, 0.0)
    rank = lax.dot_general(before, mark.astype(BF16), NN, preferred_element_type=F32)
    return mark, rank


def lines(slots):
    far = slots - 1
    return slots, slots + far, slots + 2 * far, slots + 3 * far, slots + 3 * far + 1


def plan_height(slots):
    return (lines(slots)[-1] + 3 + 7) // 8 * 8


def draft_plan(first, parity, columns, draft, wanted):
    slots, rows = columns.shape
    panel, counted, slot, order, reads = lines(slots)
    low = jnp.where(parity == 0, 2 * rows, rows)
    high = jnp.where(parity == 0, rows, 2 * rows)
    offset = columns - first
    spot = jnp.where(
        offset < 0,
        offset + (rows + low),
        jnp.where(offset >= rows, offset + (high - rows), offset),
    )
    draft[0:slots, 0:rows] = jnp.minimum(spot, 2 * rows)
    h = lax.broadcasted_iota(I32, (rows, rows), 0)
    lane = lax.broadcasted_iota(I32, (rows, rows), 1)
    ones = jnp.ones((rows, rows), BF16)
    equal = [
        jnp.where(spot[s : s + 1] - 2 * rows == h, 1.0, 0.0) for s in range(slots)
    ]
    mark, rank = ranks(functools.reduce(jnp.add, equal))
    here = jnp.where((mark > 0.5) & (rank.astype(I32) == lane), h, 0)
    wanted[0:1, 0:rows] = jnp.sum(here.astype(F32), axis=0, keepdims=True).astype(I32)
    read = jnp.sum(mark, axis=0, keepdims=True).astype(I32)
    wanted[1:2, 0:rows] = read
    draft[reads + 2 : reads + 3, 0:rows] = read
    none = jnp.zeros((1, rows), I32)
    seen = none
    tiles, places, named = [[none + start] * (slots - 1) for start in (rows, rows, 0)]
    for s in range(slots):
        place = jnp.sum(equal[s] * rank, axis=0, keepdims=True).astype(I32)
        tile = spot[s : s + 1] - 2 * rows
        far = jnp.where(tile >= 0, 1, 0)
        for j in range(min(s + 1, slots - 1)):
            hit = (far == 1) & (seen == j)
            tiles[j] = jnp.where(hit, tile, tiles[j])
            places[j] = jnp.where(hit, place, places[j])
            named[j] = jnp.where(hit, s, named[j])
        seen = seen + far
    for j in range(slots - 1):
        draft[panel + j : panel + j + 1, 0:rows] = tiles[j]
        draft[counted + j : counted + j + 1, 0:rows] = places[j]
        draft[slot + j : slot + j + 1, 0:rows] = named[j]
    along = jnp.broadcast_to(seen.astype(F32), (rows, rows))
    down = lax.dot_general(
        jnp.where(h == lane, along, 0.0).astype(BF16), ones, NN, preferred_element_type=F32
    )
    ahead = jnp.where((down < along) | ((down == along) & (h < lane)), 1.0, 0.0)
    position = jnp.sum(ahead, axis=0, keepdims=True).astype(I32)
    taken = jnp.where(position == h, 1.0, 0.0).astype(BF16)
    line = lax.broadcasted_iota(I32, (16, rows), 1).astype(BF16)
    sorted_rows = lax.dot_general(line, taken, NT, preferred_element_type=F32)
    draft[order : order + 1, 0:rows] = sorted_rows[0:1].astype(I32)
    draft[reads : reads + 1, 0:rows] = seen
    touched = jnp.sum(jnp.minimum(seen, 1).astype(F32), axis=1, keepdims=True)
    draft[reads + 1 : reads + 2, 0:rows] = jnp.broadcast_to(touched, (1, rows)).astype(I32)


def prep_kernel(
    where, columns, tiles, turned, inverse, plan, wanted,
    landing, named, draft, arrived, here, done,
):
    rows, slots, size, _ = tiles.shape
    chunks = rows // CHUNK

    def copy_in(i):
        part = pl.ds(i * CHUNK, CHUNK)
        return pltpu.make_async_copy(tiles.at[part], landing.at[part], arrived.at[i])

    copy_columns = pltpu.make_async_copy(columns, named, here)
    copy_columns.start()
    for i in range(chunks):
        copy_in(i).start()
    copy_plan = pltpu.make_async_copy(draft, plan, done)

    def step(i, carry):
        copy_in(i).wait()
        for u in range(CHUNK):
            r = i * CHUNK + u
            total = None
            for s in range(slots):
                tile = landing[r, s].T
                turned[r, pl.ds(s * size, size), :] = tile
                tile = tile.astype(F32)
                total = tile if total is None else total + tile
            inverse[pl.ds(r, 1), :] = 1.0 / jnp.sum(total, axis=0, keepdims=True)
        return carry

    lax.fori_loop(0, chunks // 2, step, 0)
    copy_columns.wait()
    draft_plan(where[0], where[1], named[...], draft, wanted)
    copy_plan.start()
    lax.fori_loop(chunks // 2, chunks, step, 0)
    copy_plan.wait()


def prep(where, columns, tiles):
    rows, slots, size, _ = tiles.shape
    height = plan_height(slots)
    return pl.pallas_call(
        prep_kernel,
        out_shape=(
            pltpu.VMEM((rows, slots * size, size), BF16),
            pltpu.VMEM((rows, size), F32),
            pltpu.SMEM((height, 128), I32),
            pltpu.VMEM((8, 128), I32),
        ),
        in_specs=[SM, HB, HB],
        out_specs=(VM, VM, SM, VM),
        scratch_shapes=[
            pltpu.VMEM(tiles.shape, BF16),
            pltpu.VMEM(columns.shape, I32),
            pltpu.VMEM((height, 128), I32),
            pltpu.SemaphoreType.DMA((rows // CHUNK,)),
            pltpu.SemaphoreType.DMA,
            pltpu.SemaphoreType.DMA,
        ],
        compiler_params=params(14),
        cost_estimate=cost(2 * tiles.size * 16, 4 * tiles.size),
        name="prep",
    )(where, in_hbm(columns), in_hbm(tiles))


def fill(window, start, panel, tile_major):
    size = window.shape[2]
    if tile_major:
        window[start : start + panel.shape[0]] = panel[...]
    else:
        for t in range(panel.shape[1] // size):
            window[start + t] = panel[:, t * size : (t + 1) * size]


def thirds(x):
    high = x.astype(BF16)
    rest = x - high.astype(F32)
    middle = rest.astype(BF16)
    low = (rest - middle.astype(F32)).astype(BF16)
    return high, middle, low


def fold(squares, vectors):
    total = None
    for a, b in ((1, 1), (0, 1), (1, 0), (0, 0)):
        part = squares[a * vectors : (a + 1) * vectors, b * vectors : (b + 1) * vectors]
        total = part if total is None else total + part
    return total


def store(image, squares, picked, results, mine):
    if squares is None:
        for r, y in zip(picked, results):
            image[r] = y.astype(BF16)
        return None
    counted = []
    for r, y, keep in zip(picked, results, mine):
        stacked = jnp.concatenate(thirds(y)[:2], axis=0)
        image[r] = stacked
        counted.append(jnp.where(keep, stacked, jnp.zeros_like(stacked)))
    wide = jnp.concatenate(counted, axis=1)
    return squares + lax.dot_general(wide, wide, NT, preferred_element_type=F32)


def near_kernel(tile_major, last, count, plan, turned, inverse, own, *refs):
    mate, (image, sums, *refs) = refs[:count], refs[count:]
    rows, depth, size = turned.shape
    slots = depth // size
    reads = lines(slots)[-1]
    window = refs[-1]
    fill(window, 0, own, tile_major)
    start = rows
    for panel in mate:
        fill(window, start, panel, tile_major)
        start += panel.shape[0]
    window[2 * rows] = jnp.zeros(window.shape[1:], BF16)

    def step(block, squares):
        picked = [block * BLOCK + u for u in range(BLOCK)]
        vectors = [
            jnp.concatenate([window[plan[s, r]] for s in range(slots)], axis=1)
            for r in picked
        ]
        products = [
            lax.dot_general(x, turned[r], NN, preferred_element_type=F32)
            for x, r in zip(vectors, picked)
        ]
        results = [y * inverse[pl.ds(r, 1), :] for r, y in zip(picked, products)]
        for r, y in zip(picked, results):
            sums[r] = y
        mine = [plan[reads, r] == 0 for r in picked]
        return store(image, squares, picked, results, mine)

    begin = jnp.zeros(refs[0].shape, F32) if last else None
    total = lax.fori_loop(0, rows // BLOCK, step, begin)
    if last:
        refs[0][...] = total


def far_part(base, plan, turned, inverse, sums, panel, image, squares):
    rows, depth, size = turned.shape
    slots = depth // size
    slot, order, reads = lines(slots)[2:]
    panel[rows] = jnp.zeros(panel.shape[1:], BF16)

    def rows_of(start, many, count):
        picked = [plan[order, start + u] for u in range(many)]
        products = []
        for r in picked:
            x = [panel[plan[base + j, r]] for j in range(count)]
            w = [
                turned[r, pl.ds(pl.multiple_of(plan[slot + j, r] * size, size), size), :]
                for j in range(count)
            ]
            products.append(
                lax.dot_general(
                    jnp.concatenate(x, axis=1),
                    jnp.concatenate(w, axis=0),
                    NN,
                    preferred_element_type=F32,
                )
            )
        return picked, [
            sums[r] + y * inverse[pl.ds(r, 1), :] for r, y in zip(picked, products)
        ]

    touched = plan[reads + 1, 0]
    end = rows
    while end > 0:
        many = min(BLOCK if end == rows else 2 * BLOCK, end)
        most = plan[reads, plan[order, end - 1]]
        for count in range(1, slots):

            @pl.when((touched > rows - end) & (most == count))
            def _(start=end - many, many=many, count=count):
                picked, results = rows_of(start, many, count)
                mine = [plan[reads, r] > 0 for r in picked]
                if squares is None:
                    store(image, None, picked, results, mine)
                else:
                    squares[...] = store(image, squares[...], picked, results, mine)

        end -= many


def pack(image, sending, send):
    for k in range(send.shape[0]):
        send[k] = image[sending[0, k]]


def halve(image, halves):
    half = halves[0].shape[0]
    for i, part in enumerate(halves):
        part[...] = image[i * half : (i + 1) * half]


def far_first_kernel(
    asked, plan, turned, inverse, other, sums, i_in, image, left, right, send, sending, panel, done
):
    rows, depth, size = turned.shape
    copy = pltpu.make_async_copy(asked, sending, done)
    copy.start()
    fill(panel, 0, other, False)
    base = lines(depth // size)[0]
    far_part(base, plan, turned, inverse, sums, panel, image, None)
    copy.wait()
    pack(image, sending, send)
    halve(image, (left, right))


def far_kernel(sending, plan, turned, inverse, other, sums, i_in, image, left, right, send, panel):
    rows, depth, size = turned.shape
    fill(panel, 0, other, True)
    base = lines(depth // size)[1]
    far_part(base, plan, turned, inverse, sums, panel, image, None)
    pack(image, sending, send)
    halve(image, (left, right))


def far_whole_kernel(
    tile_major, plan, turned, inverse, other, sums, i_in, image, left, right, panel
):
    rows, depth, size = turned.shape
    fill(panel, 0, other, tile_major)
    base = lines(depth // size)[0]
    far_part(base, plan, turned, inverse, sums, panel, image, None)
    halve(image, (left, right))


def far_last_kernel(
    whole, sending, plan, turned, inverse, other, near, sums, i_in, image, gram, panel, squares
):
    rows, depth, size = turned.shape
    slots = depth // size
    vectors = gram.shape[1]
    fill(panel, 0, other, True)
    squares[...] = near[...]
    base = lines(slots)[0 if whole else 1]
    far_part(base, plan, turned, inverse, sums, panel, image, squares)
    gram[0:vectors] = fold(squares[...], vectors)
    read = plan[lines(slots)[-1] + 2, 0]
    short = jnp.maximum(read, sending[1, 0]) > other.shape[0]
    gram[vectors:] = jnp.zeros((8, vectors), F32) + jnp.where(short, 1.0, 0.0)


def near_rows(plan, turned, inverse, own, mate, tile_major, last):
    rows, depth, size = turned.shape
    vectors = own.shape[1 if tile_major else 0]
    height = 2 * vectors if last else vectors
    shapes = (
        pltpu.VMEM((rows, height, size), BF16),
        pltpu.VMEM((rows, vectors, size), F32),
    )
    if last:
        shapes += (pltpu.VMEM((height, height), F32),)
    return pl.pallas_call(
        functools.partial(near_kernel, tile_major, last, len(mate)),
        out_shape=shapes,
        in_specs=[SM, VM, VM, VM] + [VM] * len(mate),
        out_specs=(VM,) * len(shapes),
        scratch_shapes=[pltpu.VMEM((2 * rows + 1, vectors, size), BF16)],
        compiler_params=params(4),
        cost_estimate=cost(0, 1024),
        name="near_rows",
    )(plan, *map(in_vmem, (turned, inverse, own, *mate)))


def far_call(kernel, ins, in_specs, outs, out_specs, turned, vectors, scratch=()):
    rows, depth, size = turned.shape
    return pl.pallas_call(
        kernel,
        out_shape=outs,
        in_specs=in_specs,
        out_specs=out_specs,
        scratch_shapes=[pltpu.VMEM((rows + 1, vectors, size), BF16), *scratch],
        input_output_aliases={len(ins) - 1: 0},
        compiler_params=params(4),
        cost_estimate=cost(20 * rows * depth * size, rows * depth * size),
        name="far_rows",
    )(*ins)


def of(array):
    return pltpu.VMEM(array.shape, array.dtype)


def halves_of(image):
    rows, vectors, size = image.shape
    return (pltpu.VMEM((rows // 2, vectors, size), BF16),) * 2


def far_rows_first(limit, asked, plan, turned, inverse, other, sums, image):
    rows, vectors, size = image.shape
    return far_call(
        far_first_kernel,
        (in_vmem(asked), plan, *map(in_vmem, (turned, inverse, other, sums, image))),
        [VM, SM] + [VM] * 5,
        (
            of(image),
            *halves_of(image),
            pltpu.VMEM((limit, vectors, size), BF16),
            pltpu.SMEM((8, 128), I32),
        ),
        (VM, VM, VM, VM, SM),
        turned,
        vectors,
        [pltpu.SemaphoreType.DMA],
    )


def far_rows(plan, turned, inverse, sending, other, sums, image):
    return far_call(
        far_kernel,
        (sending, plan, *map(in_vmem, (turned, inverse, other, sums, image))),
        [SM, SM] + [VM] * 5,
        (of(image), *halves_of(image), of(other)),
        (VM,) * 4,
        turned,
        image.shape[1],
    )


def far_rows_whole(plan, turned, inverse, other, sums, image, tile_major):
    return far_call(
        functools.partial(far_whole_kernel, tile_major),
        (plan, *map(in_vmem, (turned, inverse, other, sums, image))),
        [SM] + [VM] * 5,
        (of(image), *halves_of(image)),
        (VM,) * 3,
        turned,
        image.shape[1],
    )


def far_rows_last(whole, plan, turned, inverse, sending, other, near, sums, image):
    vectors = near.shape[0] // 2
    return far_call(
        functools.partial(far_last_kernel, whole),
        (sending, plan, *map(in_vmem, (turned, inverse, other, near, sums, image))),
        [SM, SM] + [VM] * 6,
        (of(image), pltpu.VMEM((vectors + 8, vectors), F32)),
        (VM,) * 2,
        turned,
        vectors,
        [pltpu.VMEM(near.shape, F32)],
    )


def inverse_factor(gram):
    count = gram.shape[0]
    step = 8
    row = lax.broadcasted_iota(I32, (count, count), 0)
    column = lax.broadcasted_iota(I32, (count, count), 1)
    work = jnp.concatenate([gram, jnp.where(row == column, 1.0, 0.0)], axis=1)
    below = lax.broadcasted_iota(I32, work.shape, 0)
    for begin in range(0, count, step):
        spread = [
            jnp.broadcast_to(work[:, k : k + 1], work.shape)
            for k in range(begin, begin + step)
        ]
        for j in range(step):
            k = begin + j
            factor = jnp.where(below > k, spread[j], 0.0)
            pivot = 1.0 / spread[j][k : k + 1]
            for q in range(j + 1, step):
                spread[q] = spread[q] - factor * (spread[q][k : k + 1] * pivot)
            work = work - factor * (work[k : k + 1] * pivot)
    pivots = jnp.sum(
        jnp.where(row == column, work[:, :count], 0.0), axis=1, keepdims=True
    )
    return work[:, count:] * lax.rsqrt(pivots)


def final_kernel(states, gram_a, gram_b, mapping, parts, out, short, ready, sent):
    rows, depth, size = parts.shape
    vectors = depth // 2
    total = gram_a[...] + gram_b[...]
    short[0] = jnp.max(total[vectors:]).astype(I32)
    factor = inverse_factor(total[:vectors] / states)
    combined = lax.dot_general(
        mapping[...],
        factor,
        (((0,), (0,)), ((), ())),
        precision=lax.Precision.HIGHEST,
        preferred_element_type=F32,
    )
    high, middle, low = thirds(combined)
    blank = jnp.zeros_like(high)
    left = jnp.concatenate(
        [
            jnp.concatenate([high, high], axis=1),
            jnp.concatenate([middle, middle], axis=1),
            jnp.concatenate([low, blank], axis=1),
        ],
        axis=0,
    )
    copies = []
    for g in range(rows // CHUNK):
        for r in range(g * CHUNK, (g + 1) * CHUNK):
            y = lax.dot_general(left, parts[r], NN, preferred_element_type=F32)
            ready[:, r * size : (r + 1) * size] = (
                y[2 * vectors :] + y[vectors : 2 * vectors]
            ) + y[:vectors]
        part = pl.ds(g * CHUNK * size, CHUNK * size)
        copies.append(pltpu.make_async_copy(ready.at[:, part], out.at[:, part], sent.at[g]))
        copies[-1].start()
    for copy in copies:
        copy.wait()


def final(states, gram_a, gram_b, mapping, parts):
    rows, depth, size = parts.shape
    vectors = depth // 2
    return pl.pallas_call(
        functools.partial(final_kernel, float(states)),
        out_shape=(
            jax.ShapeDtypeStruct((vectors, rows * size), F32),
            pltpu.SMEM((1,), I32),
        ),
        in_specs=[VM, VM, VM, VM],
        out_specs=(HB, SM),
        scratch_shapes=[
            pltpu.VMEM((vectors, rows * size), F32),
            pltpu.SemaphoreType.DMA((rows // CHUNK,)),
        ],
        compiler_params=params(8),
        cost_estimate=cost(6 * parts.size * vectors, 4 * parts.size),
        name="memberships",
    )(gram_a, gram_b, mapping, in_vmem(parts))


def memberships(whole, transition_tiles, column_tiles, schur_basis, membership_map):
    rows = transition_tiles.shape[0]
    count = lax.axis_size("rows")
    me = lax.axis_index("rows")
    mates = [(i, i ^ 1) for i in range(count)]
    others = []
    for i in range(1, count - 1, 2):
        others += [(i, i + 1), (i + 1, i)]

    def swap(array, pairs):
        return lax.ppermute(array, "rows", pairs)

    limit = 11 * rows // 16
    where = jnp.stack([me * rows, me % 2]).astype(I32)
    columns = column_tiles.T
    mate, other = swap(schur_basis, mates), swap(schur_basis, others)
    turned, inverse, plan, wanted = prep(where, columns, transition_tiles)
    asked = swap(wanted, others)
    image, sums = near_rows(plan, turned, inverse, schur_basis, (mate,), False, False)
    if whole:
        image, *halves = far_rows_whole(plan, turned, inverse, other, sums, image, False)
        send, sending = image, asked
    else:
        image, *halves, send, sending = far_rows_first(
            limit, asked, plan, turned, inverse, other, sums, image
        )
    for step in range(1, PRODUCTS):
        last = step == PRODUCTS - 1
        other = swap(send, others)
        mate = [swap(half, mates) for half in halves]
        image, sums, *near = near_rows(plan, turned, inverse, image, mate, True, last)
        if last:
            parts, gram = far_rows_last(
                whole, plan, turned, inverse, sending, other, near[0], sums, image
            )
        elif whole:
            image, *halves = far_rows_whole(plan, turned, inverse, other, sums, image, True)
            send = image
        else:
            image, *halves, send = far_rows(plan, turned, inverse, sending, other, sums, image)
    distance = 1
    while distance < count:
        partner = swap(gram, [(i, i ^ distance) for i in range(count)])
        distance *= 2
        if distance < count:
            gram = gram + partner
    states = schur_basis.shape[1] * count
    return final(states, gram, partner, membership_map, parts)


def body(transition_tiles, column_tiles, schur_basis, membership_map):
    arguments = transition_tiles, column_tiles, schur_basis, membership_map
    out, short = memberships(False, *arguments)
    return lax.cond(
        short[0] > 0,
        lambda *given: memberships(True, *given[:4])[0],
        lambda *given: given[4],
        *arguments,
        out,
    )


def solution(mesh):
    return jax.shard_map(
        body,
        mesh=mesh,
        in_specs=(
            P(("groups", "rows"), None, None, None),
            P(("groups", "rows"), None),
            P(None, ("groups", "rows")),
            P("groups", None),
        ),
        out_specs=P(None, ("groups", "rows")),
        check_vma=False,
    )
```

```python
import functools

import jax
import jax.numpy as jnp
from jax import lax
from jax.experimental import pallas as pl
from jax.experimental.pallas import tpu as pltpu
from jax.sharding import PartitionSpec as P

PRODUCTS = 4
BLOCK = 16
CHUNK = 8
F32 = jnp.float32
BF16 = jnp.bfloat16
I32 = jnp.int32
NN = (((1,), (0,)), ((), ()))
NT = (((1,), (1,)), ((), ()))
VM = pl.BlockSpec(memory_space=pltpu.VMEM)
SM = pl.BlockSpec(memory_space=pltpu.SMEM)
HB = pl.BlockSpec(memory_space=pltpu.HBM)


def in_vmem(array):
    return pltpu.with_memory_space_constraint(array, pltpu.VMEM)


def in_hbm(array):
    return pltpu.with_memory_space_constraint(array, pltpu.HBM)


def cost(flops, moved):
    return pl.CostEstimate(flops=flops, bytes_accessed=moved, transcendentals=0)


def params(mib):
    return pltpu.CompilerParams(vmem_limit_bytes=mib * 2**20)


def ranks(named):
    rows = named.shape[0]
    h = lax.broadcasted_iota(I32, (rows, rows), 0)
    other = lax.broadcasted_iota(I32, (rows, rows), 1)
    before = jnp.where(other < h, 1.0, 0.0).astype(BF16)
    ones = jnp.ones((rows, rows), BF16)
    total = lax.dot_general(named.astype(BF16), ones, NN, preferred_element_type=F32)
    mark = jnp.where(total > 0.5, 1.0, 0.0)
    rank = lax.dot_general(before, mark.astype(BF16), NN, preferred_element_type=F32)
    return mark, rank


def lines(slots):
    far = slots - 1
    return slots, slots + far, slots + 2 * far, slots + 3 * far, slots + 3 * far + 1


def plan_height(slots):
    return (lines(slots)[-1] + 3 + 7) // 8 * 8


def draft_plan(first, parity, columns, draft, wanted):
    slots, rows = columns.shape
    panel, counted, slot, order, reads = lines(slots)
    low = jnp.where(parity == 0, 2 * rows, rows)
    high = jnp.where(parity == 0, rows, 2 * rows)
    offset = columns - first
    spot = jnp.where(
        offset < 0,
        offset + (rows + low),
        jnp.where(offset >= rows, offset + (high - rows), offset),
    )
    draft[0:slots, 0:rows] = jnp.minimum(spot, 2 * rows)
    h = lax.broadcasted_iota(I32, (rows, rows), 0)
    lane = lax.broadcasted_iota(I32, (rows, rows), 1)
    ones = jnp.ones((rows, rows), BF16)
    equal = [
        jnp.where(spot[s : s + 1] - 2 * rows == h, 1.0, 0.0) for s in range(slots)
    ]
    mark, rank = ranks(functools.reduce(jnp.add, equal))
    here = jnp.where((mark > 0.5) & (rank.astype(I32) == lane), h, 0)
    wanted[0:1, 0:rows] = jnp.sum(here.astype(F32), axis=0, keepdims=True).astype(I32)
    read = jnp.sum(mark, axis=0, keepdims=True).astype(I32)
    wanted[1:2, 0:rows] = read
    draft[reads + 2 : reads + 3, 0:rows] = read
    none = jnp.zeros((1, rows), I32)
    seen = none
    tiles, places, named = [[none + start] * (slots - 1) for start in (rows, rows, 0)]
    for s in range(slots):
        place = jnp.sum(equal[s] * rank, axis=0, keepdims=True).astype(I32)
        tile = spot[s : s + 1] - 2 * rows
        far = jnp.where(tile >= 0, 1, 0)
        for j in range(min(s + 1, slots - 1)):
            hit = (far == 1) & (seen == j)
            tiles[j] = jnp.where(hit, tile, tiles[j])
            places[j] = jnp.where(hit, place, places[j])
            named[j] = jnp.where(hit, s, named[j])
        seen = seen + far
    for j in range(slots - 1):
        draft[panel + j : panel + j + 1, 0:rows] = tiles[j]
        draft[counted + j : counted + j + 1, 0:rows] = places[j]
        draft[slot + j : slot + j + 1, 0:rows] = named[j]
    along = jnp.broadcast_to(seen.astype(F32), (rows, rows))
    down = lax.dot_general(
        jnp.where(h == lane, along, 0.0).astype(BF16), ones, NN, preferred_element_type=F32
    )
    ahead = jnp.where((down < along) | ((down == along) & (h < lane)), 1.0, 0.0)
    position = jnp.sum(ahead, axis=0, keepdims=True).astype(I32)
    taken = jnp.where(position == h, 1.0, 0.0).astype(BF16)
    line = lax.broadcasted_iota(I32, (16, rows), 1).astype(BF16)
    sorted_rows = lax.dot_general(line, taken, NT, preferred_element_type=F32)
    draft[order : order + 1, 0:rows] = sorted_rows[0:1].astype(I32)
    draft[reads : reads + 1, 0:rows] = seen
    touched = jnp.sum(jnp.minimum(seen, 1).astype(F32), axis=1, keepdims=True)
    draft[reads + 1 : reads + 2, 0:rows] = jnp.broadcast_to(touched, (1, rows)).astype(I32)


def prep_kernel(
    where, columns, tiles, turned, inverse, plan, wanted,
    landing, named, draft, arrived, here, done,
):
    rows, slots, size, _ = tiles.shape
    chunks = rows // CHUNK

    def copy_in(i):
        part = pl.ds(i * CHUNK, CHUNK)
        return pltpu.make_async_copy(tiles.at[part], landing.at[part], arrived.at[i])

    copy_columns = pltpu.make_async_copy(columns, named, here)
    copy_columns.start()
    for i in range(chunks):
        copy_in(i).start()
    copy_plan = pltpu.make_async_copy(draft, plan, done)

    def step(i, carry):
        copy_in(i).wait()
        for u in range(CHUNK):
            r = i * CHUNK + u
            total = None
            for s in range(slots):
                tile = landing[r, s].T
                turned[r, pl.ds(s * size, size), :] = tile
                tile = tile.astype(F32)
                total = tile if total is None else total + tile
            total = jnp.sum(total, axis=0, keepdims=True)
            inverse[r] = jnp.broadcast_to(1.0 / total, inverse.shape[1:])
        return carry

    lax.fori_loop(0, chunks // 2, step, 0)
    copy_columns.wait()
    draft_plan(where[0], where[1], named[...], draft, wanted)
    copy_plan.start()
    lax.fori_loop(chunks // 2, chunks, step, 0)
    copy_plan.wait()


def prep(where, columns, tiles):
    rows, slots, size, _ = tiles.shape
    height = plan_height(slots)
    return pl.pallas_call(
        prep_kernel,
        out_shape=(
            pltpu.VMEM((rows, slots * size, size), BF16),
            pltpu.VMEM((rows, 8, size), F32),
            pltpu.SMEM((height, 128), I32),
            pltpu.VMEM((8, 128), I32),
        ),
        in_specs=[SM, HB, HB],
        out_specs=(VM, VM, SM, VM),
        scratch_shapes=[
            pltpu.VMEM(tiles.shape, BF16),
            pltpu.VMEM(columns.shape, I32),
            pltpu.VMEM((height, 128), I32),
            pltpu.SemaphoreType.DMA((rows // CHUNK,)),
            pltpu.SemaphoreType.DMA,
            pltpu.SemaphoreType.DMA,
        ],
        compiler_params=params(14),
        cost_estimate=cost(2 * tiles.size * 16, 4 * tiles.size),
        name="prep",
    )(where, in_hbm(columns), in_hbm(tiles))


def fill(window, start, panel, tile_major):
    size = window.shape[2]
    if tile_major:
        window[start : start + panel.shape[0]] = panel[...]
    else:
        for t in range(panel.shape[1] // size):
            window[start + t] = panel[:, t * size : (t + 1) * size]


def thirds(x):
    high = x.astype(BF16)
    rest = x - high.astype(F32)
    middle = rest.astype(BF16)
    low = (rest - middle.astype(F32)).astype(BF16)
    return high, middle, low


def fold(squares, vectors):
    total = None
    for a, b in ((1, 1), (0, 1), (1, 0), (0, 0)):
        part = squares[a * vectors : (a + 1) * vectors, b * vectors : (b + 1) * vectors]
        total = part if total is None else total + part
    return total


def scaled(y, factor):
    return (y.reshape(-1, *factor.shape) * factor[None]).reshape(y.shape)


def store(image, squares, picked, results, mine):
    if squares is None:
        for r, y in zip(picked, results):
            image[r] = y.astype(BF16)
        return None
    counted = []
    for r, y, keep in zip(picked, results, mine):
        stacked = jnp.concatenate(thirds(y)[:2], axis=0)
        image[r] = stacked
        counted.append(jnp.where(keep, stacked, jnp.zeros_like(stacked)))
    wide = jnp.concatenate(counted, axis=1)
    return squares + lax.dot_general(wide, wide, NT, preferred_element_type=F32)


def near_kernel(tile_major, last, count, plan, turned, inverse, own, *refs):
    mate, (image, sums, *refs) = refs[:count], refs[count:]
    rows, depth, size = turned.shape
    slots = depth // size
    reads = lines(slots)[-1]
    window = refs[-1]
    fill(window, 0, own, tile_major)
    start = rows
    for panel in mate:
        fill(window, start, panel, tile_major)
        start += panel.shape[0]
    window[2 * rows] = jnp.zeros(window.shape[1:], BF16)

    def step(block, squares):
        picked = [block * BLOCK + u for u in range(BLOCK)]
        vectors = [
            jnp.concatenate([window[plan[s, r]] for s in range(slots)], axis=1)
            for r in picked
        ]
        products = [
            lax.dot_general(x, turned[r], NN, preferred_element_type=F32)
            for x, r in zip(vectors, picked)
        ]
        results = [scaled(y, inverse[r]) for r, y in zip(picked, products)]
        for r, y in zip(picked, results):
            sums[r] = y
        mine = [plan[reads, r] == 0 for r in picked]
        return store(image, squares, picked, results, mine)

    begin = jnp.zeros(refs[0].shape, F32) if last else None
    total = lax.fori_loop(0, rows // BLOCK, step, begin)
    if last:
        refs[0][...] = total


def far_part(base, plan, turned, inverse, sums, panel, image, squares):
    rows, depth, size = turned.shape
    slots = depth // size
    slot, order, reads = lines(slots)[2:]
    panel[rows] = jnp.zeros(panel.shape[1:], BF16)

    def rows_of(start, count):
        picked = [plan[order, start + u] for u in range(BLOCK)]
        products = []
        for r in picked:
            x = [panel[plan[base + j, r]] for j in range(count)]
            w = [
                turned[r, pl.ds(pl.multiple_of(plan[slot + j, r] * size, size), size), :]
                for j in range(count)
            ]
            products.append(
                lax.dot_general(
                    jnp.concatenate(x, axis=1),
                    jnp.concatenate(w, axis=0),
                    NN,
                    preferred_element_type=F32,
                )
            )
        return picked, [
            sums[r] + scaled(y, inverse[r]) for r, y in zip(picked, products)
        ]

    def step(block, carry):
        start = rows - (block + 1) * BLOCK
        most = plan[reads, plan[order, start + BLOCK - 1]]
        for count in range(1, slots):

            @pl.when(most == count)
            def _():
                picked, results = rows_of(start, count)
                mine = [plan[reads, r] > 0 for r in picked]
                if squares is None:
                    store(image, None, picked, results, mine)
                else:
                    squares[...] = store(image, squares[...], picked, results, mine)

        return carry

    touched = plan[reads + 1, 0]
    lax.fori_loop(0, (touched + BLOCK - 1) // BLOCK, step, 0)


def pack(image, sending, send):
    for k in range(send.shape[0]):
        send[k] = image[sending[0, k]]


def halve(image, halves):
    half = halves[0].shape[0]
    for i, part in enumerate(halves):
        part[...] = image[i * half : (i + 1) * half]


def far_first_kernel(
    asked, plan, turned, inverse, other, sums, i_in, image, left, right, send, sending, panel, done
):
    rows, depth, size = turned.shape
    copy = pltpu.make_async_copy(asked, sending, done)
    copy.start()
    fill(panel, 0, other, False)
    base = lines(depth // size)[0]
    far_part(base, plan, turned, inverse, sums, panel, image, None)
    copy.wait()
    pack(image, sending, send)
    halve(image, (left, right))


def far_kernel(sending, plan, turned, inverse, other, sums, i_in, image, left, right, send, panel):
    rows, depth, size = turned.shape
    fill(panel, 0, other, True)
    base = lines(depth // size)[1]
    far_part(base, plan, turned, inverse, sums, panel, image, None)
    pack(image, sending, send)
    halve(image, (left, right))


def far_whole_kernel(
    tile_major, plan, turned, inverse, other, sums, i_in, image, left, right, panel
):
    rows, depth, size = turned.shape
    fill(panel, 0, other, tile_major)
    base = lines(depth // size)[0]
    far_part(base, plan, turned, inverse, sums, panel, image, None)
    halve(image, (left, right))


def far_last_kernel(
    whole, sending, plan, turned, inverse, other, near, sums, i_in, image, gram, panel, squares
):
    rows, depth, size = turned.shape
    slots = depth // size
    vectors = gram.shape[1]
    fill(panel, 0, other, True)
    squares[...] = near[...]
    base = lines(slots)[0 if whole else 1]
    far_part(base, plan, turned, inverse, sums, panel, image, squares)
    gram[0:vectors] = fold(squares[...], vectors)
    read = plan[lines(slots)[-1] + 2, 0]
    short = jnp.maximum(read, sending[1, 0]) > other.shape[0]
    gram[vectors:] = jnp.zeros((8, vectors), F32) + jnp.where(short, 1.0, 0.0)


def near_rows(plan, turned, inverse, own, mate, tile_major, last):
    rows, depth, size = turned.shape
    vectors = own.shape[1 if tile_major else 0]
    height = 2 * vectors if last else vectors
    shapes = (
        pltpu.VMEM((rows, height, size), BF16),
        pltpu.VMEM((rows, vectors, size), F32),
    )
    if last:
        shapes += (pltpu.VMEM((height, height), F32),)
    return pl.pallas_call(
        functools.partial(near_kernel, tile_major, last, len(mate)),
        out_shape=shapes,
        in_specs=[SM, VM, VM, VM] + [VM] * len(mate),
        out_specs=(VM,) * len(shapes),
        scratch_shapes=[pltpu.VMEM((2 * rows + 1, vectors, size), BF16)],
        compiler_params=params(4),
        cost_estimate=cost(0, 1024),
        name="near_rows",
    )(plan, *map(in_vmem, (turned, inverse, own, *mate)))


def far_call(kernel, ins, in_specs, outs, out_specs, turned, vectors, scratch=()):
    rows, depth, size = turned.shape
    return pl.pallas_call(
        kernel,
        out_shape=outs,
        in_specs=in_specs,
        out_specs=out_specs,
        scratch_shapes=[pltpu.VMEM((rows + 1, vectors, size), BF16), *scratch],
        input_output_aliases={len(ins) - 1: 0},
        compiler_params=params(4),
        cost_estimate=cost(20 * rows * depth * size, rows * depth * size),
        name="far_rows",
    )(*ins)


def of(array):
    return pltpu.VMEM(array.shape, array.dtype)


def halves_of(image):
    rows, vectors, size = image.shape
    return (pltpu.VMEM((rows // 2, vectors, size), BF16),) * 2


def far_rows_first(limit, asked, plan, turned, inverse, other, sums, image):
    rows, vectors, size = image.shape
    return far_call(
        far_first_kernel,
        (in_vmem(asked), plan, *map(in_vmem, (turned, inverse, other, sums, image))),
        [VM, SM] + [VM] * 5,
        (
            of(image),
            *halves_of(image),
            pltpu.VMEM((limit, vectors, size), BF16),
            pltpu.SMEM((8, 128), I32),
        ),
        (VM, VM, VM, VM, SM),
        turned,
        vectors,
        [pltpu.SemaphoreType.DMA],
    )


def far_rows(plan, turned, inverse, sending, other, sums, image):
    return far_call(
        far_kernel,
        (sending, plan, *map(in_vmem, (turned, inverse, other, sums, image))),
        [SM, SM] + [VM] * 5,
        (of(image), *halves_of(image), of(other)),
        (VM,) * 4,
        turned,
        image.shape[1],
    )


def far_rows_whole(plan, turned, inverse, other, sums, image, tile_major):
    return far_call(
        functools.partial(far_whole_kernel, tile_major),
        (plan, *map(in_vmem, (turned, inverse, other, sums, image))),
        [SM] + [VM] * 5,
        (of(image), *halves_of(image)),
        (VM,) * 3,
        turned,
        image.shape[1],
    )


def far_rows_last(whole, plan, turned, inverse, sending, other, near, sums, image):
    vectors = near.shape[0] // 2
    return far_call(
        functools.partial(far_last_kernel, whole),
        (sending, plan, *map(in_vmem, (turned, inverse, other, near, sums, image))),
        [SM, SM] + [VM] * 6,
        (of(image), pltpu.VMEM((vectors + 8, vectors), F32)),
        (VM,) * 2,
        turned,
        vectors,
        [pltpu.VMEM(near.shape, F32)],
    )


def inverse_factor(gram):
    count = gram.shape[0]
    step = 8
    row = lax.broadcasted_iota(I32, (count, count), 0)
    column = lax.broadcasted_iota(I32, (count, count), 1)
    work = jnp.concatenate([gram, jnp.where(row == column, 1.0, 0.0)], axis=1)
    below = lax.broadcasted_iota(I32, work.shape, 0)
    for begin in range(0, count, step):
        spread = [
            jnp.broadcast_to(work[:, k : k + 1], work.shape)
            for k in range(begin, begin + step)
        ]
        for j in range(step):
            k = begin + j
            factor = jnp.where(below > k, spread[j], 0.0)
            pivot = 1.0 / spread[j][k : k + 1]
            for q in range(j + 1, step):
                spread[q] = spread[q] - factor * (spread[q][k : k + 1] * pivot)
            work = work - factor * (work[k : k + 1] * pivot)
    pivots = jnp.sum(
        jnp.where(row == column, work[:, :count], 0.0), axis=1, keepdims=True
    )
    return work[:, count:] * lax.rsqrt(pivots)


def final_kernel(states, gram_a, gram_b, mapping, parts, out, short, ready, sent):
    rows, depth, size = parts.shape
    vectors = depth // 2
    total = gram_a[...] + gram_b[...]
    short[0] = jnp.max(total[vectors:]).astype(I32)
    factor = inverse_factor(total[:vectors] / states)
    combined = lax.dot_general(
        mapping[...],
        factor,
        (((0,), (0,)), ((), ())),
        precision=lax.Precision.HIGHEST,
        preferred_element_type=F32,
    )
    high, middle, low = thirds(combined)
    blank = jnp.zeros_like(high)
    left = jnp.concatenate(
        [
            jnp.concatenate([high, high], axis=1),
            jnp.concatenate([middle, middle], axis=1),
            jnp.concatenate([low, blank], axis=1),
        ],
        axis=0,
    )
    copies = []
    for g in range(rows // CHUNK):
        for r in range(g * CHUNK, (g + 1) * CHUNK):
            y = lax.dot_general(left, parts[r], NN, preferred_element_type=F32)
            ready[:, r * size : (r + 1) * size] = (
                y[2 * vectors :] + y[vectors : 2 * vectors]
            ) + y[:vectors]
        part = pl.ds(g * CHUNK * size, CHUNK * size)
        copies.append(pltpu.make_async_copy(ready.at[:, part], out.at[:, part], sent.at[g]))
        copies[-1].start()
    for copy in copies:
        copy.wait()


def final(states, gram_a, gram_b, mapping, parts):
    rows, depth, size = parts.shape
    vectors = depth // 2
    return pl.pallas_call(
        functools.partial(final_kernel, float(states)),
        out_shape=(
            jax.ShapeDtypeStruct((vectors, rows * size), F32),
            pltpu.SMEM((1,), I32),
        ),
        in_specs=[VM, VM, VM, VM],
        out_specs=(HB, SM),
        scratch_shapes=[
            pltpu.VMEM((vectors, rows * size), F32),
            pltpu.SemaphoreType.DMA((rows // CHUNK,)),
        ],
        compiler_params=params(8),
        cost_estimate=cost(6 * parts.size * vectors, 4 * parts.size),
        name="memberships",
    )(gram_a, gram_b, mapping, in_vmem(parts))


def memberships(whole, transition_tiles, column_tiles, schur_basis, membership_map):
    rows = transition_tiles.shape[0]
    count = lax.axis_size("rows")
    me = lax.axis_index("rows")
    mates = [(i, i ^ 1) for i in range(count)]
    others = []
    for i in range(1, count - 1, 2):
        others += [(i, i + 1), (i + 1, i)]

    def swap(array, pairs):
        return lax.ppermute(array, "rows", pairs)

    limit = 11 * rows // 16
    where = jnp.stack([me * rows, me % 2]).astype(I32)
    columns = column_tiles.T
    mate, other = swap(schur_basis, mates), swap(schur_basis, others)
    turned, inverse, plan, wanted = prep(where, columns, transition_tiles)
    asked = swap(wanted, others)
    image, sums = near_rows(plan, turned, inverse, schur_basis, (mate,), False, False)
    if whole:
        image, *halves = far_rows_whole(plan, turned, inverse, other, sums, image, False)
        send, sending = image, asked
    else:
        image, *halves, send, sending = far_rows_first(
            limit, asked, plan, turned, inverse, other, sums, image
        )
    for step in range(1, PRODUCTS):
        last = step == PRODUCTS - 1
        other = swap(send, others)
        mate = [swap(half, mates) for half in halves]
        image, sums, *near = near_rows(plan, turned, inverse, image, mate, True, last)
        if last:
            parts, gram = far_rows_last(
                whole, plan, turned, inverse, sending, other, near[0], sums, image
            )
        elif whole:
            image, *halves = far_rows_whole(plan, turned, inverse, other, sums, image, True)
            send = image
        else:
            image, *halves, send = far_rows(plan, turned, inverse, sending, other, sums, image)
    distance = 1
    while distance < count:
        partner = swap(gram, [(i, i ^ distance) for i in range(count)])
        distance *= 2
        if distance < count:
            gram = gram + partner
    states = schur_basis.shape[1] * count
    return final(states, gram, partner, membership_map, parts)


def body(transition_tiles, column_tiles, schur_basis, membership_map):
    arguments = transition_tiles, column_tiles, schur_basis, membership_map
    out, short = memberships(False, *arguments)
    return lax.cond(
        short[0] > 0,
        lambda *given: memberships(True, *given[:4])[0],
        lambda *given: given[4],
        *arguments,
        out,
    )


def solution(mesh):
    return jax.shard_map(
        body,
        mesh=mesh,
        in_specs=(
            P(("groups", "rows"), None, None, None),
            P(("groups", "rows"), None),
            P(None, ("groups", "rows")),
            P("groups", None),
        ),
        out_specs=P(None, ("groups", "rows")),
        check_vma=False,
    )
```

```python
import functools

import jax
import jax.numpy as jnp
from jax import lax
from jax.experimental import pallas as pl
from jax.experimental.pallas import tpu as pltpu
from jax.sharding import PartitionSpec as P

PRODUCTS = 4
BLOCK = 16
CHUNK = 8
F32 = jnp.float32
BF16 = jnp.bfloat16
I32 = jnp.int32
NN = (((1,), (0,)), ((), ()))
NT = (((1,), (1,)), ((), ()))
VM = pl.BlockSpec(memory_space=pltpu.VMEM)
SM = pl.BlockSpec(memory_space=pltpu.SMEM)
HB = pl.BlockSpec(memory_space=pltpu.HBM)


def in_vmem(array):
    return pltpu.with_memory_space_constraint(array, pltpu.VMEM)


def in_hbm(array):
    return pltpu.with_memory_space_constraint(array, pltpu.HBM)


def cost(flops, moved):
    return pl.CostEstimate(flops=flops, bytes_accessed=moved, transcendentals=0)


def params(mib):
    return pltpu.CompilerParams(vmem_limit_bytes=mib * 2**20)


def ranks(named):
    rows = named.shape[0]
    h = lax.broadcasted_iota(I32, (rows, rows), 0)
    other = lax.broadcasted_iota(I32, (rows, rows), 1)
    before = jnp.where(other < h, 1.0, 0.0).astype(BF16)
    ones = jnp.ones((rows, rows), BF16)
    total = lax.dot_general(named.astype(BF16), ones, NN, preferred_element_type=F32)
    mark = jnp.where(total > 0.5, 1.0, 0.0)
    rank = lax.dot_general(before, mark.astype(BF16), NN, preferred_element_type=F32)
    return mark, rank


def lines(slots):
    far = slots - 1
    return slots, slots + far, slots + 2 * far, slots + 3 * far, slots + 3 * far + 1


def plan_height(slots):
    return (lines(slots)[-1] + 3 + 7) // 8 * 8


def draft_plan(first, parity, columns, draft, wanted):
    slots, rows = columns.shape
    panel, counted, slot, order, reads = lines(slots)
    low = jnp.where(parity == 0, 2 * rows, rows)
    high = jnp.where(parity == 0, rows, 2 * rows)
    offset = columns - first
    spot = jnp.where(
        offset < 0,
        offset + (rows + low),
        jnp.where(offset >= rows, offset + (high - rows), offset),
    )
    draft[0:slots, 0:rows] = jnp.minimum(spot, 2 * rows)
    h = lax.broadcasted_iota(I32, (rows, rows), 0)
    lane = lax.broadcasted_iota(I32, (rows, rows), 1)
    ones = jnp.ones((rows, rows), BF16)
    equal = [
        jnp.where(spot[s : s + 1] - 2 * rows == h, 1.0, 0.0) for s in range(slots)
    ]
    mark, rank = ranks(functools.reduce(jnp.add, equal))
    here = jnp.where((mark > 0.5) & (rank.astype(I32) == lane), h, 0)
    wanted[0:1, 0:rows] = jnp.sum(here.astype(F32), axis=0, keepdims=True).astype(I32)
    read = jnp.sum(mark, axis=0, keepdims=True).astype(I32)
    wanted[1:2, 0:rows] = read
    draft[reads + 2 : reads + 3, 0:rows] = read
    none = jnp.zeros((1, rows), I32)
    seen = none
    tiles, places, named = [[none + start] * (slots - 1) for start in (rows, rows, 0)]
    for s in range(slots):
        place = jnp.sum(equal[s] * rank, axis=0, keepdims=True).astype(I32)
        tile = spot[s : s + 1] - 2 * rows
        far = jnp.where(tile >= 0, 1, 0)
        for j in range(min(s + 1, slots - 1)):
            hit = (far == 1) & (seen == j)
            tiles[j] = jnp.where(hit, tile, tiles[j])
            places[j] = jnp.where(hit, place, places[j])
            named[j] = jnp.where(hit, s, named[j])
        seen = seen + far
    for j in range(slots - 1):
        draft[panel + j : panel + j + 1, 0:rows] = tiles[j]
        draft[counted + j : counted + j + 1, 0:rows] = places[j]
        draft[slot + j : slot + j + 1, 0:rows] = named[j]
    along = jnp.broadcast_to(seen.astype(F32), (rows, rows))
    down = lax.dot_general(
        jnp.where(h == lane, along, 0.0).astype(BF16), ones, NN, preferred_element_type=F32
    )
    ahead = jnp.where((down < along) | ((down == along) & (h < lane)), 1.0, 0.0)
    position = jnp.sum(ahead, axis=0, keepdims=True).astype(I32)
    taken = jnp.where(position == h, 1.0, 0.0).astype(BF16)
    line = lax.broadcasted_iota(I32, (16, rows), 1).astype(BF16)
    sorted_rows = lax.dot_general(line, taken, NT, preferred_element_type=F32)
    draft[order : order + 1, 0:rows] = sorted_rows[0:1].astype(I32)
    draft[reads : reads + 1, 0:rows] = seen
    touched = jnp.sum(jnp.minimum(seen, 1).astype(F32), axis=1, keepdims=True)
    draft[reads + 1 : reads + 2, 0:rows] = jnp.broadcast_to(touched, (1, rows)).astype(I32)


def prep_kernel(
    where, columns, tiles, turned, inverse, plan, wanted,
    landing, named, draft, arrived, here, done,
):
    rows, slots, size, _ = tiles.shape
    chunks = rows // CHUNK

    def copy_in(i):
        part = pl.ds(i * CHUNK, CHUNK)
        return pltpu.make_async_copy(tiles.at[part], landing.at[part], arrived.at[i])

    copy_columns = pltpu.make_async_copy(columns, named, here)
    copy_columns.start()
    for i in range(chunks):
        copy_in(i).start()
    copy_plan = pltpu.make_async_copy(draft, plan, done)

    def step(i, carry):
        copy_in(i).wait()
        for u in range(CHUNK):
            r = i * CHUNK + u
            total = None
            for s in range(slots):
                tile = landing[r, s].T
                turned[r, pl.ds(s * size, size), :] = tile
                tile = tile.astype(F32)
                total = tile if total is None else total + tile
            total = jnp.sum(total, axis=0, keepdims=True)
            inverse[r] = jnp.broadcast_to(1.0 / total, inverse.shape[1:])
        return carry

    lax.fori_loop(0, chunks // 2, step, 0)
    copy_columns.wait()
    draft_plan(where[0], where[1], named[...], draft, wanted)
    copy_plan.start()
    lax.fori_loop(chunks // 2, chunks, step, 0)
    copy_plan.wait()


def prep(where, columns, tiles):
    rows, slots, size, _ = tiles.shape
    height = plan_height(slots)
    return pl.pallas_call(
        prep_kernel,
        out_shape=(
            pltpu.VMEM((rows, slots * size, size), BF16),
            pltpu.VMEM((rows, 8, size), F32),
            pltpu.SMEM((height, 128), I32),
            pltpu.VMEM((8, 128), I32),
        ),
        in_specs=[SM, HB, HB],
        out_specs=(VM, VM, SM, VM),
        scratch_shapes=[
            pltpu.VMEM(tiles.shape, BF16),
            pltpu.VMEM(columns.shape, I32),
            pltpu.VMEM((height, 128), I32),
            pltpu.SemaphoreType.DMA((rows // CHUNK,)),
            pltpu.SemaphoreType.DMA,
            pltpu.SemaphoreType.DMA,
        ],
        compiler_params=params(14),
        cost_estimate=cost(2 * tiles.size * 16, 4 * tiles.size),
        name="prep",
    )(where, in_hbm(columns), in_hbm(tiles))


def fill(window, start, panel, tile_major):
    size = window.shape[2]
    if tile_major:
        window[start : start + panel.shape[0]] = panel[...]
    else:
        for t in range(panel.shape[1] // size):
            window[start + t] = panel[:, t * size : (t + 1) * size]


def thirds(x):
    high = x.astype(BF16)
    rest = x - high.astype(F32)
    middle = rest.astype(BF16)
    low = (rest - middle.astype(F32)).astype(BF16)
    return high, middle, low


def fold(squares, vectors):
    total = None
    for a, b in ((1, 1), (0, 1), (1, 0), (0, 0)):
        part = squares[a * vectors : (a + 1) * vectors, b * vectors : (b + 1) * vectors]
        total = part if total is None else total + part
    return total


def scaled(y, factor):
    return (y.reshape(-1, *factor.shape) * factor[None]).reshape(y.shape)


def store(image, squares, picked, results, mine):
    if squares is None:
        for r, y in zip(picked, results):
            image[r] = y.astype(BF16)
        return None
    counted = []
    for r, y, keep in zip(picked, results, mine):
        stacked = jnp.concatenate(thirds(y)[:2], axis=0)
        image[r] = stacked
        counted.append(jnp.where(keep, stacked, jnp.zeros_like(stacked)))
    wide = jnp.concatenate(counted, axis=1)
    return squares + lax.dot_general(wide, wide, NT, preferred_element_type=F32)


def near_kernel(tile_major, last, count, plan, turned, inverse, own, *refs):
    mate, (image, sums, *refs) = refs[:count], refs[count:]
    rows, depth, size = turned.shape
    slots = depth // size
    reads = lines(slots)[-1]
    window = refs[-1]
    fill(window, 0, own, tile_major)
    start = rows
    for panel in mate:
        fill(window, start, panel, tile_major)
        start += panel.shape[0] if tile_major else panel.shape[1] // size
    window[2 * rows] = jnp.zeros(window.shape[1:], BF16)

    def step(block, squares):
        picked = [block * BLOCK + u for u in range(BLOCK)]
        vectors = [
            jnp.concatenate([window[plan[s, r]] for s in range(slots)], axis=1)
            for r in picked
        ]
        products = [
            lax.dot_general(x, turned[r], NN, preferred_element_type=F32)
            for x, r in zip(vectors, picked)
        ]
        results = [scaled(y, inverse[r]) for r, y in zip(picked, products)]
        for r, y in zip(picked, results):
            sums[r] = y
        mine = [plan[reads, r] == 0 for r in picked]
        return store(image, squares, picked, results, mine)

    begin = jnp.zeros(refs[0].shape, F32) if last else None
    total = lax.fori_loop(0, rows // BLOCK, step, begin)
    if last:
        refs[0][...] = total


def far_part(base, plan, turned, inverse, sums, panel, image, squares):
    rows, depth, size = turned.shape
    slots = depth // size
    slot, order, reads = lines(slots)[2:]
    panel[rows] = jnp.zeros(panel.shape[1:], BF16)

    def rows_of(start, count):
        picked = [plan[order, start + u] for u in range(BLOCK)]
        products = []
        for r in picked:
            x = [panel[plan[base + j, r]] for j in range(count)]
            w = [
                turned[r, pl.ds(pl.multiple_of(plan[slot + j, r] * size, size), size), :]
                for j in range(count)
            ]
            products.append(
                lax.dot_general(
                    jnp.concatenate(x, axis=1),
                    jnp.concatenate(w, axis=0),
                    NN,
                    preferred_element_type=F32,
                )
            )
        return picked, [
            sums[r] + scaled(y, inverse[r]) for r, y in zip(picked, products)
        ]

    def step(block, carry):
        start = rows - (block + 1) * BLOCK
        most = plan[reads, plan[order, start + BLOCK - 1]]
        for count in range(1, slots):

            @pl.when(most == count)
            def _():
                picked, results = rows_of(start, count)
                mine = [plan[reads, r] > 0 for r in picked]
                if squares is None:
                    store(image, None, picked, results, mine)
                else:
                    squares[...] = store(image, squares[...], picked, results, mine)

        return carry

    touched = plan[reads + 1, 0]
    lax.fori_loop(0, (touched + BLOCK - 1) // BLOCK, step, 0)


def pack(image, sending, send):
    for k in range(send.shape[0]):
        send[k] = image[sending[0, k]]


def halve(image, halves):
    half = halves[0].shape[0]
    for i, part in enumerate(halves):
        part[...] = image[i * half : (i + 1) * half]


def far_first_kernel(
    asked, plan, turned, inverse, other, sums, i_in, image, left, right, send, sending, panel, done
):
    rows, depth, size = turned.shape
    copy = pltpu.make_async_copy(asked, sending, done)
    copy.start()
    fill(panel, 0, other, False)
    base = lines(depth // size)[0]
    far_part(base, plan, turned, inverse, sums, panel, image, None)
    copy.wait()
    pack(image, sending, send)
    halve(image, (left, right))


def far_kernel(sending, plan, turned, inverse, other, sums, i_in, image, left, right, send, panel):
    rows, depth, size = turned.shape
    fill(panel, 0, other, True)
    base = lines(depth // size)[1]
    far_part(base, plan, turned, inverse, sums, panel, image, None)
    pack(image, sending, send)
    halve(image, (left, right))


def far_whole_kernel(
    tile_major, plan, turned, inverse, other, sums, i_in, image, left, right, panel
):
    rows, depth, size = turned.shape
    fill(panel, 0, other, tile_major)
    base = lines(depth // size)[0]
    far_part(base, plan, turned, inverse, sums, panel, image, None)
    halve(image, (left, right))


def far_last_kernel(
    whole, sending, plan, turned, inverse, other, near, sums, i_in, image, gram, panel, squares
):
    rows, depth, size = turned.shape
    slots = depth // size
    vectors = gram.shape[1]
    fill(panel, 0, other, True)
    squares[...] = near[...]
    base = lines(slots)[0 if whole else 1]
    far_part(base, plan, turned, inverse, sums, panel, image, squares)
    gram[0:vectors] = fold(squares[...], vectors)
    read = plan[lines(slots)[-1] + 2, 0]
    short = jnp.maximum(read, sending[1, 0]) > other.shape[0]
    gram[vectors:] = jnp.zeros((8, vectors), F32) + jnp.where(short, 1.0, 0.0)


def near_rows(plan, turned, inverse, own, mate, tile_major, last):
    rows, depth, size = turned.shape
    vectors = own.shape[1 if tile_major else 0]
    height = 2 * vectors if last else vectors
    shapes = (
        pltpu.VMEM((rows, height, size), BF16),
        pltpu.VMEM((rows, vectors, size), F32),
    )
    if last:
        shapes += (pltpu.VMEM((height, height), F32),)
    return pl.pallas_call(
        functools.partial(near_kernel, tile_major, last, len(mate)),
        out_shape=shapes,
        in_specs=[SM, VM, VM, VM] + [VM] * len(mate),
        out_specs=(VM,) * len(shapes),
        scratch_shapes=[pltpu.VMEM((2 * rows + 1, vectors, size), BF16)],
        compiler_params=params(4),
        cost_estimate=cost(0, 1024),
        name="near_rows",
    )(plan, *map(in_vmem, (turned, inverse, own, *mate)))


def far_call(kernel, ins, in_specs, outs, out_specs, turned, vectors, scratch=()):
    rows, depth, size = turned.shape
    return pl.pallas_call(
        kernel,
        out_shape=outs,
        in_specs=in_specs,
        out_specs=out_specs,
        scratch_shapes=[pltpu.VMEM((rows + 1, vectors, size), BF16), *scratch],
        input_output_aliases={len(ins) - 1: 0},
        compiler_params=params(4),
        cost_estimate=cost(20 * rows * depth * size, rows * depth * size),
        name="far_rows",
    )(*ins)


def of(array):
    return pltpu.VMEM(array.shape, array.dtype)


def halves_of(image):
    rows, vectors, size = image.shape
    return (pltpu.VMEM((rows // 2, vectors, size), BF16),) * 2


def far_rows_first(limit, asked, plan, turned, inverse, other, sums, image):
    rows, vectors, size = image.shape
    return far_call(
        far_first_kernel,
        (in_vmem(asked), plan, *map(in_vmem, (turned, inverse, other, sums, image))),
        [VM, SM] + [VM] * 5,
        (
            of(image),
            *halves_of(image),
            pltpu.VMEM((limit, vectors, size), BF16),
            pltpu.SMEM((8, 128), I32),
        ),
        (VM, VM, VM, VM, SM),
        turned,
        vectors,
        [pltpu.SemaphoreType.DMA],
    )


def far_rows(plan, turned, inverse, sending, other, sums, image):
    return far_call(
        far_kernel,
        (sending, plan, *map(in_vmem, (turned, inverse, other, sums, image))),
        [SM, SM] + [VM] * 5,
        (of(image), *halves_of(image), of(other)),
        (VM,) * 4,
        turned,
        image.shape[1],
    )


def far_rows_whole(plan, turned, inverse, other, sums, image, tile_major):
    return far_call(
        functools.partial(far_whole_kernel, tile_major),
        (plan, *map(in_vmem, (turned, inverse, other, sums, image))),
        [SM] + [VM] * 5,
        (of(image), *halves_of(image)),
        (VM,) * 3,
        turned,
        image.shape[1],
    )


def far_rows_last(whole, plan, turned, inverse, sending, other, near, sums, image):
    vectors = near.shape[0] // 2
    return far_call(
        functools.partial(far_last_kernel, whole),
        (sending, plan, *map(in_vmem, (turned, inverse, other, near, sums, image))),
        [SM, SM] + [VM] * 6,
        (of(image), pltpu.VMEM((vectors + 8, vectors), F32)),
        (VM,) * 2,
        turned,
        vectors,
        [pltpu.VMEM(near.shape, F32)],
    )


def inverse_factor(gram):
    count = gram.shape[0]
    step = 8
    row = lax.broadcasted_iota(I32, (count, count), 0)
    column = lax.broadcasted_iota(I32, (count, count), 1)
    work = jnp.concatenate([gram, jnp.where(row == column, 1.0, 0.0)], axis=1)
    below = lax.broadcasted_iota(I32, work.shape, 0)
    for begin in range(0, count, step):
        spread = [
            jnp.broadcast_to(work[:, k : k + 1], work.shape)
            for k in range(begin, begin + step)
        ]
        for j in range(step):
            k = begin + j
            factor = jnp.where(below > k, spread[j], 0.0)
            pivot = 1.0 / spread[j][k : k + 1]
            for q in range(j + 1, step):
                spread[q] = spread[q] - factor * (spread[q][k : k + 1] * pivot)
            work = work - factor * (work[k : k + 1] * pivot)
    pivots = jnp.sum(
        jnp.where(row == column, work[:, :count], 0.0), axis=1, keepdims=True
    )
    return work[:, count:] * lax.rsqrt(pivots)


def final_kernel(states, gram_a, gram_b, mapping, parts, out, short, ready, sent):
    rows, depth, size = parts.shape
    vectors = depth // 2
    total = gram_a[...] + gram_b[...]
    short[0] = jnp.max(total[vectors:]).astype(I32)
    factor = inverse_factor(total[:vectors] / states)
    combined = lax.dot_general(
        mapping[...],
        factor,
        (((0,), (0,)), ((), ())),
        precision=lax.Precision.HIGHEST,
        preferred_element_type=F32,
    )
    high, middle, low = thirds(combined)
    blank = jnp.zeros_like(high)
    left = jnp.concatenate(
        [
            jnp.concatenate([high, high], axis=1),
            jnp.concatenate([middle, middle], axis=1),
            jnp.concatenate([low, blank], axis=1),
        ],
        axis=0,
    )
    copies = []
    for g in range(rows // CHUNK):
        for r in range(g * CHUNK, (g + 1) * CHUNK):
            y = lax.dot_general(left, parts[r], NN, preferred_element_type=F32)
            ready[:, r * size : (r + 1) * size] = (
                y[2 * vectors :] + y[vectors : 2 * vectors]
            ) + y[:vectors]
        part = pl.ds(g * CHUNK * size, CHUNK * size)
        copies.append(pltpu.make_async_copy(ready.at[:, part], out.at[:, part], sent.at[g]))
        copies[-1].start()
    for copy in copies:
        copy.wait()


def final(states, gram_a, gram_b, mapping, parts):
    rows, depth, size = parts.shape
    vectors = depth // 2
    return pl.pallas_call(
        functools.partial(final_kernel, float(states)),
        out_shape=(
            jax.ShapeDtypeStruct((vectors, rows * size), F32),
            pltpu.SMEM((1,), I32),
        ),
        in_specs=[VM, VM, VM, VM],
        out_specs=(HB, SM),
        scratch_shapes=[
            pltpu.VMEM((vectors, rows * size), F32),
            pltpu.SemaphoreType.DMA((rows // CHUNK,)),
        ],
        compiler_params=params(8),
        cost_estimate=cost(6 * parts.size * vectors, 4 * parts.size),
        name="memberships",
    )(gram_a, gram_b, mapping, in_vmem(parts))


def memberships(whole, transition_tiles, column_tiles, schur_basis, membership_map):
    rows = transition_tiles.shape[0]
    count = lax.axis_size("rows")
    me = lax.axis_index("rows")
    mates = [(i, i ^ 1) for i in range(count)]
    others = []
    for i in range(1, count - 1, 2):
        others += [(i, i + 1), (i + 1, i)]

    def swap(array, pairs):
        return lax.ppermute(array, "rows", pairs)

    limit = 11 * rows // 16
    where = jnp.stack([me * rows, me % 2]).astype(I32)
    columns = column_tiles.T
    other = swap(schur_basis, others)
    mate = [swap(half, mates) for half in jnp.split(schur_basis, 2, axis=1)]
    turned, inverse, plan, wanted = prep(where, columns, transition_tiles)
    asked = swap(wanted, others)
    image, sums = near_rows(plan, turned, inverse, schur_basis, mate, False, False)
    if whole:
        image, *halves = far_rows_whole(plan, turned, inverse, other, sums, image, False)
        send, sending = image, asked
    else:
        image, *halves, send, sending = far_rows_first(
            limit, asked, plan, turned, inverse, other, sums, image
        )
    for step in range(1, PRODUCTS):
        last = step == PRODUCTS - 1
        other = swap(send, others)
        mate = [swap(half, mates) for half in halves]
        image, sums, *near = near_rows(plan, turned, inverse, image, mate, True, last)
        if last:
            parts, gram = far_rows_last(
                whole, plan, turned, inverse, sending, other, near[0], sums, image
            )
        elif whole:
            image, *halves = far_rows_whole(plan, turned, inverse, other, sums, image, True)
            send = image
        else:
            image, *halves, send = far_rows(plan, turned, inverse, sending, other, sums, image)
    distance = 1
    while distance < count:
        partner = swap(gram, [(i, i ^ distance) for i in range(count)])
        distance *= 2
        if distance < count:
            gram = gram + partner
    states = schur_basis.shape[1] * count
    return final(states, gram, partner, membership_map, parts)


def body(transition_tiles, column_tiles, schur_basis, membership_map):
    arguments = transition_tiles, column_tiles, schur_basis, membership_map
    out, short = memberships(False, *arguments)
    return lax.cond(
        short[0] > 0,
        lambda *given: memberships(True, *given[:4])[0],
        lambda *given: given[4],
        *arguments,
        out,
    )


def solution(mesh):
    return jax.shard_map(
        body,
        mesh=mesh,
        in_specs=(
            P(("groups", "rows"), None, None, None),
            P(("groups", "rows"), None),
            P(None, ("groups", "rows")),
            P("groups", None),
        ),
        out_specs=P(None, ("groups", "rows")),
        check_vma=False,
    )
```

```python
import functools

import jax
import jax.numpy as jnp
from jax import lax
from jax.experimental import pallas as pl
from jax.experimental.pallas import tpu as pltpu
from jax.sharding import PartitionSpec as P

PRODUCTS = 4
BLOCK = 16
CHUNK = 8
F32 = jnp.float32
BF16 = jnp.bfloat16
I32 = jnp.int32
NN = (((1,), (0,)), ((), ()))
NT = (((1,), (1,)), ((), ()))
VM = pl.BlockSpec(memory_space=pltpu.VMEM)
SM = pl.BlockSpec(memory_space=pltpu.SMEM)
HB = pl.BlockSpec(memory_space=pltpu.HBM)


def in_vmem(array):
    return pltpu.with_memory_space_constraint(array, pltpu.VMEM)


def in_hbm(array):
    return pltpu.with_memory_space_constraint(array, pltpu.HBM)


def cost(flops, moved):
    return pl.CostEstimate(flops=flops, bytes_accessed=moved, transcendentals=0)


def params(mib):
    return pltpu.CompilerParams(vmem_limit_bytes=mib * 2**20)


def ranks(named):
    rows = named.shape[0]
    h = lax.broadcasted_iota(I32, (rows, rows), 0)
    other = lax.broadcasted_iota(I32, (rows, rows), 1)
    before = jnp.where(other < h, 1.0, 0.0).astype(BF16)
    ones = jnp.ones((rows, rows), BF16)
    total = lax.dot_general(named.astype(BF16), ones, NN, preferred_element_type=F32)
    mark = jnp.where(total > 0.5, 1.0, 0.0)
    rank = lax.dot_general(before, mark.astype(BF16), NN, preferred_element_type=F32)
    return mark, rank


def lines(slots):
    far = slots - 1
    return slots, slots + far, slots + 2 * far, slots + 3 * far, slots + 3 * far + 1


def plan_height(slots):
    return (lines(slots)[-1] + 3 + 7) // 8 * 8


def draft_plan(first, parity, columns, draft, wanted):
    slots, rows = columns.shape
    panel, counted, slot, order, reads = lines(slots)
    low = jnp.where(parity == 0, 2 * rows, rows)
    high = jnp.where(parity == 0, rows, 2 * rows)
    offset = columns - first
    spot = jnp.where(
        offset < 0,
        offset + (rows + low),
        jnp.where(offset >= rows, offset + (high - rows), offset),
    )
    draft[0:slots, 0:rows] = jnp.minimum(spot, 2 * rows)
    h = lax.broadcasted_iota(I32, (rows, rows), 0)
    lane = lax.broadcasted_iota(I32, (rows, rows), 1)
    ones = jnp.ones((rows, rows), BF16)
    equal = [
        jnp.where(spot[s : s + 1] - 2 * rows == h, 1.0, 0.0) for s in range(slots)
    ]
    mark, rank = ranks(functools.reduce(jnp.add, equal))
    here = jnp.where((mark > 0.5) & (rank.astype(I32) == lane), h, 0)
    wanted[0:1, 0:rows] = jnp.sum(here.astype(F32), axis=0, keepdims=True).astype(I32)
    read = jnp.sum(mark, axis=0, keepdims=True).astype(I32)
    wanted[1:2, 0:rows] = read
    draft[reads + 2 : reads + 3, 0:rows] = read
    none = jnp.zeros((1, rows), I32)
    seen = none
    tiles, places, named = [[none + start] * (slots - 1) for start in (rows, rows, 0)]
    for s in range(slots):
        place = jnp.sum(equal[s] * rank, axis=0, keepdims=True).astype(I32)
        tile = spot[s : s + 1] - 2 * rows
        far = jnp.where(tile >= 0, 1, 0)
        for j in range(min(s + 1, slots - 1)):
            hit = (far == 1) & (seen == j)
            tiles[j] = jnp.where(hit, tile, tiles[j])
            places[j] = jnp.where(hit, place, places[j])
            named[j] = jnp.where(hit, s, named[j])
        seen = seen + far
    for j in range(slots - 1):
        draft[panel + j : panel + j + 1, 0:rows] = tiles[j]
        draft[counted + j : counted + j + 1, 0:rows] = places[j]
        draft[slot + j : slot + j + 1, 0:rows] = named[j]
    along = jnp.broadcast_to(seen.astype(F32), (rows, rows))
    down = lax.dot_general(
        jnp.where(h == lane, along, 0.0).astype(BF16), ones, NN, preferred_element_type=F32
    )
    ahead = jnp.where((down < along) | ((down == along) & (h < lane)), 1.0, 0.0)
    position = jnp.sum(ahead, axis=0, keepdims=True).astype(I32)
    taken = jnp.where(position == h, 1.0, 0.0).astype(BF16)
    line = lax.broadcasted_iota(I32, (16, rows), 1).astype(BF16)
    sorted_rows = lax.dot_general(line, taken, NT, preferred_element_type=F32)
    draft[order : order + 1, 0:rows] = sorted_rows[0:1].astype(I32)
    draft[reads : reads + 1, 0:rows] = seen
    touched = jnp.sum(jnp.minimum(seen, 1).astype(F32), axis=1, keepdims=True)
    draft[reads + 1 : reads + 2, 0:rows] = jnp.broadcast_to(touched, (1, rows)).astype(I32)


def prep_kernel(
    where, columns, tiles, turned, inverse, plan, wanted,
    landing, named, draft, arrived, here, done,
):
    rows, slots, size, _ = tiles.shape
    chunks = rows // CHUNK

    def copy_in(i):
        part = pl.ds(i * CHUNK, CHUNK)
        return pltpu.make_async_copy(tiles.at[part], landing.at[part], arrived.at[i])

    copy_columns = pltpu.make_async_copy(columns, named, here)
    copy_columns.start()
    for i in range(chunks):
        copy_in(i).start()
    copy_plan = pltpu.make_async_copy(draft, plan, done)

    def step(i, carry):
        copy_in(i).wait()
        for u in range(CHUNK):
            r = i * CHUNK + u
            total = None
            for s in range(slots):
                tile = landing[r, s].T
                turned[r, pl.ds(s * size, size), :] = tile
                tile = tile.astype(F32)
                total = tile if total is None else total + tile
            total = jnp.sum(total, axis=0, keepdims=True)
            inverse[r] = jnp.broadcast_to(1.0 / total, inverse.shape[1:])
        return carry

    lax.fori_loop(0, chunks // 2, step, 0)
    copy_columns.wait()
    step(chunks // 2, 0)
    draft_plan(where[0], where[1], named[...], draft, wanted)
    copy_plan.start()
    lax.fori_loop(chunks // 2 + 1, chunks, step, 0)
    copy_plan.wait()


def prep(where, columns, tiles):
    rows, slots, size, _ = tiles.shape
    height = plan_height(slots)
    return pl.pallas_call(
        prep_kernel,
        out_shape=(
            pltpu.VMEM((rows, slots * size, size), BF16),
            pltpu.VMEM((rows, 8, size), F32),
            pltpu.SMEM((height, 128), I32),
            pltpu.VMEM((8, 128), I32),
        ),
        in_specs=[SM, HB, HB],
        out_specs=(VM, VM, SM, VM),
        scratch_shapes=[
            pltpu.VMEM(tiles.shape, BF16),
            pltpu.VMEM(columns.shape, I32),
            pltpu.VMEM((height, 128), I32),
            pltpu.SemaphoreType.DMA((rows // CHUNK,)),
            pltpu.SemaphoreType.DMA,
            pltpu.SemaphoreType.DMA,
        ],
        compiler_params=params(14),
        cost_estimate=cost(2 * tiles.size * 16, 4 * tiles.size),
        name="prep",
    )(where, in_hbm(columns), in_hbm(tiles))


def fill(window, start, panel, tile_major):
    size = window.shape[2]
    if tile_major:
        window[start : start + panel.shape[0]] = panel[...]
    else:
        for t in range(panel.shape[1] // size):
            window[start + t] = panel[:, t * size : (t + 1) * size]


def thirds(x):
    high = x.astype(BF16)
    rest = x - high.astype(F32)
    middle = rest.astype(BF16)
    low = (rest - middle.astype(F32)).astype(BF16)
    return high, middle, low


def fold(squares, vectors):
    total = None
    for a, b in ((1, 1), (0, 1), (1, 0), (0, 0)):
        part = squares[a * vectors : (a + 1) * vectors, b * vectors : (b + 1) * vectors]
        total = part if total is None else total + part
    return total


def scaled(y, factor):
    return (y.reshape(-1, *factor.shape) * factor[None]).reshape(y.shape)


def store(image, squares, picked, results, mine):
    if squares is None:
        for r, y in zip(picked, results):
            image[r] = y.astype(BF16)
        return None
    counted = []
    for r, y, keep in zip(picked, results, mine):
        stacked = jnp.concatenate(thirds(y)[:2], axis=0)
        image[r] = stacked
        counted.append(jnp.where(keep, stacked, jnp.zeros_like(stacked)))
    wide = jnp.concatenate(counted, axis=1)
    return squares + lax.dot_general(wide, wide, NT, preferred_element_type=F32)


def near_kernel(tile_major, last, count, plan, turned, inverse, own, *refs):
    mate, (image, sums, *refs) = refs[:count], refs[count:]
    rows, depth, size = turned.shape
    slots = depth // size
    reads = lines(slots)[-1]
    window = refs[-1]
    fill(window, 0, own, tile_major)
    start = rows
    for panel in mate:
        fill(window, start, panel, tile_major)
        start += panel.shape[0]
    window[2 * rows] = jnp.zeros(window.shape[1:], BF16)

    def step(block, squares):
        picked = [block * BLOCK + u for u in range(BLOCK)]
        vectors = [
            jnp.concatenate([window[plan[s, r]] for s in range(slots)], axis=1)
            for r in picked
        ]
        products = [
            lax.dot_general(x, turned[r], NN, preferred_element_type=F32)
            for x, r in zip(vectors, picked)
        ]
        results = [scaled(y, inverse[r]) for r, y in zip(picked, products)]
        for r, y in zip(picked, results):
            sums[r] = y
        mine = [plan[reads, r] == 0 for r in picked]
        return store(image, squares, picked, results, mine)

    begin = jnp.zeros(refs[0].shape, F32) if last else None
    total = lax.fori_loop(0, rows // BLOCK, step, begin)
    if last:
        refs[0][...] = total


def far_part(base, plan, turned, inverse, sums, panel, image, squares):
    rows, depth, size = turned.shape
    slots = depth // size
    slot, order, reads = lines(slots)[2:]
    panel[rows] = jnp.zeros(panel.shape[1:], BF16)

    def rows_of(start, count):
        picked = [plan[order, start + u] for u in range(BLOCK)]
        products = []
        for r in picked:
            x = [panel[plan[base + j, r]] for j in range(count)]
            w = [
                turned[r, pl.ds(pl.multiple_of(plan[slot + j, r] * size, size), size), :]
                for j in range(count)
            ]
            products.append(
                lax.dot_general(
                    jnp.concatenate(x, axis=1),
                    jnp.concatenate(w, axis=0),
                    NN,
                    preferred_element_type=F32,
                )
            )
        return picked, [
            sums[r] + scaled(y, inverse[r]) for r, y in zip(picked, products)
        ]

    def step(block, carry):
        start = rows - (block + 1) * BLOCK
        most = plan[reads, plan[order, start + BLOCK - 1]]
        for count in range(1, slots):

            @pl.when(most == count)
            def _():
                picked, results = rows_of(start, count)
                mine = [plan[reads, r] > 0 for r in picked]
                if squares is None:
                    store(image, None, picked, results, mine)
                else:
                    squares[...] = store(image, squares[...], picked, results, mine)

        return carry

    touched = plan[reads + 1, 0]
    lax.fori_loop(0, (touched + BLOCK - 1) // BLOCK, step, 0)


def pack(image, sending, send):
    for k in range(send.shape[0]):
        send[k] = image[sending[0, k]]


def halve(image, halves):
    half = halves[0].shape[0]
    for i, part in enumerate(halves):
        part[...] = image[i * half : (i + 1) * half]


def far_first_kernel(
    asked, plan, turned, inverse, other, sums, i_in, image, left, right, send, sending, panel, done
):
    rows, depth, size = turned.shape
    copy = pltpu.make_async_copy(asked, sending, done)
    copy.start()
    fill(panel, 0, other, False)
    base = lines(depth // size)[0]
    far_part(base, plan, turned, inverse, sums, panel, image, None)
    copy.wait()
    pack(image, sending, send)
    halve(image, (left, right))


def far_kernel(sending, plan, turned, inverse, other, sums, i_in, image, left, right, send, panel):
    rows, depth, size = turned.shape
    fill(panel, 0, other, True)
    base = lines(depth // size)[1]
    far_part(base, plan, turned, inverse, sums, panel, image, None)
    pack(image, sending, send)
    halve(image, (left, right))


def far_whole_kernel(
    tile_major, plan, turned, inverse, other, sums, i_in, image, left, right, panel
):
    rows, depth, size = turned.shape
    fill(panel, 0, other, tile_major)
    base = lines(depth // size)[0]
    far_part(base, plan, turned, inverse, sums, panel, image, None)
    halve(image, (left, right))


def far_last_kernel(
    whole, sending, plan, turned, inverse, other, near, sums, i_in, image, gram, panel, squares
):
    rows, depth, size = turned.shape
    slots = depth // size
    vectors = gram.shape[1]
    fill(panel, 0, other, True)
    squares[...] = near[...]
    base = lines(slots)[0 if whole else 1]
    far_part(base, plan, turned, inverse, sums, panel, image, squares)
    gram[0:vectors] = fold(squares[...], vectors)
    read = plan[lines(slots)[-1] + 2, 0]
    short = jnp.maximum(read, sending[1, 0]) > other.shape[0]
    gram[vectors:] = jnp.zeros((8, vectors), F32) + jnp.where(short, 1.0, 0.0)


def near_rows(plan, turned, inverse, own, mate, tile_major, last):
    rows, depth, size = turned.shape
    vectors = own.shape[1 if tile_major else 0]
    height = 2 * vectors if last else vectors
    shapes = (
        pltpu.VMEM((rows, height, size), BF16),
        pltpu.VMEM((rows, vectors, size), F32),
    )
    if last:
        shapes += (pltpu.VMEM((height, height), F32),)
    return pl.pallas_call(
        functools.partial(near_kernel, tile_major, last, len(mate)),
        out_shape=shapes,
        in_specs=[SM, VM, VM, VM] + [VM] * len(mate),
        out_specs=(VM,) * len(shapes),
        scratch_shapes=[pltpu.VMEM((2 * rows + 1, vectors, size), BF16)],
        compiler_params=params(4),
        cost_estimate=cost(0, 1024),
        name="near_rows",
    )(plan, *map(in_vmem, (turned, inverse, own, *mate)))


def far_call(kernel, ins, in_specs, outs, out_specs, turned, vectors, scratch=()):
    rows, depth, size = turned.shape
    return pl.pallas_call(
        kernel,
        out_shape=outs,
        in_specs=in_specs,
        out_specs=out_specs,
        scratch_shapes=[pltpu.VMEM((rows + 1, vectors, size), BF16), *scratch],
        input_output_aliases={len(ins) - 1: 0},
        compiler_params=params(4),
        cost_estimate=cost(20 * rows * depth * size, rows * depth * size),
        name="far_rows",
    )(*ins)


def of(array):
    return pltpu.VMEM(array.shape, array.dtype)


def halves_of(image):
    rows, vectors, size = image.shape
    return (pltpu.VMEM((rows // 2, vectors, size), BF16),) * 2


def far_rows_first(limit, asked, plan, turned, inverse, other, sums, image):
    rows, vectors, size = image.shape
    return far_call(
        far_first_kernel,
        (in_vmem(asked), plan, *map(in_vmem, (turned, inverse, other, sums, image))),
        [VM, SM] + [VM] * 5,
        (
            of(image),
            *halves_of(image),
            pltpu.VMEM((limit, vectors, size), BF16),
            pltpu.SMEM((8, 128), I32),
        ),
        (VM, VM, VM, VM, SM),
        turned,
        vectors,
        [pltpu.SemaphoreType.DMA],
    )


def far_rows(plan, turned, inverse, sending, other, sums, image):
    return far_call(
        far_kernel,
        (sending, plan, *map(in_vmem, (turned, inverse, other, sums, image))),
        [SM, SM] + [VM] * 5,
        (of(image), *halves_of(image), of(other)),
        (VM,) * 4,
        turned,
        image.shape[1],
    )


def far_rows_whole(plan, turned, inverse, other, sums, image, tile_major):
    return far_call(
        functools.partial(far_whole_kernel, tile_major),
        (plan, *map(in_vmem, (turned, inverse, other, sums, image))),
        [SM] + [VM] * 5,
        (of(image), *halves_of(image)),
        (VM,) * 3,
        turned,
        image.shape[1],
    )


def far_rows_last(whole, plan, turned, inverse, sending, other, near, sums, image):
    vectors = near.shape[0] // 2
    return far_call(
        functools.partial(far_last_kernel, whole),
        (sending, plan, *map(in_vmem, (turned, inverse, other, near, sums, image))),
        [SM, SM] + [VM] * 6,
        (of(image), pltpu.VMEM((vectors + 8, vectors), F32)),
        (VM,) * 2,
        turned,
        vectors,
        [pltpu.VMEM(near.shape, F32)],
    )


def inverse_factor(gram):
    count = gram.shape[0]
    step = 8
    row = lax.broadcasted_iota(I32, (count, count), 0)
    column = lax.broadcasted_iota(I32, (count, count), 1)
    work = jnp.concatenate([gram, jnp.where(row == column, 1.0, 0.0)], axis=1)
    below = lax.broadcasted_iota(I32, work.shape, 0)
    for begin in range(0, count, step):
        spread = [
            jnp.broadcast_to(work[:, k : k + 1], work.shape)
            for k in range(begin, begin + step)
        ]
        for j in range(step):
            k = begin + j
            factor = jnp.where(below > k, spread[j], 0.0)
            pivot = 1.0 / spread[j][k : k + 1]
            for q in range(j + 1, step):
                spread[q] = spread[q] - factor * (spread[q][k : k + 1] * pivot)
            work = work - factor * (work[k : k + 1] * pivot)
    pivots = jnp.sum(
        jnp.where(row == column, work[:, :count], 0.0), axis=1, keepdims=True
    )
    return work[:, count:] * lax.rsqrt(pivots)


def final_kernel(states, gram_a, gram_b, mapping, parts, out, short, ready, sent):
    rows, depth, size = parts.shape
    vectors = depth // 2
    total = gram_a[...] + gram_b[...]
    short[0] = jnp.max(total[vectors:]).astype(I32)
    factor = inverse_factor(total[:vectors] / states)
    combined = lax.dot_general(
        mapping[...],
        factor,
        (((0,), (0,)), ((), ())),
        precision=lax.Precision.HIGHEST,
        preferred_element_type=F32,
    )
    high, middle, low = thirds(combined)
    blank = jnp.zeros_like(high)
    left = jnp.concatenate(
        [
            jnp.concatenate([high, high], axis=1),
            jnp.concatenate([middle, middle], axis=1),
            jnp.concatenate([low, blank], axis=1),
        ],
        axis=0,
    )
    copies = []
    for g in range(rows // CHUNK):
        for r in range(g * CHUNK, (g + 1) * CHUNK):
            y = lax.dot_general(left, parts[r], NN, preferred_element_type=F32)
            ready[:, r * size : (r + 1) * size] = (
                y[2 * vectors :] + y[vectors : 2 * vectors]
            ) + y[:vectors]
        part = pl.ds(g * CHUNK * size, CHUNK * size)
        copies.append(pltpu.make_async_copy(ready.at[:, part], out.at[:, part], sent.at[g]))
        copies[-1].start()
    for copy in copies:
        copy.wait()


def final(states, gram_a, gram_b, mapping, parts):
    rows, depth, size = parts.shape
    vectors = depth // 2
    return pl.pallas_call(
        functools.partial(final_kernel, float(states)),
        out_shape=(
            jax.ShapeDtypeStruct((vectors, rows * size), F32),
            pltpu.SMEM((1,), I32),
        ),
        in_specs=[VM, VM, VM, VM],
        out_specs=(HB, SM),
        scratch_shapes=[
            pltpu.VMEM((vectors, rows * size), F32),
            pltpu.SemaphoreType.DMA((rows // CHUNK,)),
        ],
        compiler_params=params(8),
        cost_estimate=cost(6 * parts.size * vectors, 4 * parts.size),
        name="memberships",
    )(gram_a, gram_b, mapping, in_vmem(parts))


def memberships(whole, transition_tiles, column_tiles, schur_basis, membership_map):
    rows = transition_tiles.shape[0]
    count = lax.axis_size("rows")
    me = lax.axis_index("rows")
    mates = [(i, i ^ 1) for i in range(count)]
    others = []
    for i in range(1, count - 1, 2):
        others += [(i, i + 1), (i + 1, i)]

    def swap(array, pairs):
        return lax.ppermute(array, "rows", pairs)

    limit = 11 * rows // 16
    where = jnp.stack([me * rows, me % 2]).astype(I32)
    columns = column_tiles.T
    mate, other = swap(schur_basis, mates), swap(schur_basis, others)
    turned, inverse, plan, wanted = prep(where, columns, transition_tiles)
    asked = swap(wanted, others)
    image, sums = near_rows(plan, turned, inverse, schur_basis, (mate,), False, False)
    if whole:
        image, *halves = far_rows_whole(plan, turned, inverse, other, sums, image, False)
        send, sending = image, asked
    else:
        image, *halves, send, sending = far_rows_first(
            limit, asked, plan, turned, inverse, other, sums, image
        )
    for step in range(1, PRODUCTS):
        last = step == PRODUCTS - 1
        other = swap(send, others)
        mate = [swap(half, mates) for half in halves]
        image, sums, *near = near_rows(plan, turned, inverse, image, mate, True, last)
        if last:
            parts, gram = far_rows_last(
                whole, plan, turned, inverse, sending, other, near[0], sums, image
            )
        elif whole:
            image, *halves = far_rows_whole(plan, turned, inverse, other, sums, image, True)
            send = image
        else:
            image, *halves, send = far_rows(plan, turned, inverse, sending, other, sums, image)
    distance = 1
    while distance < count:
        partner = swap(gram, [(i, i ^ distance) for i in range(count)])
        distance *= 2
        if distance < count:
            gram = gram + partner
    states = schur_basis.shape[1] * count
    return final(states, gram, partner, membership_map, parts)


def body(transition_tiles, column_tiles, schur_basis, membership_map):
    arguments = transition_tiles, column_tiles, schur_basis, membership_map
    out, short = memberships(False, *arguments)
    return lax.cond(
        short[0] > 0,
        lambda *given: memberships(True, *given[:4])[0],
        lambda *given: given[4],
        *arguments,
        out,
    )


def solution(mesh):
    return jax.shard_map(
        body,
        mesh=mesh,
        in_specs=(
            P(("groups", "rows"), None, None, None),
            P(("groups", "rows"), None),
            P(None, ("groups", "rows")),
            P("groups", None),
        ),
        out_specs=P(None, ("groups", "rows")),
        check_vma=False,
    )
```
